32 devices in a mesh: rep: 8 (over z, x), shard: 4 (over y, core).
Axes of the slice: x: 2, y: 2, z: 4, core: 2. Of those that a mesh axis runs over, the one named last changes fastest.
Arguments:
- hidden_in: bfloat16 [32768, 768], P(('rep', 'shard')), may hold values from -6 to 6
- enc_states: bfloat16 [32768, 768], P(('rep', 'shard')), may hold values from -6 to 6
- dec_segments: int32 [32768], P(('rep', 'shard')), may hold values from 0 to 1, as said below
- enc_segments: int32 [32768], P(('rep', 'shard')), may hold values from 0 to 1, as said below
- out_grad: bfloat16 [32768, 768], P(('rep', 'shard')), may hold values from -6 to 6
- gains: bfloat16 [3, 768], P(None, 'shard'), may hold values from 0.5 to 1.5
- rel_table: bfloat16 [32, 12], P('shard'), may hold values from -4 to 4
- self_qkv: bfloat16 [768, 2304], P('shard'), may hold values from -0.109375 to 0.109375
- self_out: bfloat16 [768, 768], P('shard'), may hold values from -2.5 to 2.5
- cross_q: bfloat16 [768, 768], P('shard'), may hold values from -0.109375 to 0.109375
- cross_kv: bfloat16 [768, 1536], P('shard'), may hold values from -0.109375 to 0.109375
- cross_out: bfloat16 [768, 768], P('shard'), may hold values from -2.5 to 2.5
- ff_in: bfloat16 [768, 4096], P('shard'), may hold values from -0.21875 to 0.21875
- ff_out: bfloat16 [2048, 768], P('shard'), may hold values from -0.1875 to 0.1875
Outputs:
- layer_out: bfloat16 [32768, 768], P(('rep', 'shard'))
- in_grad: float32 [32768, 768], P(('rep', 'shard'))
- enc_grad: float32 [32768, 768], P(('rep', 'shard'))
- gains_grad: float32 [3, 768], P(None, 'shard')
- rel_table_grad: float32 [32, 12], P('shard')
- self_qkv_grad: float32 [768, 2304], P('shard')
- self_out_grad: float32 [768, 768], P('shard')
- cross_query_gradient: float32 [768, 768], P('shard')
- cross_kv_grad: float32 [768, 1536], P('shard')
- cross_out_grad: float32 [768, 768], P('shard')
- ff_in_grad: float32 [768, 4096], P('shard')
- ff_out_grad: float32 [2048, 768], P('shard')
The draws below stay inside these ranges and needn't reach their ends.
Inputs may be any that keep to these rules, and one draw needn't show every extreme that they name: `dec_segments`: in every decoder sequence of 512 tokens the positions before a cut, drawn for each sequence from 128 to 384, have number 0 and the rest number 1. `enc_segments`: in every encoder sequence of 512 states the positions before a cut, drawn for each sequence from 128 to 384, have number 0 and the rest number 1.
All inputs are finite; a program needn't handle non-finite values.
Results may differ from the reference program's by a relative error of at most 0.025.
The reference program's roundings to bfloat16 on the way count: a program that leaves them out, or rounds other values in their place, can miss the bound.
Values may be sent and summed in bfloat16 or wider, within the bound.
No kernel may reach another device: no remote copies, remote signals or barrier semaphores. Data moves between devices by JAX's collectives and lax.ppermute only.
A program may use at most 320 MiB of HBM per device.

```python
import math
import jax
import jax.numpy as jnp
import numpy as np
from jax import lax

D = 768
HEADS = 12
HEAD_DIM = 64
FF = 2048
NUM_BUCKETS = 32
SEQ = 512
ENC_SEQ = 512
INNER = 768
TOKENS = 32768
ENC_TOKENS = 32768


def segment_ids(key, seq_count, length):
    cut_points = jax.random.randint(key, (seq_count, 1), length // 4, 3 * length // 4 + 1)
    places = jnp.arange(length, dtype=jnp.int32)[None, :]
    return (places >= cut_points).astype(jnp.int32).reshape(-1)


def draw_dec_segments(key, part):
    key = jax.random.fold_in(key, 11)
    return segment_ids(key, TOKENS // SEQ, SEQ)


def draw_enc_segments(key, part):
    key = jax.random.fold_in(key, 23)
    return segment_ids(key, ENC_TOKENS // ENC_SEQ, ENC_SEQ)


def steps_of(own_key, extent, shards, smallest, high):
    factor_of = 1.0
    for position, shards_of in shards:
        heights = jax.random.uniform(jax.random.fold_in(jax.random.fold_in(own_key, 6), position), (shards_of,), jnp.float32, smallest / len(shards), high / len(shards))
        factor_of = factor_of * jnp.repeat(jnp.exp(heights), extent[position] // shards_of).reshape((-1,) + (1,) * (len(extent) - 1 - position))
    return factor_of


def scatter_about(own_key, dims, spread, reach, shards=(), kind=jnp.bfloat16):
    values = spread * jax.random.normal(own_key, dims, jnp.float32)
    if shards:
        values = values * steps_of(own_key, dims, shards, -0.22, 0.18)
    return jnp.clip(values, -reach, reach).astype(kind)


def setup_inputs(seed: int = 0) -> dict:
    arg_keys = jax.random.split(jax.random.key(seed), 15)
    hidden_in = scatter_about(arg_keys[0], (TOKENS, D), 1.0, 6.0, ((0, 32),))
    enc_states = scatter_about(arg_keys[1], (ENC_TOKENS, D), 1.0, 6.0, ((0, 32),))
    dec_segments = draw_dec_segments(jax.random.fold_in(arg_keys[14], 71), 0)
    enc_segments = draw_enc_segments(jax.random.fold_in(arg_keys[14], 71), 0)
    out_grad = scatter_about(arg_keys[4], (TOKENS, D), 1.0, 6.0, ((0, 32),))
    gains = jnp.clip(1.0 + 0.1 * jax.random.normal(arg_keys[5], (3, D), jnp.float32), 0.5, 1.5).astype(jnp.bfloat16)
    rel_table = scatter_about(arg_keys[6], (NUM_BUCKETS, HEADS), 1.0, 4.0, ((0, 4),))
    self_qkv = scatter_about(arg_keys[7], (D, 3 * INNER), (4 * D) ** -0.5, 0.109375, ((0, 4),))
    self_out = scatter_about(arg_keys[8], (INNER, D), (max(INNER // 128, 1)) ** -0.5, 2.5, ((0, 4),))
    cross_q = scatter_about(arg_keys[9], (D, INNER), (4 * D) ** -0.5, 0.109375, ((0, 4),))
    cross_kv = scatter_about(arg_keys[10], (D, 2 * INNER), (4 * D) ** -0.5, 0.109375, ((0, 4),))
    cross_out = scatter_about(arg_keys[11], (INNER, D), (max(INNER // 128, 1)) ** -0.5, 2.5, ((0, 4),))
    ff_in = scatter_about(arg_keys[12], (D, 2 * FF), D ** -0.5, 0.21875, ((0, 4),))
    ff_out = scatter_about(arg_keys[13], (FF, D), (FF // 2) ** -0.5, 0.1875, ((0, 4),))
    return dict(hidden_in=hidden_in, enc_states=enc_states, dec_segments=dec_segments, enc_segments=enc_segments, out_grad=out_grad, gains=gains, rel_table=rel_table, self_qkv=self_qkv, self_out=self_out, cross_q=cross_q, cross_kv=cross_kv, cross_out=cross_out, ff_in=ff_in, ff_out=ff_out)


eps = 1e-06
masked_score = -1e+30
highest = lax.Precision.HIGHEST
bucket_edges = np.array(list(range(1, 16)) + [int(math.ceil(16.0 * 8.0 ** ((b - 16) / 16.0))) for b in range(16, 32)], dtype=np.int32)

@jax.custom_vjp
def low(v):
    return lax.optimization_barrier(v.astype(jnp.bfloat16)).astype(jnp.float32)

@jax.custom_vjp
def low_back(v):
    return v

def low_keep(v):
    return (low(v), None)

def low_pass(kept, grad):
    return (grad,)

def back_keep(v):
    return (v, None)

def back_low(kept, grad):
    return (low(grad),)
low.defvjp(low_keep, low_pass)
low_back.defvjp(back_keep, back_low)

def bucket_table(length):
    rows = jnp.arange(length, dtype=jnp.int32)
    distance = jnp.maximum(rows[:, None] - rows[None, :], 0)
    total = jnp.zeros((length, length), jnp.int32)
    for edge_value in bucket_edges:
        total = total + (distance >= int(edge_value)).astype(jnp.int32)
    return total

def rms_norm(values, gain):
    return values * lax.rsqrt(lax.optimization_barrier(jnp.mean(values * values, -1, keepdims=True)) + eps) * gain

def attend(queries, key_rows, value_rows, position_bias, visible):
    scores = jnp.einsum('bqhd,bkhd->bhqk', queries, key_rows, precision=highest)
    if position_bias is not None:
        scores = scores + position_bias
    scores = low_back(scores)
    scores = jnp.where(visible[:, None], scores, masked_score)
    top = lax.optimization_barrier(jnp.max(scores, -1, keepdims=True))
    expd = jnp.exp(scores - top)
    probs = expd / lax.optimization_barrier(jnp.sum(expd, -1, keepdims=True))
    return jnp.einsum('bhqk,bkhd->bqhd', low(probs), value_rows, precision=highest)

def decoder_layer(hidden, encoded, gains, rel_table, self_qkv, self_out, cross_q, cross_kv, cross_out, ff_in, ff_out, dec_ids, enc_ids, bucket):
    bundle = hidden.shape[0]
    inner_width = HEADS * HEAD_DIM
    positions = jnp.arange(SEQ, dtype=jnp.int32)
    causal = positions[:, None] >= positions[None, :]
    causal_segment_mask = causal[None] & (dec_ids[:, :, None] == dec_ids[:, None, :])
    cross_mask = dec_ids[:, :, None] == enc_ids[:, None, :]
    normed = low(rms_norm(hidden, gains[0]))
    qkv = low_back(low(jnp.dot(normed, self_qkv, precision=highest)))
    heads_q = qkv[..., :inner_width].reshape(bundle, SEQ, HEADS, HEAD_DIM)
    heads_k = qkv[..., inner_width:2 * inner_width].reshape(bundle, SEQ, HEADS, HEAD_DIM)
    heads_v = qkv[..., 2 * inner_width:].reshape(bundle, SEQ, HEADS, HEAD_DIM)
    position_bias = jnp.transpose(rel_table[bucket], (2, 0, 1))
    mixed = attend(heads_q, heads_k, heads_v, position_bias, causal_segment_mask).reshape(bundle, SEQ, inner_width)
    mixed = low_back(low(mixed))
    first = hidden + low_back(jnp.dot(mixed, self_out, precision=highest))
    normed_two = low(rms_norm(first, gains[1]))
    cross_heads = low_back(low(jnp.dot(normed_two, cross_q, precision=highest))).reshape(bundle, SEQ, HEADS, HEAD_DIM)
    enc_kv = low_back(low(jnp.dot(encoded, cross_kv, precision=highest)))
    enc_k = enc_kv[..., :inner_width].reshape(bundle, ENC_SEQ, HEADS, HEAD_DIM)
    enc_v = enc_kv[..., inner_width:].reshape(bundle, ENC_SEQ, HEADS, HEAD_DIM)
    mixed_two = attend(cross_heads, enc_k, enc_v, None, cross_mask).reshape(bundle, SEQ, inner_width)
    mixed_two = low_back(low(mixed_two))
    second = first + low_back(jnp.dot(mixed_two, cross_out, precision=highest))
    normed_three = low(rms_norm(second, gains[2]))
    pre = low_back(jnp.dot(normed_three, ff_in, precision=highest))
    gate_part = pre[..., :FF]
    up_part = pre[..., FF:]
    hidden_units = low_back(low(jax.nn.gelu(gate_part, approximate=True) * up_part))
    return second + low_back(jnp.dot(hidden_units, ff_out, precision=highest))

def reference(hidden_in, enc_states, dec_segments, enc_segments, out_grad, gains, rel_table, self_qkv, self_out, cross_q, cross_kv, cross_out, ff_in, ff_out):
    weights = tuple((w.astype(jnp.float32) for w in (gains, rel_table, self_qkv, self_out, cross_q, cross_kv, cross_out, ff_in, ff_out)))
    blocks = TOKENS // (4 * SEQ)
    hidden_blocks = hidden_in.astype(jnp.float32).reshape(blocks, 4, SEQ, D)
    enc_blocks = enc_states.astype(jnp.float32).reshape(blocks, 4, ENC_SEQ, D)
    dec_blocks = dec_segments.reshape(blocks, 4, SEQ)
    encseg_blocks = enc_segments.reshape(blocks, 4, ENC_SEQ)
    cot_blocks = out_grad.astype(jnp.float32).reshape(blocks, 4, SEQ, D)
    bucket = bucket_table(SEQ)

    def group_step(carry, items):
        block_in, block_enc, block_dec, block_encseg, block_cot = items

        def forward(hidden, encoded, *params):
            return decoder_layer(hidden, encoded, *params, block_dec, block_encseg, bucket)
        result, pullback = jax.vjp(forward, block_in, block_enc, *weights)
        grads = pullback(block_cot)
        summed = tuple((c + g for c, g in zip(carry, grads[2:])))
        return (summed, (result, grads[0], grads[1]))
    start = tuple((jnp.zeros_like(w) for w in weights))
    totals, (outputs, in_grads, enc_grads) = lax.scan(group_step, start, (hidden_blocks, enc_blocks, dec_blocks, encseg_blocks, cot_blocks))
    return (outputs.reshape(TOKENS, D).astype(jnp.bfloat16), in_grads.reshape(TOKENS, D), enc_grads.reshape(ENC_TOKENS, D), totals[0], totals[1], totals[2], totals[3], totals[4], totals[5], totals[6], totals[7], totals[8])
```

```python
from functools import partial
import math

import jax
import jax.numpy as jnp
import numpy as np
from jax import lax
from jax.experimental import pallas as pl
from jax.experimental.pallas import tpu as pltpu
from jax.sharding import PartitionSpec as P

HEADS = 12
HEAD_DIM = 64
FF = 2048
NUM_BUCKETS = 32
SEQ = 512
D = 768
INNER = HEADS * HEAD_DIM
PAIRS = HEADS // 2
LANES = 128
SPAN = SEQ + LANES
FF_BLOCK = 512
ROWS = 256

eps = 1e-06
masked_score = -1e30
bf16 = jnp.bfloat16
f32 = jnp.float32
VMEM_LIMIT = 56 * 1024 * 1024

bucket_edges = np.array(
    list(range(1, 16)) + [int(math.ceil(16.0 * 8.0 ** ((b - 16) / 16.0))) for b in range(16, 32)],
    dtype=np.int32,
)

SELF_RANGES = ((0, 128), (0, 256), (0, 384), (128, 512))
CROSS_RANGES = ((0, 384), (0, 512), (0, 512), (128, 512))


def dot_nn(a, b):
    return lax.dot_general(a, b, (((1,), (0,)), ((), ())), preferred_element_type=f32)


def dot_nt(a, b):
    return lax.dot_general(a, b, (((1,), (1,)), ((), ())), preferred_element_type=f32)


def dot_tn(a, b):
    return lax.dot_general(a, b, (((0,), (0,)), ((), ())), preferred_element_type=f32)


def half_masks():
    lane = lax.broadcasted_iota(jnp.int32, (1, LANES), 1)
    low = (lane < HEAD_DIM).astype(f32)
    return low.astype(bf16), (1.0 - low).astype(bf16)


def pieces(value):
    lane = lax.broadcasted_iota(jnp.int32, value.shape, 1) % HEAD_DIM
    high = value.astype(bf16).astype(f32)
    rest = value - high
    middle = rest.astype(bf16).astype(f32)
    last = rest - middle
    return jnp.where(
        lane == 2, high, jnp.where(lane == 3, middle, jnp.where(lane == 4, last, 0.0))
    )


def stacked(block, low, high):
    return jnp.concatenate([block * low, block * high], axis=0)


def toeplitz(row):
    wide = jnp.broadcast_to(row, (LANES, SPAN))
    return pltpu.roll(wide, 0, 1, stride=1, stride_axis=0)[:, :SEQ]


def attend_forward_kernel(ranges, biased, *refs):
    if biased:
        q_ref, k_ref, v_ref, qa_ref, ka_ref, g_ref, o_ref, l_ref, slab = refs

        @pl.when(pl.program_id(1) == 0)
        def _():
            slab[0:LANES] = toeplitz(g_ref[0, 0:1, :])
            slab[LANES : 2 * LANES] = toeplitz(g_ref[0, 1:2, :])
    else:
        q_ref, k_ref, v_ref, qa_ref, ka_ref, o_ref, l_ref = refs
    low, high = half_masks()
    keys = jnp.concatenate([k_ref[...], ka_ref[...]], axis=1)
    values = jnp.concatenate([v_ref[...], jnp.ones((SEQ, LANES), bf16)], axis=1)
    lane = lax.broadcasted_iota(jnp.int32, (LANES, LANES), 1)
    for block, (start, stop) in enumerate(ranges):
        rows = slice(block * LANES, (block + 1) * LANES)
        extra = qa_ref[rows, :]
        left = jnp.concatenate(
            [stacked(q_ref[rows, :], low, high), jnp.concatenate([extra, extra], axis=0)], axis=1
        )
        scores = dot_nt(left, keys[start:stop])
        if biased:
            scores = scores + slab[:, SEQ - (stop - start) :]
        top = jnp.max(scores, axis=1, keepdims=True)
        expd = jnp.exp(scores - top)
        mixed = dot_nn(expd.astype(bf16), values[start:stop])
        total = mixed[:, LANES:]
        mixed = mixed[:, :LANES] / total
        o_ref[rows, :] = jnp.where(lane < HEAD_DIM, mixed[:LANES], mixed[LANES:]).astype(bf16)
        negative = pieces(-(top + jnp.log(total)))
        l_ref[rows, :] = jnp.where(lane < HEAD_DIM, negative[:LANES], negative[LANES:]).astype(bf16)


def attend_forward(q, q_at, k, k_at, v, v_at, q_extra, k_extra, g, ranges):
    tokens = q.shape[0]
    sequences = tokens // SEQ
    biased = g is not None

    def block(at):
        return pl.BlockSpec((SEQ, LANES), lambda p, s: (s, at + p))

    shared = pl.BlockSpec((SEQ, LANES), lambda p, s: (s, 0))
    in_specs = [block(q_at), block(k_at), block(v_at), shared, shared]
    args = [q, k, v, q_extra, k_extra]
    scratch = []
    if biased:
        in_specs.append(pl.BlockSpec((1, 2, SPAN), lambda p, s: (p, 0, 0)))
        args.append(g)
        scratch.append(pltpu.VMEM((2 * LANES, SEQ), f32))
    seen = sum(stop - start for start, stop in ranges)
    return pl.pallas_call(
        partial(attend_forward_kernel, ranges, biased),
        grid=(PAIRS, sequences),
        in_specs=in_specs,
        out_specs=[block(0), block(0)],
        out_shape=[jax.ShapeDtypeStruct((tokens, INNER), bf16)] * 2,
        scratch_shapes=scratch,
        compiler_params=pltpu.CompilerParams(vmem_limit_bytes=VMEM_LIMIT),
        cost_estimate=pl.CostEstimate(
            flops=2 * 2 * PAIRS * sequences * seen * 256 * 256,
            bytes_accessed=tokens * INNER * 10,
            transcendentals=PAIRS * sequences * seen * 256,
        ),
    )(*args)


def attend_backward_kernel(ranges, biased, waits, *refs):
    refs = refs[waits:]
    if biased:
        (q_ref, k_ref, v_ref, qa_ref, ka_ref, l_ref, o_ref, d_ref, g_ref) = refs[:9]
        out_ref, rel_ref, dk, dv, slab, dslab = refs[9:]

        @pl.when(pl.program_id(1) == 0)
        def _():
            slab[:, 0:LANES] = toeplitz(g_ref[0, 0:1, :]).T
            slab[:, LANES : 2 * LANES] = toeplitz(g_ref[0, 1:2, :]).T
            dslab[...] = jnp.zeros_like(dslab)
    else:
        (q_ref, k_ref, v_ref, qa_ref, ka_ref, l_ref, o_ref, d_ref) = refs[:8]
        dq_ref, out_ref, dk, dv = refs[8:]
    low, high = half_masks()
    low_lane = lax.broadcasted_iota(jnp.int32, (LANES, LANES), 1) < HEAD_DIM
    low_row = lax.broadcasted_iota(jnp.int32, (LANES, LANES), 0) < HEAD_DIM
    keys = jnp.concatenate([k_ref[...], ka_ref[...]], axis=1)
    values = jnp.concatenate([v_ref[...], ka_ref[...]], axis=1)
    keys_t = k_ref[...].T
    dk[...] = jnp.zeros_like(dk)
    dv[...] = jnp.zeros_like(dv)
    for block, (start, stop) in enumerate(ranges):
        rows = slice(block * LANES, (block + 1) * LANES)
        seen = slice(start, stop)
        q2 = stacked(q_ref[rows, :], low, high)
        extra = qa_ref[rows, :]
        totals = l_ref[rows, :]
        q_right = jnp.concatenate(
            [q2, jnp.concatenate([extra + totals * low, extra + totals * high], axis=0)], axis=1
        )
        scores = dot_nt(keys[seen], q_right)
        if biased:
            scores = scores + slab[SEQ - (stop - start) :, :]
        probs = jnp.exp(scores)
        grad = d_ref[rows, :]
        d2 = stacked(grad, low, high)
        product = grad.astype(f32) * o_ref[rows, :].astype(f32)
        sum_low = jnp.sum(jnp.where(low_lane, product, 0.0), axis=1, keepdims=True)
        sum_high = jnp.sum(jnp.where(low_lane, 0.0, product), axis=1, keepdims=True)
        delta = pieces(
            -jnp.concatenate(
                [
                    jnp.broadcast_to(sum_low, (LANES, LANES)),
                    jnp.broadcast_to(sum_high, (LANES, LANES)),
                ],
                axis=0,
            )
        ).astype(bf16)
        lows = jnp.concatenate([delta[:LANES] * low, delta[LANES:] * high], axis=0)
        d_right = jnp.concatenate([d2, lows], axis=1)
        grad_scores = probs * dot_nt(values[seen], d_right)
        probs16 = probs.astype(bf16)
        scores16 = grad_scores.astype(bf16)
        dv[seen, :] += dot_nn(probs16, d2)
        dk[seen, :] += dot_nn(scores16, q2)
        dq = dot_nn(keys_t[:, seen], scores16)
        dq = jnp.where(low_row, dq[:, :LANES], dq[:, LANES:]).T.astype(bf16)
        if biased:
            out_ref[0, rows, :] = dq
            dslab[SEQ - (stop - start) :, :] += grad_scores
        else:
            dq_ref[rows, :] = dq
    first = 1 if biased else 0
    out_ref[first] = dk[...].astype(bf16)
    out_ref[first + 1] = dv[...].astype(bf16)
    if biased:

        @pl.when(pl.program_id(1) == pl.num_programs(1) - 1)
        def _():
            for head in range(2):
                square = dslab[:, head * LANES : (head + 1) * LANES].T
                wide = jnp.concatenate([square, jnp.zeros((LANES, LANES), f32)], axis=1)
                half = LANES // 2
                while half >= 1:
                    wide = wide[:half] + pltpu.roll(wide[half:], SPAN - half, 1)
                    half //= 2
                rel_ref[0, head : head + 1, :] = wide


def attend_backward(q, q_at, k, k_at, v, v_at, q_extra, k_extra, lows, mixed, grad, g, ranges, after=()):
    tokens = q.shape[0]
    sequences = tokens // SEQ
    biased = g is not None

    def block(at):
        return pl.BlockSpec((SEQ, LANES), lambda p, s: (s, at + p))

    shared = pl.BlockSpec((SEQ, LANES), lambda p, s: (s, 0))
    in_specs = [block(q_at), block(k_at), block(v_at), shared, shared, block(0), block(0), block(0)]
    args = [q, k, v, q_extra, k_extra, lows, mixed, grad]
    scratch = [pltpu.VMEM((SEQ, LANES), f32), pltpu.VMEM((SEQ, LANES), f32)]
    if biased:
        in_specs.append(pl.BlockSpec((1, 2, SPAN), lambda p, s: (p, 0, 0)))
        args.append(g)
        scratch += [pltpu.VMEM((SEQ, 2 * LANES), f32)] * 2
        out_specs = [
            pl.BlockSpec((3, SEQ, LANES), lambda p, s: (0, s, p)),
            pl.BlockSpec((1, 2, SPAN), lambda p, s: (p, 0, 0)),
        ]
        out_shape = [
            jax.ShapeDtypeStruct((3, tokens, INNER), bf16),
            jax.ShapeDtypeStruct((PAIRS, 2, SPAN), f32),
        ]
    else:
        out_specs = [block(0), pl.BlockSpec((2, SEQ, LANES), lambda p, s: (0, s, p))]
        out_shape = [
            jax.ShapeDtypeStruct((tokens, INNER), bf16),
            jax.ShapeDtypeStruct((2, tokens, INNER), bf16),
        ]
    seen = sum(stop - start for start, stop in ranges)
    return pl.pallas_call(
        partial(attend_backward_kernel, ranges, biased, len(after)),
        grid=(PAIRS, sequences),
        in_specs=[pl.BlockSpec(memory_space=pl.ANY)] * len(after) + in_specs,
        out_specs=out_specs,
        out_shape=out_shape,
        scratch_shapes=scratch,
        compiler_params=pltpu.CompilerParams(vmem_limit_bytes=VMEM_LIMIT),
        cost_estimate=pl.CostEstimate(
            flops=5 * 2 * PAIRS * sequences * seen * 256 * 256,
            bytes_accessed=tokens * INNER * 20,
            transcendentals=PAIRS * sequences * seen * 256,
        ),
    )(*after, *args)


def shares(core, value, keep_ref, send_ref, *at):
    rows, cols = value.shape
    parts = value.astype(bf16).reshape(2, 2, rows // 4, cols)
    for y in range(2):
        place = (y,) + at
        keep_ref[place] = jnp.where(core == 0, parts[y, 0], parts[y, 1])
        send_ref[place] = jnp.where(core == 0, parts[y, 1], parts[y, 0])


def feed_forward_kernel(
    core_ref, x_ref, gain_ref, dout_ref, wg_ref, wu_ref, wo_ref,
    layer_ref, gx_ref, gx16_ref, gain_grad_ref, gk_ref, gs_ref, ok_ref, os_ref,
    n3, n3t, acc, dn, hid, dgate, dup,
):
    step = pl.program_id(0)
    tokens = x_ref.shape[0]
    chunks = tokens // ROWS

    @pl.when(step == 0)
    def _():
        gain = gain_ref[...]
        for chunk in range(chunks):
            rows = slice(chunk * ROWS, (chunk + 1) * ROWS)
            x = x_ref[rows, :]
            factor = lax.rsqrt(jnp.mean(x * x, -1, keepdims=True) + eps)
            normed = (x * factor * gain).astype(bf16)
            n3[rows, :] = normed
            n3t[:, rows] = normed.T
            acc[rows, :] = jnp.zeros((ROWS, D), f32)
            dn[rows, :] = jnp.zeros((ROWS, D), f32)

    c = math.sqrt(2.0 / math.pi)
    for chunk in range(chunks):
        rows = slice(chunk * ROWS, (chunk + 1) * ROWS)
        normed = n3[rows, :]
        gate = dot_nn(normed, wg_ref[...])
        up = dot_nn(normed, wu_ref[...])
        dhidden = dot_nt(dout_ref[rows, :], wo_ref[...]).astype(bf16).astype(f32)
        square = gate * gate
        t = jnp.tanh(c * gate * (1.0 + 0.044715 * square))
        half = 0.5 * (1.0 + t)
        act = gate * half
        slope = half + (0.5 * c) * gate * (1.0 - t * t) * (1.0 + (3.0 * 0.044715) * square)
        hid[rows, :] = (act * up).astype(bf16)
        dgate[rows, :] = (dhidden * up * slope).astype(bf16)
        dup[rows, :] = (dhidden * act).astype(bf16)
        acc[rows, :] += dot_nn(hid[rows, :], wo_ref[...])
        dn[rows, :] += dot_nt(dgate[rows, :], wg_ref[...]) + dot_nt(dup[rows, :], wu_ref[...])
    core = core_ref[0]
    shares(core, dot_nn(n3t[...], dgate[...]), gk_ref, gs_ref, 0)
    shares(core, dot_nn(n3t[...], dup[...]), gk_ref, gs_ref, 1)
    out_grad = dot_tn(hid[...], dout_ref[...]).astype(bf16)

    @pl.when(step % 2 == core)
    def _():
        ok_ref[0] = out_grad

    @pl.when(step % 2 != core)
    def _():
        os_ref[0] = out_grad

    @pl.when(step == pl.num_programs(0) - 1)
    def _():
        gain = gain_ref[...]
        total = jnp.zeros((1, D), f32)
        for chunk in range(chunks):
            rows = slice(chunk * ROWS, (chunk + 1) * ROWS)
            x = x_ref[rows, :]
            layer_ref[rows, :] = (x + acc[rows, :]).astype(bf16)
            factor = lax.rsqrt(jnp.mean(x * x, -1, keepdims=True) + eps)
            d = dn[rows, :]
            weighted = d * gain
            total += jnp.sum(d * x * factor, axis=0, keepdims=True)
            back = factor * weighted - x * (
                factor * factor * factor * jnp.mean(weighted * x, -1, keepdims=True)
            )
            gx = dout_ref[rows, :].astype(f32) + back
            gx_ref[rows, :] = gx
            gx16_ref[rows, :] = gx.astype(bf16)
        gain_grad_ref[...] = total


def feed_forward(core, x, gain, dout, ff_in, ff_out):
    tokens = x.shape[0]
    steps = FF // FF_BLOCK
    whole = pl.BlockSpec((tokens, D), lambda f, c: (0, 0))
    row = pl.BlockSpec((1, D), lambda f, c: (0, 0))
    columns = pl.BlockSpec((D, FF_BLOCK), lambda f, c: (0, f))
    in_share = pl.BlockSpec((2, 2, D // 4, FF_BLOCK), lambda f, c: (0, 0, 0, f))
    out_share = pl.BlockSpec((1, FF_BLOCK, D), lambda f, c: (f // 2, 0, 0))
    in_type = jax.ShapeDtypeStruct((2, 2, D // 4, FF), bf16)
    out_type = jax.ShapeDtypeStruct((2, FF_BLOCK, D), bf16)
    return pl.pallas_call(
        feed_forward_kernel,
        grid_spec=pltpu.PrefetchScalarGridSpec(
            num_scalar_prefetch=1,
            grid=(steps,),
            in_specs=[
                whole,
                row,
                whole,
                columns,
                pl.BlockSpec((D, FF_BLOCK), lambda f, c: (0, steps + f)),
                pl.BlockSpec((FF_BLOCK, D), lambda f, c: (f, 0)),
            ],
            out_specs=[
                whole, whole, whole, row, in_share, in_share, out_share, out_share,
            ],
            scratch_shapes=[
                pltpu.VMEM((tokens, D), bf16),
                pltpu.VMEM((D, tokens), bf16),
                pltpu.VMEM((tokens, D), f32),
                pltpu.VMEM((tokens, D), f32),
                pltpu.VMEM((tokens, FF_BLOCK), bf16),
                pltpu.VMEM((tokens, FF_BLOCK), bf16),
                pltpu.VMEM((tokens, FF_BLOCK), bf16),
            ],
        ),
        out_shape=[
            jax.ShapeDtypeStruct((tokens, D), bf16),
            jax.ShapeDtypeStruct((tokens, D), f32),
            jax.ShapeDtypeStruct((tokens, D), bf16),
            jax.ShapeDtypeStruct((1, D), f32),
            in_type, in_type, out_type, out_type,
        ],
        compiler_params=pltpu.CompilerParams(vmem_limit_bytes=VMEM_LIMIT),
        cost_estimate=pl.CostEstimate(
            flops=18 * tokens * D * FF,
            bytes_accessed=tokens * D * 16 + 12 * D * FF,
            transcendentals=tokens * FF,
        ),
    )(core, x, gain, dout, ff_in, ff_in, ff_out)


def norm_back_kernel(normed, onward, waits, *refs):
    refs = refs[waits:]
    grad_ref, w_ref = refs[:2]
    total = None
    for part in range(grad_ref.shape[0]):
        term = dot_nt(grad_ref[part], w_ref[:, part * D : (part + 1) * D])
        total = term if total is None else total + term
    if not normed:
        refs[2][...] = total
        return
    x_ref, gain_ref, up_ref = refs[2:5]
    refs = refs[5:]
    if onward:
        next_ref, out_ref, gain_grad_ref, out16_ref, onward_ref = refs
    else:
        out_ref, gain_grad_ref = refs
    x = x_ref[...].astype(f32)
    factor = lax.rsqrt(jnp.mean(x * x, -1, keepdims=True) + eps)
    weighted = total * gain_ref[...]
    grad_gain = jnp.sum(total * x * factor, axis=0, keepdims=True)

    @pl.when(pl.program_id(0) == 0)
    def _():
        gain_grad_ref[...] = jnp.zeros_like(gain_grad_ref)

    gain_grad_ref[...] += grad_gain
    scale = factor * factor * factor * jnp.mean(weighted * x, -1, keepdims=True)
    out = up_ref[...] + factor * weighted - x * scale
    out_ref[...] = out
    if onward:
        out16 = out.astype(bf16)
        out16_ref[...] = out16
        onward_ref[...] = dot_nt(out16, next_ref[...]).astype(bf16)


def norm_back(grads, w, x=None, gain=None, upstream=None, w_next=None, after=()):
    if grads.ndim == 2:
        grads = grads[None]
    parts, tokens, _ = grads.shape
    block = pl.BlockSpec((ROWS, D), lambda i: (i, 0))
    row = pl.BlockSpec((1, D), lambda i: (0, 0))
    in_specs = [pl.BlockSpec(memory_space=pl.ANY)] * len(after)
    in_specs += [
        pl.BlockSpec((parts, ROWS, D), lambda i: (0, i, 0)),
        pl.BlockSpec((D, parts * D), lambda i: (0, 0)),
    ]
    args = [*after, grads, w]
    wide = jax.ShapeDtypeStruct((tokens, D), f32)
    half = jax.ShapeDtypeStruct((tokens, D), bf16)
    out_specs, out_shape = [block], [wide]
    if x is not None:
        in_specs += [block, row, block]
        args += [x, gain, upstream]
        out_specs.append(row)
        out_shape.append(jax.ShapeDtypeStruct((1, D), f32))
        if w_next is not None:
            in_specs.append(pl.BlockSpec((D, D), lambda i: (0, 0)))
            args.append(w_next)
            out_specs += [block, block]
            out_shape += [half, half]
    return pl.pallas_call(
        partial(norm_back_kernel, x is not None, w_next is not None, len(after)),
        grid=(tokens // ROWS,),
        in_specs=in_specs,
        out_specs=out_specs,
        out_shape=out_shape,
        compiler_params=pltpu.CompilerParams(vmem_limit_bytes=VMEM_LIMIT),
        cost_estimate=pl.CostEstimate(
            flops=2 * tokens * D * D * (parts + (w_next is not None)),
            bytes_accessed=tokens * D * (2 * parts + 12) + D * D * 2 * parts,
            transcendentals=0,
        ),
    )(*args)


def weight_grad_kernel(counts, waits, core_ref, *refs):
    refs = refs[waits:]
    lefts, rights = refs[0 : len(counts)], refs[len(counts) : 2 * len(counts)]
    keep_ref, send_ref, left_t = refs[2 * len(counts) :]
    step = pl.program_id(0)
    core = core_ref[0]
    at = 0
    for left, right, count in zip(lefts, rights, counts):

        @pl.when(step == at)
        def _():
            left_t[...] = left[...].T

        @pl.when((step >= at) & (step < at + count))
        def _():
            block = right[...] if len(right.shape) == 2 else right[0]
            shares(core, dot_nn(left_t[...], block), keep_ref, send_ref)

        at += count


def weight_grad(core, terms, after=()):
    tokens = terms[0][0].shape[0]
    counts = []
    rights = []
    at = 0
    for _, right in terms:
        count = right.shape[-1] * (right.shape[0] if right.ndim == 3 else 1) // ROWS
        blocks = right.shape[-1] // ROWS

        def place(j, c, at=at, count=count, blocks=blocks, deep=right.ndim == 3):
            j = jnp.clip(j - at, 0, count - 1)
            return (j // blocks, 0, j % blocks) if deep else (0, j)

        shape = (1, tokens, ROWS) if right.ndim == 3 else (tokens, ROWS)
        rights.append(pl.BlockSpec(shape, place))
        counts.append(count)
        at += count
    share = pl.BlockSpec((2, D // 4, ROWS), lambda j, c: (0, 0, j))
    out_type = jax.ShapeDtypeStruct((2, D // 4, at * ROWS), bf16)
    return pl.pallas_call(
        partial(weight_grad_kernel, counts, len(after)),
        grid_spec=pltpu.PrefetchScalarGridSpec(
            num_scalar_prefetch=1,
            grid=(at,),
            in_specs=[pl.BlockSpec(memory_space=pl.ANY)] * len(after)
            + [pl.BlockSpec((tokens, D), lambda j, c: (0, 0))] * len(terms)
            + rights,
            out_specs=[share, share],
            scratch_shapes=[pltpu.VMEM((D, tokens), bf16)],
        ),
        out_shape=[out_type, out_type],
        compiler_params=pltpu.CompilerParams(vmem_limit_bytes=VMEM_LIMIT),
        cost_estimate=pl.CostEstimate(
            flops=2 * tokens * D * ROWS * at,
            bytes_accessed=tokens * (D * len(terms) + ROWS * at) * 2 + D * ROWS * at * 2,
            transcendentals=0,
        ),
    )(core, *after, *[left for left, _ in terms], *[right for _, right in terms])


def exchange(array, axis, size, bit):
    return lax.ppermute(array, axis, [(i, i ^ bit) for i in range(size)])


def part_of(array, dim, index):
    half = array.shape[dim] // 2
    return lax.dynamic_slice_in_dim(array, index * half, half, dim)


class Chain:
    def __init__(self, keep, send, sizes, dim, order):
        self.shards, self.reps = sizes
        self.dim = dim
        self.shard = lax.axis_index("shard")
        self.rep = lax.axis_index("rep")
        self.bits = [1 << b for b in range(self.reps.bit_length() - 1)]
        steps = []
        for name in order:
            steps += [("shard", 2)] if name == "y" else [("rep", bit) for bit in self.bits]
        self.steps = steps
        self.keep = keep
        self.got = exchange(send, "shard", self.shards, 1)
        self.at = 0

    def own(self):
        return (self.keep.astype(f32) + self.got.astype(f32)).astype(bf16)

    def advance(self):
        own = self.own()
        axis, bit = self.steps[self.at]
        self.at += 1
        index = lax.axis_index(axis)
        mine = (index // bit) % 2
        dim = 0 if axis == "shard" else self.dim
        size = self.shards if axis == "shard" else self.reps
        self.keep = part_of(own, dim, mine)
        self.got = exchange(part_of(own, dim, 1 - mine), axis, size, bit)
        return self.got

    def finish(self, permutes):
        while self.at < len(self.steps):
            self.advance()
        own = self.own()
        if permutes:
            for bit in reversed(self.bits):
                got = exchange(own, "rep", self.reps, bit)
                mine = (self.rep // bit) % 2
                low = jnp.where(mine == 0, own, got)
                high = jnp.where(mine == 0, got, own)
                own = jnp.concatenate([low, high], axis=self.dim)
            return own[0].astype(f32)
        full = lax.all_gather(own[0], "rep", axis=0)
        width = len(self.bits)
        shape = own[0].shape
        dim = self.dim - 1
        full = full.reshape((2,) * width + shape)
        rest = [width + d for d in range(len(shape))]
        turned = list(reversed(range(width)))
        full = full.transpose(rest[:dim] + turned + rest[dim:])
        return full.reshape(shape[:dim] + (-1,) + shape[dim + 1 :]).astype(f32)


def bias_rows(table):
    lane = np.arange(SPAN)
    distance = np.where(lane < SEQ, SEQ - LANES - lane, 2 * SEQ - lane)
    bucket = np.zeros(SPAN, np.int64)
    for edge in bucket_edges:
        bucket += distance >= edge
    onehot = np.zeros((SPAN, NUM_BUCKETS), np.float32)
    valid = (distance >= 0) & (distance < SEQ)
    onehot[np.arange(SPAN)[valid], bucket[valid]] = 1.0
    return onehot, valid


def norm_forward(inputs, gain):
    factor = lax.rsqrt(jnp.mean(inputs * inputs, -1, keepdims=True) + eps)
    return factor, inputs * factor * gain


def local(
    sizes,
    hidden_in,
    enc_states,
    dec_segments,
    enc_segments,
    out_grad,
    gains,
    rel_table,
    self_qkv,
    self_out,
    cross_q,
    cross_kv,
    cross_out,
    ff_in,
    ff_out,
):
    shards, reps = sizes
    own_rows = D // shards
    own_buckets = NUM_BUCKETS // shards
    small = jnp.zeros((own_rows, LANES), bf16)
    small = small.at[:, 0:3].set(gains.T)
    small = small.at[0:own_buckets, 16 : 16 + HEADS].set(rel_table)
    self_set = lax.all_gather(
        jnp.concatenate([self_qkv, self_out, small], axis=1), "shard", axis=0, tiled=True
    )
    cross_set = lax.all_gather(
        jnp.concatenate([cross_kv, cross_q, cross_out], axis=1), "shard", axis=0, tiled=True
    )
    ff_in = lax.all_gather(ff_in, "shard", axis=0, tiled=True)
    ff_out = lax.all_gather(ff_out, "shard", axis=0, tiled=True)
    w_qkv = self_set[:, : 3 * INNER]
    w_self_out = self_set[:, 3 * INNER : 4 * INNER]
    w_kv = cross_set[:, : 2 * INNER]
    w_cq = cross_set[:, 2 * INNER : 3 * INNER]
    w_cross_out = cross_set[:, 3 * INNER :]
    gains = self_set[:, 4 * INNER : 4 * INNER + 3].T.astype(f32)
    table = self_set[:, 4 * INNER + 16 : 4 * INNER + 16 + HEADS]
    table = table.reshape(shards, own_rows, HEADS)[:, :own_buckets].reshape(NUM_BUCKETS, HEADS)

    lane = jnp.arange(LANES, dtype=jnp.int32)[None, :]
    dec_ids = dec_segments[:, None]
    enc_ids = enc_segments[:, None]
    ones = ((lane % HEAD_DIM >= 2) & (lane % HEAD_DIM <= 4)).astype(f32)

    def key_extra(ids):
        return jnp.where(lane < 2, jnp.where(lane != ids, masked_score, 0.0), ones).astype(bf16)

    q_extra = ((lane < 2) & (lane == dec_ids)).astype(bf16)
    self_extra = key_extra(dec_ids)
    cross_extra = key_extra(enc_ids)
    onehot, valid = bias_rows(table)
    g = jnp.einsum("ub,bh->hu", onehot.astype(bf16), table, preferred_element_type=f32)
    g = jnp.where(valid[None], g, masked_score).reshape(PAIRS, 2, SPAN)

    inputs = hidden_in.astype(f32)
    factor_one, normed_one = norm_forward(inputs, gains[0])
    normed_one = normed_one.astype(bf16)
    qkv = dot_nn(normed_one, w_qkv).astype(bf16)
    ckv = dot_nn(enc_states, w_kv).astype(bf16)
    attn_one, lows_one = attend_forward(
        qkv, 0, qkv, PAIRS, qkv, 2 * PAIRS, q_extra, self_extra, g, SELF_RANGES
    )
    first = inputs + dot_nn(attn_one, w_self_out)
    factor_two, normed_two = norm_forward(first, gains[1])
    normed_two = normed_two.astype(bf16)
    cq = dot_nn(normed_two, w_cq).astype(bf16)
    attn_two, lows_two = attend_forward(
        cq, 0, ckv, 0, ckv, PAIRS, q_extra, cross_extra, None, CROSS_RANGES
    )
    second = first + dot_nn(attn_two, w_cross_out)

    core = (lax.axis_index("shard") % 2).astype(jnp.int32).reshape(1)
    layer_out, grad_second, out_two, gain_three, in_keep, in_send, out_keep, out_send = feed_forward(
        core, second, gains[2:3], out_grad, ff_in, ff_out
    )
    ff_in_chain = Chain(in_keep, in_send, sizes, 3, "yr")
    ff_out_chain = Chain(out_keep, out_send, sizes, 1, "ry")
    grad_attn_two = dot_nt(out_two, w_cross_out).astype(bf16)
    grad_cq, grad_ckv = attend_backward(
        cq, 0, ckv, 0, ckv, PAIRS, q_extra, cross_extra, lows_two, attn_two, grad_attn_two,
        None, CROSS_RANGES, after=[ff_in_chain.got, ff_out_chain.got],
    )
    ff_in_chain.advance()
    ff_out_chain.advance()
    cross_keep, cross_send = weight_grad(
        core,
        [(enc_states, grad_ckv), (normed_two, grad_cq), (attn_two, out_two)],
        after=[ff_out_chain.got],
    )
    cross_chain = Chain(cross_keep, cross_send, sizes, 2, "yr")
    ff_out_chain.advance()
    grad_first, gain_two, out_one, grad_attn_one = norm_back(
        grad_cq, w_cq, first, gains[1:2], grad_second, w_self_out,
        after=[ff_in_chain.got, cross_keep],
    )
    ff_in_chain.advance()
    grad_qkv, rel_part = attend_backward(
        qkv, 0, qkv, PAIRS, qkv, 2 * PAIRS, q_extra, self_extra, lows_one, attn_one,
        grad_attn_one, g, SELF_RANGES, after=[cross_chain.got, ff_out_chain.got],
    )
    cross_chain.advance()
    ff_out_chain.advance()
    self_keep, self_send = weight_grad(
        core, [(normed_one, grad_qkv), (attn_one, out_one)],
        after=[ff_in_chain.got, ff_out_chain.got, cross_chain.got],
    )
    self_chain = Chain(self_keep, self_send, sizes, 2, "yr")
    ff_in_chain.advance()
    ff_out_chain.advance()
    cross_chain.advance()
    (enc_grad,) = norm_back(grad_ckv, w_kv, after=[self_keep])
    in_grad, gain_one = norm_back(
        grad_qkv, w_qkv, hidden_in, gains[0:1], grad_first, after=[self_chain.got, enc_grad]
    )
    self_chain.advance()
    ff_in_grad = ff_in_chain.finish(False)
    ff_in_grad = jnp.concatenate([ff_in_grad[0], ff_in_grad[1]], axis=1)
    ff_out_grad = ff_out_chain.finish(False)
    cross_grad = cross_chain.finish(True)
    self_grad = self_chain.finish(True)

    table_part = jnp.einsum(
        "hu,ub->bh",
        rel_part.reshape(HEADS, SPAN),
        onehot,
        precision=lax.Precision.HIGHEST,
        preferred_element_type=f32,
    )
    tiny = jnp.zeros((8, D), f32)
    tiny = tiny.at[0].set(gain_one[0]).at[1].set(gain_two[0]).at[2].set(gain_three[0])
    tiny = tiny.at[3, : NUM_BUCKETS * HEADS].set(table_part.reshape(-1))
    tiny = jnp.sum(lax.all_gather(tiny, ("rep", "shard"), axis=0), axis=0)
    shard = lax.axis_index("shard")
    gains_grad = lax.dynamic_slice_in_dim(tiny[:3], shard * own_rows, own_rows, 1)
    rel_table_grad = lax.dynamic_slice_in_dim(
        tiny[3, : NUM_BUCKETS * HEADS].reshape(NUM_BUCKETS, HEADS), shard * own_buckets, own_buckets, 0
    )
    return (
        layer_out,
        in_grad,
        enc_grad,
        gains_grad,
        rel_table_grad,
        self_grad[:, : 3 * INNER],
        self_grad[:, 3 * INNER :],
        cross_grad[:, 2 * INNER : 3 * INNER],
        cross_grad[:, : 2 * INNER],
        cross_grad[:, 3 * INNER :],
        ff_in_grad,
        ff_out_grad,
    )


def solution(mesh):
    tokens = P(("rep", "shard"), None)
    ids = P(("rep", "shard"))
    rows = P("shard", None)
    columns = P(None, "shard")
    in_specs = (tokens, tokens, ids, ids, tokens, columns) + (rows,) * 8
    out_specs = (tokens, tokens, tokens, columns) + (rows,) * 8
    sizes = (mesh.shape["shard"], mesh.shape["rep"])
    return jax.shard_map(
        partial(local, sizes), mesh=mesh, in_specs=in_specs, out_specs=out_specs, check_vma=False
    )
```

```python
from functools import partial
import math

import jax
import jax.numpy as jnp
import numpy as np
from jax import lax
from jax.experimental import pallas as pl
from jax.experimental.pallas import tpu as pltpu
from jax.sharding import PartitionSpec as P

HEADS = 12
HEAD_DIM = 64
FF = 2048
NUM_BUCKETS = 32
SEQ = 512
D = 768
INNER = HEADS * HEAD_DIM
PAIRS = HEADS // 2
LANES = 128
SPAN = SEQ + LANES
FF_BLOCK = 512
ROWS = 256

eps = 1e-06
masked_score = -1e30
bf16 = jnp.bfloat16
f32 = jnp.float32
VMEM_LIMIT = 56 * 1024 * 1024

bucket_edges = np.array(
    list(range(1, 16)) + [int(math.ceil(16.0 * 8.0 ** ((b - 16) / 16.0))) for b in range(16, 32)],
    dtype=np.int32,
)

SELF_RANGES = ((0, 128), (0, 256), (0, 384), (128, 512))
CROSS_RANGES = ((0, 384), (0, 512), (0, 512), (128, 512))


def dot_nn(a, b):
    return lax.dot_general(a, b, (((1,), (0,)), ((), ())), preferred_element_type=f32)


def dot_nt(a, b):
    return lax.dot_general(a, b, (((1,), (1,)), ((), ())), preferred_element_type=f32)


def dot_tn(a, b):
    return lax.dot_general(a, b, (((0,), (0,)), ((), ())), preferred_element_type=f32)


def half_masks():
    lane = lax.broadcasted_iota(jnp.int32, (1, LANES), 1)
    low = (lane < HEAD_DIM).astype(f32)
    return low.astype(bf16), (1.0 - low).astype(bf16)


def pieces(value):
    lane = lax.broadcasted_iota(jnp.int32, value.shape, 1) % HEAD_DIM
    high = value.astype(bf16).astype(f32)
    rest = value - high
    middle = rest.astype(bf16).astype(f32)
    last = rest - middle
    return jnp.where(
        lane == 2, high, jnp.where(lane == 3, middle, jnp.where(lane == 4, last, 0.0))
    )


def stacked(block, low, high):
    return jnp.concatenate([block * low, block * high], axis=0)


def toeplitz(row):
    wide = jnp.broadcast_to(row, (LANES, SPAN))
    return pltpu.roll(wide, 0, 1, stride=1, stride_axis=0)[:, :SEQ]


def attend_forward_kernel(ranges, biased, waits, *refs):
    refs = refs[waits:]
    if biased:
        q_ref, k_ref, v_ref, qa_ref, ka_ref, g_ref, o_ref, l_ref, slab = refs

        @pl.when(pl.program_id(1) == 0)
        def _():
            slab[0:LANES] = toeplitz(g_ref[0, 0:1, :])
            slab[LANES : 2 * LANES] = toeplitz(g_ref[0, 1:2, :])
    else:
        q_ref, k_ref, v_ref, qa_ref, ka_ref, o_ref, l_ref = refs
    low, high = half_masks()
    keys = jnp.concatenate([k_ref[...], ka_ref[...]], axis=1)
    values = jnp.concatenate([v_ref[...], jnp.ones((SEQ, LANES), bf16)], axis=1)
    lane = lax.broadcasted_iota(jnp.int32, (LANES, LANES), 1)
    for block, (start, stop) in enumerate(ranges):
        rows = slice(block * LANES, (block + 1) * LANES)
        extra = qa_ref[rows, :]
        left = jnp.concatenate(
            [stacked(q_ref[rows, :], low, high), jnp.concatenate([extra, extra], axis=0)], axis=1
        )
        scores = dot_nt(left, keys[start:stop])
        if biased:
            scores = scores + slab[:, SEQ - (stop - start) :]
        top = jnp.max(scores, axis=1, keepdims=True)
        expd = jnp.exp(scores - top)
        mixed = dot_nn(expd.astype(bf16), values[start:stop])
        total = mixed[:, LANES:]
        mixed = mixed[:, :LANES] / total
        o_ref[rows, :] = jnp.where(lane < HEAD_DIM, mixed[:LANES], mixed[LANES:]).astype(bf16)
        negative = pieces(-(top + jnp.log(total)))
        l_ref[rows, :] = jnp.where(lane < HEAD_DIM, negative[:LANES], negative[LANES:]).astype(bf16)


def attend_forward(q, q_at, k, k_at, v, v_at, q_extra, k_extra, g, ranges, after=()):
    tokens = q.shape[0]
    sequences = tokens // SEQ
    biased = g is not None

    def block(at):
        return pl.BlockSpec((SEQ, LANES), lambda p, s: (s, at + p))

    shared = pl.BlockSpec((SEQ, LANES), lambda p, s: (s, 0))
    in_specs = [block(q_at), block(k_at), block(v_at), shared, shared]
    args = [q, k, v, q_extra, k_extra]
    scratch = []
    if biased:
        in_specs.append(pl.BlockSpec((1, 2, SPAN), lambda p, s: (p, 0, 0)))
        args.append(g)
        scratch.append(pltpu.VMEM((2 * LANES, SEQ), f32))
    seen = sum(stop - start for start, stop in ranges)
    return pl.pallas_call(
        partial(attend_forward_kernel, ranges, biased, len(after)),
        grid=(PAIRS, sequences),
        in_specs=[pl.BlockSpec(memory_space=pl.ANY)] * len(after) + in_specs,
        out_specs=[block(0), block(0)],
        out_shape=[jax.ShapeDtypeStruct((tokens, INNER), bf16)] * 2,
        scratch_shapes=scratch,
        compiler_params=pltpu.CompilerParams(vmem_limit_bytes=VMEM_LIMIT),
        cost_estimate=pl.CostEstimate(
            flops=2 * 2 * PAIRS * sequences * seen * 256 * 256,
            bytes_accessed=tokens * INNER * 10,
            transcendentals=PAIRS * sequences * seen * 256,
        ),
    )(*after, *args)


def attend_backward_kernel(ranges, biased, waits, *refs):
    refs = refs[waits:]
    if biased:
        (q_ref, k_ref, v_ref, qa_ref, ka_ref, l_ref, o_ref, d_ref, g_ref) = refs[:9]
        out_ref, rel_ref, dk, dv, slab, dslab = refs[9:]

        @pl.when(pl.program_id(1) == 0)
        def _():
            slab[:, 0:LANES] = toeplitz(g_ref[0, 0:1, :]).T
            slab[:, LANES : 2 * LANES] = toeplitz(g_ref[0, 1:2, :]).T
            dslab[...] = jnp.zeros_like(dslab)
    else:
        (q_ref, k_ref, v_ref, qa_ref, ka_ref, l_ref, o_ref, d_ref) = refs[:8]
        dq_ref, out_ref, dk, dv = refs[8:]
    low, high = half_masks()
    low_lane = lax.broadcasted_iota(jnp.int32, (LANES, LANES), 1) < HEAD_DIM
    low_row = lax.broadcasted_iota(jnp.int32, (LANES, LANES), 0) < HEAD_DIM
    keys = jnp.concatenate([k_ref[...], ka_ref[...]], axis=1)
    values = jnp.concatenate([v_ref[...], ka_ref[...]], axis=1)
    keys_t = k_ref[...].T
    dk[...] = jnp.zeros_like(dk)
    dv[...] = jnp.zeros_like(dv)
    for block, (start, stop) in enumerate(ranges):
        rows = slice(block * LANES, (block + 1) * LANES)
        seen = slice(start, stop)
        q2 = stacked(q_ref[rows, :], low, high)
        extra = qa_ref[rows, :]
        totals = l_ref[rows, :]
        q_right = jnp.concatenate(
            [q2, jnp.concatenate([extra + totals * low, extra + totals * high], axis=0)], axis=1
        )
        scores = dot_nt(keys[seen], q_right)
        if biased:
            scores = scores + slab[SEQ - (stop - start) :, :]
        probs = jnp.exp(scores)
        grad = d_ref[rows, :]
        d2 = stacked(grad, low, high)
        product = grad.astype(f32) * o_ref[rows, :].astype(f32)
        sum_low = jnp.sum(jnp.where(low_lane, product, 0.0), axis=1, keepdims=True)
        sum_high = jnp.sum(jnp.where(low_lane, 0.0, product), axis=1, keepdims=True)
        delta = pieces(
            -jnp.concatenate(
                [
                    jnp.broadcast_to(sum_low, (LANES, LANES)),
                    jnp.broadcast_to(sum_high, (LANES, LANES)),
                ],
                axis=0,
            )
        ).astype(bf16)
        lows = jnp.concatenate([delta[:LANES] * low, delta[LANES:] * high], axis=0)
        d_right = jnp.concatenate([d2, lows], axis=1)
        grad_scores = probs * dot_nt(values[seen], d_right)
        probs16 = probs.astype(bf16)
        scores16 = grad_scores.astype(bf16)
        dv[seen, :] += dot_nn(probs16, d2)
        dk[seen, :] += dot_nn(scores16, q2)
        dq = dot_nn(keys_t[:, seen], scores16)
        dq = jnp.where(low_row, dq[:, :LANES], dq[:, LANES:]).T.astype(bf16)
        if biased:
            out_ref[0, rows, :] = dq
            dslab[SEQ - (stop - start) :, :] += grad_scores
        else:
            dq_ref[rows, :] = dq
    first = 1 if biased else 0
    out_ref[first] = dk[...].astype(bf16)
    out_ref[first + 1] = dv[...].astype(bf16)
    if biased:

        @pl.when(pl.program_id(1) == pl.num_programs(1) - 1)
        def _():
            for head in range(2):
                square = dslab[:, head * LANES : (head + 1) * LANES].T
                wide = jnp.concatenate([square, jnp.zeros((LANES, LANES), f32)], axis=1)
                half = LANES // 2
                while half >= 1:
                    wide = wide[:half] + pltpu.roll(wide[half:], SPAN - half, 1)
                    half //= 2
                rel_ref[0, head : head + 1, :] = wide


def attend_backward(q, q_at, k, k_at, v, v_at, q_extra, k_extra, lows, mixed, grad, g, ranges, after=()):
    tokens = q.shape[0]
    sequences = tokens // SEQ
    biased = g is not None

    def block(at):
        return pl.BlockSpec((SEQ, LANES), lambda p, s: (s, at + p))

    shared = pl.BlockSpec((SEQ, LANES), lambda p, s: (s, 0))
    in_specs = [block(q_at), block(k_at), block(v_at), shared, shared, block(0), block(0), block(0)]
    args = [q, k, v, q_extra, k_extra, lows, mixed, grad]
    scratch = [pltpu.VMEM((SEQ, LANES), f32), pltpu.VMEM((SEQ, LANES), f32)]
    if biased:
        in_specs.append(pl.BlockSpec((1, 2, SPAN), lambda p, s: (p, 0, 0)))
        args.append(g)
        scratch += [pltpu.VMEM((SEQ, 2 * LANES), f32)] * 2
        out_specs = [
            pl.BlockSpec((3, SEQ, LANES), lambda p, s: (0, s, p)),
            pl.BlockSpec((1, 2, SPAN), lambda p, s: (p, 0, 0)),
        ]
        out_shape = [
            jax.ShapeDtypeStruct((3, tokens, INNER), bf16),
            jax.ShapeDtypeStruct((PAIRS, 2, SPAN), f32),
        ]
    else:
        out_specs = [block(0), pl.BlockSpec((2, SEQ, LANES), lambda p, s: (0, s, p))]
        out_shape = [
            jax.ShapeDtypeStruct((tokens, INNER), bf16),
            jax.ShapeDtypeStruct((2, tokens, INNER), bf16),
        ]
    seen = sum(stop - start for start, stop in ranges)
    return pl.pallas_call(
        partial(attend_backward_kernel, ranges, biased, len(after)),
        grid=(PAIRS, sequences),
        in_specs=[pl.BlockSpec(memory_space=pl.ANY)] * len(after) + in_specs,
        out_specs=out_specs,
        out_shape=out_shape,
        scratch_shapes=scratch,
        compiler_params=pltpu.CompilerParams(vmem_limit_bytes=VMEM_LIMIT),
        cost_estimate=pl.CostEstimate(
            flops=5 * 2 * PAIRS * sequences * seen * 256 * 256,
            bytes_accessed=tokens * INNER * 20,
            transcendentals=PAIRS * sequences * seen * 256,
        ),
    )(*after, *args)


def shares(core, value, keep_ref, send_ref, *at):
    rows, cols = value.shape
    parts = value.astype(bf16).reshape(2, 2, rows // 4, cols)
    for y in range(2):
        place = (y,) + at
        keep_ref[place] = jnp.where(core == 0, parts[y, 0], parts[y, 1])
        send_ref[place] = jnp.where(core == 0, parts[y, 1], parts[y, 0])


def place_pieces(where_ref, full, own, core, y, x, yc, xc):
    shard = where_ref[0]
    rows, cols = own.shape
    half = cols // 2

    def at(index):
        return pl.ds(pl.multiple_of(index * rows, rows), rows)

    full[at(shard), :] = own[...]
    full[at(shard ^ 1), :] = core[...]
    for bit in range(2):

        @pl.when(where_ref[1] == bit)
        def _():
            mine = slice(bit * half, (bit + 1) * half)
            other = slice((1 - bit) * half, (2 - bit) * half)
            full[at(shard ^ 2), mine] = y[...]
            full[at(shard ^ 2), other] = x[...]
            full[at(shard ^ 3), mine] = yc[...]
            full[at(shard ^ 3), other] = xc[...]


def whole_spec(array):
    return pl.BlockSpec(
        array.shape, lambda i, c: (0,) * array.ndim, pipeline_mode=pl.Buffered(1)
    )


def normed_rows(x, gain):
    factor = lax.rsqrt(jnp.mean(x * x, -1, keepdims=True) + eps)
    return (x * factor * gain).astype(bf16)


def first_kernel(where_ref, x_ref, onehot_ref, valid_ref, *refs):
    pieces_in = refs[:6]
    full, gains_ref, g_ref, n_ref, qkv_ref = refs[6:]

    @pl.when(pl.program_id(0) == 0)
    def _():
        place_pieces(where_ref, full, *pieces_in)
        small = full[:, 4 * INNER : 4 * INNER + LANES].astype(f32).T
        gains_ref[...] = small[0:8]
        table = small[16:32].astype(bf16)
        bias = jnp.where(valid_ref[...] > 0, dot_nn(table, onehot_ref[...]), masked_score)
        for pair in range(PAIRS):
            g_ref[pair] = bias[2 * pair : 2 * pair + 2]

    normed = normed_rows(x_ref[...].astype(f32), gains_ref[0:1, :])
    n_ref[...] = normed
    for part in range(3):
        columns = slice(part * D, (part + 1) * D)
        qkv_ref[:, columns] = dot_nn(normed, full[:, columns]).astype(bf16)


def first_step(where, x, pieces_in, onehot, valid):
    tokens = x.shape[0]
    width = pieces_in[0].shape[1]
    block = pl.BlockSpec((ROWS, D), lambda i, c: (i, 0))
    return pl.pallas_call(
        first_kernel,
        grid_spec=pltpu.PrefetchScalarGridSpec(
            num_scalar_prefetch=1,
            grid=(tokens // ROWS,),
            in_specs=[block, whole_spec(onehot), whole_spec(valid)]
            + [whole_spec(p) for p in pieces_in],
            out_specs=[
                pl.BlockSpec((D, width), lambda i, c: (0, 0)),
                pl.BlockSpec((8, D), lambda i, c: (0, 0)),
                pl.BlockSpec((PAIRS, 2, SPAN), lambda i, c: (0, 0, 0)),
                block,
                pl.BlockSpec((ROWS, 3 * INNER), lambda i, c: (i, 0)),
            ],
        ),
        out_shape=[
            jax.ShapeDtypeStruct((D, width), bf16),
            jax.ShapeDtypeStruct((8, D), f32),
            jax.ShapeDtypeStruct((PAIRS, 2, SPAN), f32),
            jax.ShapeDtypeStruct((tokens, D), bf16),
            jax.ShapeDtypeStruct((tokens, 3 * INNER), bf16),
        ],
        compiler_params=pltpu.CompilerParams(vmem_limit_bytes=VMEM_LIMIT),
        cost_estimate=pl.CostEstimate(
            flops=6 * tokens * D * D, bytes_accessed=tokens * D * 10 + D * width * 4,
            transcendentals=0,
        ),
    )(where, x, onehot, valid, *pieces_in)


def encoder_kernel(waits, where_ref, *refs):
    refs = refs[waits:]
    x_ref, pieces_in = refs[0], refs[1:7]
    full, kv_ref = refs[7:]

    @pl.when(pl.program_id(0) == 0)
    def _():
        place_pieces(where_ref, full, *pieces_in)

    for part in range(2):
        columns = slice(part * D, (part + 1) * D)
        kv_ref[:, columns] = dot_nn(x_ref[...], full[:, columns]).astype(bf16)


def encoder_step(where, x, pieces_in, after):
    tokens = x.shape[0]
    width = pieces_in[0].shape[1]
    return pl.pallas_call(
        partial(encoder_kernel, len(after)),
        grid_spec=pltpu.PrefetchScalarGridSpec(
            num_scalar_prefetch=1,
            grid=(tokens // ROWS,),
            in_specs=[pl.BlockSpec(memory_space=pl.ANY)] * len(after)
            + [pl.BlockSpec((ROWS, D), lambda i, c: (i, 0))]
            + [whole_spec(p) for p in pieces_in],
            out_specs=[
                pl.BlockSpec((D, width), lambda i, c: (0, 0)),
                pl.BlockSpec((ROWS, 2 * INNER), lambda i, c: (i, 0)),
            ],
        ),
        out_shape=[
            jax.ShapeDtypeStruct((D, width), bf16),
            jax.ShapeDtypeStruct((tokens, 2 * INNER), bf16),
        ],
        compiler_params=pltpu.CompilerParams(vmem_limit_bytes=VMEM_LIMIT),
        cost_estimate=pl.CostEstimate(
            flops=4 * tokens * D * D, bytes_accessed=tokens * D * 6 + D * width * 4,
            transcendentals=0,
        ),
    )(where, *after, x, *pieces_in)


def middle_kernel(x_ref, attn_ref, out_w_ref, gain_ref, q_w_ref, first_ref, n_ref, cq_ref):
    first = x_ref[...].astype(f32) + dot_nn(attn_ref[...], out_w_ref[...])
    first_ref[...] = first
    normed = normed_rows(first, gain_ref[...])
    n_ref[...] = normed
    cq_ref[...] = dot_nn(normed, q_w_ref[...]).astype(bf16)


def middle_step(x, attn, w_self, gain, w_cross):
    tokens = x.shape[0]
    block = pl.BlockSpec((ROWS, D), lambda i: (i, 0))
    return pl.pallas_call(
        middle_kernel,
        grid=(tokens // ROWS,),
        in_specs=[
            block,
            block,
            pl.BlockSpec((D, D), lambda i: (0, 3)),
            pl.BlockSpec((1, D), lambda i: (0, 0)),
            pl.BlockSpec((D, D), lambda i: (0, 2)),
        ],
        out_specs=[block] * 3,
        out_shape=[
            jax.ShapeDtypeStruct((tokens, D), f32),
            jax.ShapeDtypeStruct((tokens, D), bf16),
            jax.ShapeDtypeStruct((tokens, D), bf16),
        ],
        compiler_params=pltpu.CompilerParams(vmem_limit_bytes=VMEM_LIMIT),
        cost_estimate=pl.CostEstimate(
            flops=4 * tokens * D * D, bytes_accessed=tokens * D * 12 + D * D * 4, transcendentals=0
        ),
    )(x, attn, w_self, gain, w_cross)


def shares(core, value, keep_ref, send_ref, *at):
    rows, cols = value.shape
    parts = value.astype(bf16).reshape(2, 2, rows // 4, cols)
    columns = slice(0, cols)
    for y in range(2):
        place = (y,) + at + (slice(None), columns)
        keep_ref[place] = jnp.where(core == 0, parts[y, 0], parts[y, 1])
        send_ref[place] = jnp.where(core == 0, parts[y, 1], parts[y, 0])


def feed_forward_kernel(
    where_ref, x1_ref, attn_ref, w2_ref, gain_ref, dout_ref,
    own_g, own_u, core_g, core_u, y_in, x_in, yc_in, xc_in,
    own_o, core_o, y_o, x_o, yc_o, xc_o,
    layer_ref, gx_ref, gx16_ref, gk_ref, gs_ref, ok_ref, os_ref,
    wg, wu, wo, n3, n3t, acc, dn, hid, dgate, dup,
):
    step = pl.program_id(0)
    shard, across = where_ref[0], where_ref[1]
    tokens = x1_ref.shape[0]
    chunks = tokens // ROWS
    rows_in = own_g.shape[0]

    def at(index):
        return pl.ds(pl.multiple_of(index * rows_in, rows_in), rows_in)

    wg[at(shard), :] = own_g[...]
    wu[at(shard), :] = own_u[...]
    wg[at(shard ^ 1), :] = core_g[...]
    wu[at(shard ^ 1), :] = core_u[...]

    @pl.when(across == 0)
    def _():
        wg[at(shard ^ 2), :] = y_in[...]
        wu[at(shard ^ 2), :] = x_in[...]
        wg[at(shard ^ 3), :] = yc_in[...]
        wu[at(shard ^ 3), :] = xc_in[...]

    @pl.when(across == 1)
    def _():
        wg[at(shard ^ 2), :] = x_in[...]
        wu[at(shard ^ 2), :] = y_in[...]
        wg[at(shard ^ 3), :] = xc_in[...]
        wu[at(shard ^ 3), :] = yc_in[...]

    half = D // 2
    for turn, whole in ((0, own_o), (1, core_o)):

        @pl.when(step == turn)
        def _():
            wo[...] = whole[...]

    for turn, near, far in ((2, y_o, x_o), (3, yc_o, xc_o)):
        for bit in range(2):

            @pl.when((step == turn) & (across == bit))
            def _():
                wo[:, bit * half : (bit + 1) * half] = near[...]
                wo[:, (1 - bit) * half : (2 - bit) * half] = far[...]

    @pl.when(step == 0)
    def _():
        gain = gain_ref[...]
        for chunk in range(chunks):
            rows = slice(chunk * ROWS, (chunk + 1) * ROWS)
            x = x1_ref[rows, :] + dot_nn(attn_ref[rows, :], w2_ref[...])
            gx_ref[rows, :] = x
            normed = normed_rows(x, gain)
            n3[rows, :] = normed
            n3t[:, rows] = normed.T
            acc[rows, :] = jnp.zeros((ROWS, D), f32)
            dn[rows, :] = jnp.zeros((ROWS, D), f32)

    c = math.sqrt(2.0 / math.pi)
    for chunk in range(chunks):
        rows = slice(chunk * ROWS, (chunk + 1) * ROWS)
        normed = n3[rows, :]
        gate = dot_nn(normed, wg[...])
        up = dot_nn(normed, wu[...])
        dhidden = dot_nt(dout_ref[rows, :], wo[...]).astype(bf16).astype(f32)
        square = gate * gate
        t = jnp.tanh(c * gate * (1.0 + 0.044715 * square))
        mid = 0.5 * (1.0 + t)
        act = gate * mid
        slope = mid + (0.5 * c) * gate * (1.0 - t * t) * (1.0 + (3.0 * 0.044715) * square)
        hid[rows, :] = (act * up).astype(bf16)
        dgate[rows, :] = (dhidden * up * slope).astype(bf16)
        dup[rows, :] = (dhidden * act).astype(bf16)
        acc[rows, :] += dot_nn(hid[rows, :], wo[...])
        dn[rows, :] += dot_nt(dgate[rows, :], wg[...]) + dot_nt(dup[rows, :], wu[...])
    core = shard % 2
    shares(core, dot_nn(n3t[...], dgate[...]), gk_ref, gs_ref, 0)
    shares(core, dot_nn(n3t[...], dup[...]), gk_ref, gs_ref, 1)
    out_grad = dot_tn(hid[...], dout_ref[...]).astype(bf16)

    @pl.when(step % 2 == 0)
    def _():
        ok_ref[0] = out_grad

    @pl.when(step % 2 == 1)
    def _():
        os_ref[0] = out_grad

    @pl.when(step == pl.num_programs(0) - 1)
    def _():
        gain = gain_ref[...]
        for chunk in range(chunks):
            rows = slice(chunk * ROWS, (chunk + 1) * ROWS)
            x = gx_ref[rows, :]
            layer_ref[rows, :] = (x + acc[rows, :]).astype(bf16)
            factor = lax.rsqrt(jnp.mean(x * x, -1, keepdims=True) + eps)
            d = dn[rows, :]
            weighted = d * gain
            back = factor * weighted - x * (
                factor * factor * factor * jnp.mean(weighted * x, -1, keepdims=True)
            )
            gx = dout_ref[rows, :].astype(f32) + back
            gx_ref[rows, :] = gx
            gx16_ref[rows, :] = gx.astype(bf16)


def feed_forward(where, x1, attn, w_cross, gain, dout, in_pieces, out_pieces):
    tokens = x1.shape[0]
    steps = FF // FF_BLOCK
    one = pl.Buffered(1)
    rows_in = in_pieces[0].shape[0]

    def whole(width=D):
        return pl.BlockSpec((tokens, width), lambda f, c: (0, 0), pipeline_mode=one)

    def streamed(at):
        return pl.BlockSpec((rows_in, FF_BLOCK), lambda f, c: (0, at + (c[0] ^ f)))

    resident = pl.BlockSpec((tokens, D), lambda f, c: (0, 0))
    in_share = pl.BlockSpec((2, 2, D // 4, FF_BLOCK), lambda f, c: (0, 0, 0, c[0] ^ f))
    out_share = pl.BlockSpec((1, FF_BLOCK, D), lambda f, c: ((c[0] ^ f) // 2, 0, 0))
    in_type = jax.ShapeDtypeStruct((2, 2, D // 4, FF), bf16)
    out_type = jax.ShapeDtypeStruct((2, FF_BLOCK, D), bf16)
    own_i, core_i, *halves_i = in_pieces
    return pl.pallas_call(
        feed_forward_kernel,
        grid_spec=pltpu.PrefetchScalarGridSpec(
            num_scalar_prefetch=1,
            grid=(steps,),
            in_specs=[
                whole(),
                whole(),
                pl.BlockSpec((D, D), lambda f, c: (0, 3), pipeline_mode=one),
                pl.BlockSpec((1, D), lambda f, c: (0, 0)),
                whole(),
                streamed(0), streamed(steps), streamed(0), streamed(steps),
                streamed(0), streamed(0), streamed(0), streamed(0),
            ]
            + [whole_spec(p) for p in out_pieces],
            out_specs=[resident, resident, resident, in_share, in_share, out_share, out_share],
            scratch_shapes=[
                pltpu.VMEM((D, FF_BLOCK), bf16),
                pltpu.VMEM((D, FF_BLOCK), bf16),
                pltpu.VMEM((FF_BLOCK, D), bf16),
                pltpu.VMEM((tokens, D), bf16),
                pltpu.VMEM((D, tokens), bf16),
                pltpu.VMEM((tokens, D), f32),
                pltpu.VMEM((tokens, D), f32),
                pltpu.VMEM((tokens, FF_BLOCK), bf16),
                pltpu.VMEM((tokens, FF_BLOCK), bf16),
                pltpu.VMEM((tokens, FF_BLOCK), bf16),
            ],
        ),
        out_shape=[
            jax.ShapeDtypeStruct((tokens, D), bf16),
            jax.ShapeDtypeStruct((tokens, D), f32),
            jax.ShapeDtypeStruct((tokens, D), bf16),
            in_type, in_type, out_type, out_type,
        ],
        compiler_params=pltpu.CompilerParams(vmem_limit_bytes=VMEM_LIMIT),
        cost_estimate=pl.CostEstimate(
            flops=18 * tokens * D * FF,
            bytes_accessed=tokens * D * 16 + 12 * D * FF,
            transcendentals=tokens * FF,
        ),
    )(where, x1, attn, w_cross, gain, dout, own_i, own_i, core_i, core_i, *halves_i, *out_pieces)


def weight_grad_kernel(counts, firsts, waits, core_ref, *refs):
    refs = refs[waits:]
    terms = len(counts)
    lefts, rights = refs[0:terms], refs[terms : 2 * terms]
    refs = refs[2 * terms :]
    second = firsts is not None
    if second:
        tiny_ref, keep_ref, send_ref, keep2_ref, send2_ref, left_t = refs
    else:
        keep_ref, send_ref, left_t = refs
    step = pl.program_id(0)
    core = core_ref[0] % 2
    at = 0
    for left, right, count in zip(lefts, rights, counts):

        @pl.when(step == at)
        def _():
            left_t[...] = left[...].T

        @pl.when((step >= at) & (step < at + count))
        def _():
            block = right[...] if len(right.shape) == 2 else right[0]
            value = dot_nn(left_t[...], block)
            if not second:
                shares(core, value, keep_ref, send_ref)
            else:

                @pl.when(step < firsts)
                def _():
                    shares(core, value, keep_ref, send_ref)

                @pl.when(step >= firsts)
                def _():
                    shares(core, value, keep2_ref, send2_ref)
                    tiny = tiny_ref[...]
                    for y in range(2):
                        keep2_ref[y, :, D:] = jnp.where(core == 0, tiny[y, 0], tiny[y, 1])
                        send2_ref[y, :, D:] = jnp.where(core == 0, tiny[y, 1], tiny[y, 0])

        at += count


def weight_grad(where, terms, tiny=None, after=()):
    tokens = terms[0][0].shape[0]
    counts = []
    rights = []
    at = 0
    for _, right in terms:
        deep = right.ndim == 3
        count = right.shape[0] if deep else 1

        def place(j, c, at=at, count=count, deep=deep):
            return (jnp.clip(j - at, 0, count - 1), 0, 0) if deep else (0, 0)

        rights.append(pl.BlockSpec((1, tokens, D) if deep else (tokens, D), place))
        counts.append(count)
        at += count
    firsts = None if tiny is None else at - 1
    blocks = at if tiny is None else at - 1
    share = pl.BlockSpec((2, D // 4, D), lambda j, c: (0, 0, jnp.minimum(j, blocks - 1)))
    out_specs = [share, share]
    out_shape = [jax.ShapeDtypeStruct((2, D // 4, blocks * D), bf16)] * 2
    extra_specs, extra = [], []
    if tiny is not None:
        extra_specs, extra = [pl.BlockSpec(tiny.shape, lambda j, c: (0, 0, 0, 0))], [tiny]
        wide = D + tiny.shape[-1]
        out_specs += [pl.BlockSpec((2, D // 4, wide), lambda j, c: (0, 0, 0))] * 2
        out_shape += [jax.ShapeDtypeStruct((2, D // 4, wide), bf16)] * 2
    return pl.pallas_call(
        partial(weight_grad_kernel, counts, firsts, len(after)),
        grid_spec=pltpu.PrefetchScalarGridSpec(
            num_scalar_prefetch=1,
            grid=(at,),
            in_specs=[pl.BlockSpec(memory_space=pl.ANY)] * len(after)
            + [pl.BlockSpec((tokens, D), lambda j, c: (0, 0))] * len(terms)
            + rights
            + extra_specs,
            out_specs=out_specs,
            scratch_shapes=[pltpu.VMEM((D, tokens), bf16)],
        ),
        out_shape=out_shape,
        compiler_params=pltpu.CompilerParams(vmem_limit_bytes=VMEM_LIMIT),
        cost_estimate=pl.CostEstimate(
            flops=2 * tokens * D * D * at,
            bytes_accessed=tokens * D * (len(terms) + at) * 2 + D * D * at * 2,
            transcendentals=0,
        ),
    )(where, *after, *[left for left, _ in terms], *[right for _, right in terms], *extra)


def norm_back_kernel(normed, onward, waits, *refs):
    refs = refs[waits:]
    grad_ref, w_ref = refs[:2]
    total = None
    for part in range(grad_ref.shape[0]):
        term = dot_nt(grad_ref[part], w_ref[:, part * D : (part + 1) * D])
        total = term if total is None else total + term
    if not normed:
        refs[2][...] = total.astype(refs[2].dtype)
        return
    x_ref, gain_ref, up_ref = refs[2:5]
    refs = refs[5:]
    if onward:
        next_ref, out_ref, gain_grad_ref, out16_ref, onward_ref = refs
    else:
        out_ref, gain_grad_ref = refs
    x = x_ref[...].astype(f32)
    factor = lax.rsqrt(jnp.mean(x * x, -1, keepdims=True) + eps)
    weighted = total * gain_ref[...]
    grad_gain = jnp.sum(total * x * factor, axis=0, keepdims=True)

    @pl.when(pl.program_id(0) == 0)
    def _():
        gain_grad_ref[...] = jnp.zeros_like(gain_grad_ref)

    gain_grad_ref[...] += grad_gain
    scale = factor * factor * factor * jnp.mean(weighted * x, -1, keepdims=True)
    out = up_ref[...] + factor * weighted - x * scale
    out_ref[...] = out
    if onward:
        out16 = out.astype(bf16)
        out16_ref[...] = out16
        onward_ref[...] = dot_nt(out16, next_ref[...]).astype(bf16)


def norm_back(
    grads, w, w_at, x=None, gain=None, upstream=None, w_next=None, next_at=0, after=(), kind=f32
):
    if grads.ndim == 2:
        grads = grads[None]
    parts, tokens, _ = grads.shape
    block = pl.BlockSpec((ROWS, D), lambda i: (i, 0))
    row = pl.BlockSpec((1, D), lambda i: (0, 0))
    in_specs = [pl.BlockSpec(memory_space=pl.ANY)] * len(after)
    in_specs += [
        pl.BlockSpec((parts, ROWS, D), lambda i: (0, i, 0)),
        pl.BlockSpec((D, parts * D), lambda i: (0, w_at)),
    ]
    args = [*after, grads, w]
    wide = jax.ShapeDtypeStruct((tokens, D), kind)
    half = jax.ShapeDtypeStruct((tokens, D), bf16)
    out_specs, out_shape = [block], [wide]
    if x is not None:
        in_specs += [block, row, block]
        args += [x, gain, upstream]
        out_specs.append(row)
        out_shape.append(jax.ShapeDtypeStruct((1, D), f32))
        if w_next is not None:
            in_specs.append(pl.BlockSpec((D, D), lambda i: (0, next_at)))
            args.append(w_next)
            out_specs += [block, block]
            out_shape += [half, half]
    return pl.pallas_call(
        partial(norm_back_kernel, x is not None, w_next is not None, len(after)),
        grid=(tokens // ROWS,),
        in_specs=in_specs,
        out_specs=out_specs,
        out_shape=out_shape,
        compiler_params=pltpu.CompilerParams(vmem_limit_bytes=VMEM_LIMIT),
        cost_estimate=pl.CostEstimate(
            flops=2 * tokens * D * D * (parts + (w_next is not None)),
            bytes_accessed=tokens * D * (2 * parts + 12) + D * D * 2 * parts,
            transcendentals=0,
        ),
    )(*args)


def exchange(array, axis, size, bit):
    return lax.ppermute(array, axis, [(i, i ^ bit) for i in range(size)])


def part_of(array, dim, index):
    half = array.shape[dim] // 2
    return lax.dynamic_slice_in_dim(array, index * half, half, dim)


def tie(value, *others):
    return lax.optimization_barrier((value, *others))[0]


class Gather:
    def __init__(self, own, sizes, *after):
        self.sizes = sizes
        self.own = own
        half = part_of(own, 1, lax.axis_index("rep") % 2)
        if after:
            half = tie(half, *after)
        self.half = half
        self.y = exchange(half, "shard", sizes[0], 2)

    def cross(self, *after):
        if after:
            self.y = tie(self.y, *after)
        self.x = exchange(self.y, "rep", self.sizes[1], 1)
        self.core = exchange(tie(self.own, self.y), "shard", self.sizes[0], 1)
        self.yc = exchange(self.y, "shard", self.sizes[0], 1)

    def pieces(self, *after):
        if after:
            self.x = tie(self.x, *after)
        xc = exchange(self.x, "shard", self.sizes[0], 1)
        return self.own, self.core, self.y, self.x, self.yc, xc


class Chain:
    def __init__(self, keep, send, sizes, dims, order):
        self.shards, self.reps = sizes
        self.bits = [1 << b for b in range(self.reps.bit_length() - 1)]
        self.dims = [dims[min(i, len(dims) - 1)] for i in range(len(self.bits))]
        steps = []
        for name in order:
            if name == "y":
                steps.append(("shard", 2, 0))
            else:
                steps += [("rep", bit, dim) for bit, dim in zip(self.bits, self.dims)]
        self.steps = steps
        self.kept = [keep]
        self.got = exchange(send, "shard", self.shards, 1)
        self.sent = send
        self.at = 0

    def own(self):
        while self.at < len(self.steps):
            self.advance()
        total = self.got.astype(f32)
        for part in self.kept:
            total = total + part.astype(f32)
        return total.astype(bf16)

    def advance(self, *after):
        if after:
            self.got = tie(self.got, *after)
        axis, bit, dim = self.steps[self.at]
        self.at += 1
        mine = (lax.axis_index(axis) // bit) % 2
        size = self.shards if axis == "shard" else self.reps
        parts = self.kept + [self.got]
        total = None
        for part in parts:
            term = part_of(part, dim, 1 - mine).astype(f32)
            total = term if total is None else total + term
        self.sent = total.astype(bf16)
        self.kept = [part_of(part, dim, mine) for part in parts]
        self.got = exchange(self.sent, axis, size, bit)
        return self.got


def spread(own, sizes, bits, dims):
    rep = lax.axis_index("rep")
    for bit, dim in zip(reversed(bits), reversed(dims)):
        got = exchange(own, "rep", sizes[1], bit)
        mine = (rep // bit) % 2
        low = jnp.where(mine == 0, own, got)
        high = jnp.where(mine == 0, got, own)
        own = jnp.concatenate([low, high], axis=dim)
    return own


def unpack_kernel(blocks_ref, w_ref, in_ref, out_ref, sum_ref):
    reps, _, rows, cols = blocks_ref.shape
    out_rows = out_ref.shape[0] // reps
    total = jnp.zeros((rows, LANES), f32)
    for rep in range(reps):
        turned = int(format(rep, "0%db" % (reps.bit_length() - 1))[::-1], 2)
        for part in range(2):
            place = slice(part * FF + turned * cols, part * FF + (turned + 1) * cols)
            block = blocks_ref[rep, part].astype(f32)
            in_ref[:, place] = block
            product = block * w_ref[:, place].astype(f32)
            for lane in range(0, cols, LANES):
                total = total + product[:, lane : lane + LANES]
        out_place = slice(turned * out_rows, (turned + 1) * out_rows)
        for group in range(D // cols):
            out_ref[out_place, group * cols : (group + 1) * cols] = blocks_ref[
                rep, 2, group * out_rows : (group + 1) * out_rows, :
            ].astype(f32)
    row = jnp.broadcast_to(jnp.sum(total, axis=1, keepdims=True), (rows, LANES)).T
    sum_ref[...] = row[0:8]


def unpack(blocks, w):
    reps, _, rows, cols = blocks.shape
    return pl.pallas_call(
        unpack_kernel,
        out_shape=[
            jax.ShapeDtypeStruct((rows, 2 * FF), f32),
            jax.ShapeDtypeStruct((FF * rows // D, D), f32),
            jax.ShapeDtypeStruct((8, rows), f32),
        ],
        compiler_params=pltpu.CompilerParams(vmem_limit_bytes=VMEM_LIMIT),
        cost_estimate=pl.CostEstimate(
            flops=4 * rows * FF, bytes_accessed=rows * FF * 16, transcendentals=0
        ),
    )(blocks, w)


def bias_rows(shards):
    lane = np.arange(SPAN)
    distance = np.where(lane < SEQ, SEQ - LANES - lane, 2 * SEQ - lane)
    bucket = np.zeros(SPAN, np.int64)
    for edge in bucket_edges:
        bucket += distance >= edge
    valid = (distance >= 0) & (distance < SEQ)
    onehot = np.zeros((SPAN, NUM_BUCKETS), np.float32)
    onehot[np.arange(SPAN)[valid], bucket[valid]] = 1.0
    own = NUM_BUCKETS // shards
    rows = np.arange(NUM_BUCKETS) // own * (D // shards) + np.arange(NUM_BUCKETS) % own
    placed = np.zeros((D, SPAN), np.float32)
    placed[rows] = onehot.T
    return onehot, placed, valid[None].astype(np.float32)


def local(
    sizes,
    hidden_in,
    enc_states,
    dec_segments,
    enc_segments,
    out_grad,
    gains,
    rel_table,
    self_qkv,
    self_out,
    cross_q,
    cross_kv,
    cross_out,
    ff_in,
    ff_out,
):
    shards, reps = sizes
    own_rows = D // shards
    own_buckets = NUM_BUCKETS // shards
    width = reps.bit_length() - 1
    shard = lax.axis_index("shard")
    where = jnp.stack([shard, lax.axis_index("rep") % 2]).astype(jnp.int32)
    small = jnp.concatenate(
        [
            gains.T,
            jnp.zeros((own_rows, 13), bf16),
            jnp.pad(rel_table, ((0, own_rows - own_buckets), (0, 2 * LANES - 16 - HEADS))),
        ],
        axis=1,
    )
    self_set = Gather(jnp.concatenate([self_qkv, self_out, small], axis=1), sizes)
    self_set.cross()
    cross_set = Gather(
        jnp.concatenate([cross_kv, cross_q, cross_out], axis=1), sizes, self_set.y
    )
    self_pieces = self_set.pieces()

    lane = jnp.arange(LANES, dtype=jnp.int32)[None, :]
    dec_ids = dec_segments[:, None]
    enc_ids = enc_segments[:, None]
    ones = ((lane % HEAD_DIM >= 2) & (lane % HEAD_DIM <= 4)).astype(f32)

    def key_extra(ids):
        return jnp.where(lane < 2, jnp.where(lane != ids, masked_score, 0.0), ones).astype(bf16)

    q_extra = ((lane < 2) & (lane == dec_ids)).astype(bf16)
    self_extra = key_extra(dec_ids)
    cross_extra = key_extra(enc_ids)
    onehot, placed, valid = bias_rows(shards)
    w_self, gains_all, g, normed_one, qkv = first_step(
        where, hidden_in, self_pieces, placed.astype(bf16), valid
    )
    cross_set.cross(normed_one)
    out_set = Gather(ff_out, sizes, cross_set.y, normed_one)
    in_set = Gather(ff_in, sizes, cross_set.y, normed_one)
    attn_one, lows_one = attend_forward(
        qkv, 0, qkv, PAIRS, qkv, 2 * PAIRS, q_extra, self_extra, g, SELF_RANGES,
        after=[out_set.half, in_set.half],
    )
    cross_pieces = cross_set.pieces(attn_one)
    out_set.cross(attn_one)
    in_set.cross(attn_one)
    w_cross, ckv = encoder_step(where, enc_states, cross_pieces, [attn_one])
    first, normed_two, cq = middle_step(hidden_in, attn_one, w_self, gains_all[1:2], w_cross)
    attn_two, lows_two = attend_forward(
        cq, 0, ckv, 0, ckv, PAIRS, q_extra, cross_extra, None, CROSS_RANGES
    )
    ff_out_pieces = out_set.pieces(attn_two)
    ff_in_pieces = in_set.pieces(attn_two)
    layer_out, grad_second, out_two, in_keep, in_send, out_keep, out_send = feed_forward(
        where, first, attn_two, w_cross, gains_all[2:3], out_grad, ff_in_pieces, ff_out_pieces
    )
    ff_in_chain = Chain(in_keep, in_send, sizes, [3], "yr")
    ff_out_chain = Chain(out_keep, out_send, sizes, [1], "ry")
    (grad_attn_two,) = norm_back(out_two, w_cross, 3, kind=bf16, after=[layer_out])
    ff_out_chain.advance(grad_attn_two)
    ff_in_chain.advance(grad_attn_two)
    grad_cq, grad_ckv = attend_backward(
        cq, 0, ckv, 0, ckv, PAIRS, q_extra, cross_extra, lows_two, attn_two, grad_attn_two,
        None, CROSS_RANGES, after=[ff_in_chain.sent, ff_out_chain.sent],
    )
    ff_out_chain.advance(grad_cq)
    grad_first, _, out_one, grad_attn_one = norm_back(
        grad_cq, w_cross, 2, first, gains_all[1:2], grad_second, w_self, 3,
        after=[ff_out_chain.sent],
    )
    ff_in_chain.advance(grad_attn_one)
    ff_out_chain.advance(grad_attn_one)
    cross_keep, cross_send = weight_grad(
        where,
        [(enc_states, grad_ckv), (normed_two, grad_cq), (attn_two, out_two), (attn_one, out_one)],
        after=[ff_in_chain.sent, ff_out_chain.sent],
    )
    cross_chain = Chain(cross_keep, cross_send, sizes, [2, 1], "yr")
    (enc_grad,) = norm_back(grad_ckv, w_cross, 0, after=[cross_keep])
    ff_in_chain.advance(enc_grad)
    ff_out_chain.advance(enc_grad)
    cross_chain.advance(enc_grad)
    grad_qkv, rel_part = attend_backward(
        qkv, 0, qkv, PAIRS, qkv, 2 * PAIRS, q_extra, self_extra, lows_one, attn_one,
        grad_attn_one, g, SELF_RANGES,
        after=[cross_chain.sent, ff_out_chain.sent, ff_in_chain.sent],
    )
    ff_in_chain.advance(grad_qkv)
    cross_chain.advance(grad_qkv)
    table_part = jnp.einsum(
        "hu,ub->bh",
        rel_part.reshape(HEADS, SPAN),
        onehot,
        precision=lax.Precision.HIGHEST,
        preferred_element_type=f32,
    )
    tiny = table_part.reshape(2, 2, own_buckets, HEADS).astype(bf16)
    tiny = jnp.pad(tiny, ((0, 0), (0, 0), (0, own_rows - own_buckets), (0, 2 * LANES - HEADS)))
    self_keep, self_send, last_keep, last_send = weight_grad(
        where, [(normed_one, grad_qkv)], tiny=tiny, after=[ff_in_chain.sent, cross_chain.sent]
    )
    self_chain = Chain(self_keep, self_send, sizes, [2, 1], "yr")
    last_chain = Chain(last_keep, last_send, sizes, [2, 1], "ry")
    cross_chain.advance(self_keep)
    in_own = ff_in_chain.own()[0]
    out_own = ff_out_chain.own()[0]
    rows, columns = in_own.shape[1:]
    out_rows = out_own.shape[0]
    out_own = out_own.reshape(out_rows, -1, columns).transpose(1, 0, 2).reshape(1, rows, columns)
    blocks = lax.all_gather(
        tie(jnp.concatenate([in_own, out_own], axis=0), self_keep), "rep", axis=0
    )
    self_chain.advance(self_keep)
    last_chain.advance(self_keep)
    in_grad, _ = norm_back(
        grad_qkv, w_self, 0, hidden_in, gains_all[0:1], grad_first,
        after=[self_chain.sent, last_chain.sent, cross_chain.sent],
    )
    self_chain.advance(in_grad)
    last_chain.advance(in_grad)
    cross_chain.advance(in_grad)
    while last_chain.at < len(last_chain.steps):
        if self_chain.at < len(self_chain.steps):
            self_chain.advance()
        last_chain.advance()
    cross_grad = spread(cross_chain.own(), sizes, cross_chain.bits, cross_chain.dims)
    self_width = self_chain.own().shape[2]
    self_own = jnp.concatenate([self_chain.own(), last_chain.own()], axis=2)
    self_all = spread(self_own, sizes, self_chain.bits[1:], self_chain.dims[1:])
    other = exchange(self_all, "rep", reps, 1)
    here = lax.axis_index("rep") % 2
    low = jnp.where(here == 0, self_all, other)[0]
    high = jnp.where(here == 0, other, self_all)[0]
    self_grad = jnp.concatenate(
        [low[:, :self_width], high[:, :self_width], low[:, self_width:], high[:, self_width:]],
        axis=1,
    ).astype(f32)
    cross_grad = cross_grad[0].astype(f32)

    if reps == 8:
        ff_in_grad, ff_out_grad, in_sums = unpack(blocks, ff_in)
        in_sums = in_sums[0]
    else:
        blocks = blocks.reshape((2,) * width + blocks.shape[1:])
        order = list(reversed(range(width)))
        in_grads = blocks[..., :2, :, :].transpose([width + 1, width] + order + [width + 2])
        ff_in_grad = in_grads.reshape(own_rows, 2 * FF).astype(f32)
        out_grads = blocks[..., 2, :, :].reshape((2,) * width + (-1, out_rows, columns))
        out_grads = out_grads.transpose(order + [width + 1, width, width + 2])
        ff_out_grad = out_grads.reshape(ff_out.shape).astype(f32)
        in_sums = jnp.sum(ff_in.astype(f32) * ff_in_grad, axis=1)

    self_qkv_grad = self_grad[:, : 3 * INNER]
    cross_query_gradient = cross_grad[:, 2 * INNER : 3 * INNER]

    sums = jnp.stack(
        [
            jnp.sum(self_qkv.astype(f32) * self_qkv_grad, axis=1),
            jnp.sum(cross_q.astype(f32) * cross_query_gradient, axis=1),
            in_sums,
        ]
    )
    gains_grad = sums / gains.astype(f32)
    rel_table_grad = self_grad[:own_buckets, 3 * INNER : 3 * INNER + HEADS]
    return (
        layer_out,
        in_grad,
        enc_grad,
        gains_grad,
        rel_table_grad,
        self_qkv_grad,
        cross_grad[:, 3 * INNER + D :],
        cross_query_gradient,
        cross_grad[:, : 2 * INNER],
        cross_grad[:, 3 * INNER : 3 * INNER + D],
        ff_in_grad,
        ff_out_grad,
    )


def solution(mesh):
    tokens = P(("rep", "shard"), None)
    ids = P(("rep", "shard"))
    rows = P("shard", None)
    columns = P(None, "shard")
    in_specs = (tokens, tokens, ids, ids, tokens, columns) + (rows,) * 8
    out_specs = (tokens, tokens, tokens, columns) + (rows,) * 8
    sizes = (mesh.shape["shard"], mesh.shape["rep"])
    return jax.shard_map(
        partial(local, sizes), mesh=mesh, in_specs=in_specs, out_specs=out_specs, check_vma=False
    )
```

```python
from functools import partial
import math

import jax
import jax.numpy as jnp
import numpy as np
from jax import lax
from jax.experimental import pallas as pl
from jax.experimental.pallas import tpu as pltpu
from jax.sharding import PartitionSpec as P

HEADS = 12
HEAD_DIM = 64
FF = 2048
NUM_BUCKETS = 32
SEQ = 512
D = 768
INNER = HEADS * HEAD_DIM
PAIRS = HEADS // 2
LANES = 128
SPAN = SEQ + LANES
FF_BLOCK = 512
ROWS = 256

eps = 1e-06
masked_score = -1e30
bf16 = jnp.bfloat16
f32 = jnp.float32
VMEM_LIMIT = 56 * 1024 * 1024
LIGHT = pl.CostEstimate(flops=1000000, bytes_accessed=100000, transcendentals=0)

bucket_edges = np.array(
    list(range(1, 16)) + [int(math.ceil(16.0 * 8.0 ** ((b - 16) / 16.0))) for b in range(16, 32)],
    dtype=np.int32,
)

SELF_RANGES = ((0, 128), (0, 256), (0, 384), (128, 512))
CROSS_RANGES = ((0, 384), (0, 512), (0, 512), (128, 512))


def dot_nn(a, b):
    return lax.dot_general(a, b, (((1,), (0,)), ((), ())), preferred_element_type=f32)


def dot_nt(a, b):
    return lax.dot_general(a, b, (((1,), (1,)), ((), ())), preferred_element_type=f32)


def dot_tn(a, b):
    return lax.dot_general(a, b, (((0,), (0,)), ((), ())), preferred_element_type=f32)


def half_masks():
    lane = lax.broadcasted_iota(jnp.int32, (1, LANES), 1)
    low = (lane < HEAD_DIM).astype(f32)
    return low.astype(bf16), (1.0 - low).astype(bf16)


def pieces(value):
    lane = lax.broadcasted_iota(jnp.int32, value.shape, 1) % HEAD_DIM
    high = value.astype(bf16).astype(f32)
    rest = value - high
    middle = rest.astype(bf16).astype(f32)
    last = rest - middle
    return jnp.where(
        lane == 2, high, jnp.where(lane == 3, middle, jnp.where(lane == 4, last, 0.0))
    )


def stacked(block, low, high):
    return jnp.concatenate([block * low, block * high], axis=0)


def toeplitz(row):
    wide = jnp.broadcast_to(row, (LANES, SPAN))
    return pltpu.roll(wide, 0, 1, stride=1, stride_axis=0)[:, :SEQ]


def attend_forward_kernel(ranges, biased, waits, *refs):
    refs = refs[waits:]
    if biased:
        q_ref, k_ref, v_ref, qa_ref, ka_ref, g_ref, o_ref, l_ref, slab = refs

        @pl.when(pl.program_id(1) == 0)
        def _():
            slab[0:LANES] = toeplitz(g_ref[0, 0:1, :])
            slab[LANES : 2 * LANES] = toeplitz(g_ref[0, 1:2, :])
    else:
        q_ref, k_ref, v_ref, qa_ref, ka_ref, o_ref, l_ref = refs
    low, high = half_masks()
    keys = jnp.concatenate([k_ref[...], ka_ref[...]], axis=1)
    values = jnp.concatenate([v_ref[...], jnp.ones((SEQ, LANES), bf16)], axis=1)
    lane = lax.broadcasted_iota(jnp.int32, (LANES, LANES), 1)
    for block, (start, stop) in enumerate(ranges):
        rows = slice(block * LANES, (block + 1) * LANES)
        extra = qa_ref[rows, :]
        left = jnp.concatenate(
            [stacked(q_ref[rows, :], low, high), jnp.concatenate([extra, extra], axis=0)], axis=1
        )
        scores = dot_nt(left, keys[start:stop])
        if biased:
            scores = scores + slab[:, SEQ - (stop - start) :]
        top = jnp.max(scores, axis=1, keepdims=True)
        expd = jnp.exp(scores - top)
        mixed = dot_nn(expd.astype(bf16), values[start:stop])
        total = mixed[:, LANES:]
        mixed = mixed[:, :LANES] / total
        o_ref[rows, :] = jnp.where(lane < HEAD_DIM, mixed[:LANES], mixed[LANES:]).astype(bf16)
        negative = pieces(-(top + jnp.log(total)))
        l_ref[rows, :] = jnp.where(lane < HEAD_DIM, negative[:LANES], negative[LANES:]).astype(bf16)


def attend_forward(q, q_at, k, k_at, v, v_at, q_extra, k_extra, g, ranges, after=()):
    tokens = q.shape[0]
    sequences = tokens // SEQ
    biased = g is not None

    def block(at):
        return pl.BlockSpec((SEQ, LANES), lambda p, s: (s, at + p))

    shared = pl.BlockSpec((SEQ, LANES), lambda p, s: (s, 0))
    in_specs = [block(q_at), block(k_at), block(v_at), shared, shared]
    args = [q, k, v, q_extra, k_extra]
    scratch = []
    if biased:
        in_specs.append(pl.BlockSpec((1, 2, SPAN), lambda p, s: (p, 0, 0)))
        args.append(g)
        scratch.append(pltpu.VMEM((2 * LANES, SEQ), f32))
    seen = sum(stop - start for start, stop in ranges)
    return pl.pallas_call(
        partial(attend_forward_kernel, ranges, biased, len(after)),
        grid=(PAIRS, sequences),
        in_specs=[pl.BlockSpec(memory_space=pl.ANY)] * len(after) + in_specs,
        out_specs=[block(0), block(0)],
        out_shape=[jax.ShapeDtypeStruct((tokens, INNER), bf16)] * 2,
        scratch_shapes=scratch,
        compiler_params=pltpu.CompilerParams(vmem_limit_bytes=VMEM_LIMIT),
        cost_estimate=LIGHT,
    )(*after, *args)


def attend_backward_kernel(ranges, biased, waits, *refs):
    refs = refs[waits:]
    if biased:
        (q_ref, k_ref, v_ref, qa_ref, ka_ref, l_ref, o_ref, d_ref, g_ref) = refs[:9]
        out_ref, rel_ref, dk, dv, slab, dslab = refs[9:]

        @pl.when(pl.program_id(1) == 0)
        def _():
            slab[:, 0:LANES] = toeplitz(g_ref[0, 0:1, :]).T
            slab[:, LANES : 2 * LANES] = toeplitz(g_ref[0, 1:2, :]).T
            dslab[...] = jnp.zeros_like(dslab)
    else:
        (q_ref, k_ref, v_ref, qa_ref, ka_ref, l_ref, o_ref, d_ref) = refs[:8]
        dq_ref, out_ref, dk, dv = refs[8:]
    low, high = half_masks()
    low_lane = lax.broadcasted_iota(jnp.int32, (LANES, LANES), 1) < HEAD_DIM
    low_row = lax.broadcasted_iota(jnp.int32, (LANES, LANES), 0) < HEAD_DIM
    keys = jnp.concatenate([k_ref[...], ka_ref[...]], axis=1)
    values = jnp.concatenate([v_ref[...], ka_ref[...]], axis=1)
    keys_t = k_ref[...].T
    dk[...] = jnp.zeros_like(dk)
    dv[...] = jnp.zeros_like(dv)
    for block, (start, stop) in enumerate(ranges):
        rows = slice(block * LANES, (block + 1) * LANES)
        seen = slice(start, stop)
        q2 = stacked(q_ref[rows, :], low, high)
        extra = qa_ref[rows, :]
        totals = l_ref[rows, :]
        q_right = jnp.concatenate(
            [q2, jnp.concatenate([extra + totals * low, extra + totals * high], axis=0)], axis=1
        )
        scores = dot_nt(keys[seen], q_right)
        if biased:
            scores = scores + slab[SEQ - (stop - start) :, :]
        probs = jnp.exp(scores)
        grad = d_ref[rows, :]
        d2 = stacked(grad, low, high)
        product = grad.astype(f32) * o_ref[rows, :].astype(f32)
        sum_low = jnp.sum(jnp.where(low_lane, product, 0.0), axis=1, keepdims=True)
        sum_high = jnp.sum(jnp.where(low_lane, 0.0, product), axis=1, keepdims=True)
        delta = pieces(
            -jnp.concatenate(
                [
                    jnp.broadcast_to(sum_low, (LANES, LANES)),
                    jnp.broadcast_to(sum_high, (LANES, LANES)),
                ],
                axis=0,
            )
        ).astype(bf16)
        lows = jnp.concatenate([delta[:LANES] * low, delta[LANES:] * high], axis=0)
        d_right = jnp.concatenate([d2, lows], axis=1)
        grad_scores = probs * dot_nt(values[seen], d_right)
        probs16 = probs.astype(bf16)
        scores16 = grad_scores.astype(bf16)
        dv[seen, :] += dot_nn(probs16, d2)
        dk[seen, :] += dot_nn(scores16, q2)
        dq = dot_nn(keys_t[:, seen], scores16)
        dq = jnp.where(low_row, dq[:, :LANES], dq[:, LANES:]).T.astype(bf16)
        if biased:
            out_ref[0, rows, :] = dq
            dslab[SEQ - (stop - start) :, :] += grad_scores
        else:
            dq_ref[rows, :] = dq
    first = 1 if biased else 0
    out_ref[first] = dk[...].astype(bf16)
    out_ref[first + 1] = dv[...].astype(bf16)
    if biased:

        @pl.when(pl.program_id(1) == pl.num_programs(1) - 1)
        def _():
            for head in range(2):
                square = dslab[:, head * LANES : (head + 1) * LANES].T
                wide = jnp.concatenate([square, jnp.zeros((LANES, LANES), f32)], axis=1)
                half = LANES // 2
                while half >= 1:
                    wide = wide[:half] + pltpu.roll(wide[half:], SPAN - half, 1)
                    half //= 2
                rel_ref[0, head : head + 1, :] = wide


def attend_backward(q, q_at, k, k_at, v, v_at, q_extra, k_extra, lows, mixed, grad, g, ranges, after=(),
                    first=0, pairs=PAIRS, into=None):
    tokens = q.shape[0]
    sequences = tokens // SEQ
    biased = g is not None

    def block(at):
        return pl.BlockSpec((SEQ, LANES), lambda p, s: (s, at + first + p))

    shared = pl.BlockSpec((SEQ, LANES), lambda p, s: (s, 0))
    in_specs = [block(q_at), block(k_at), block(v_at), shared, shared, block(0), block(0), block(0)]
    args = [q, k, v, q_extra, k_extra, lows, mixed, grad]
    scratch = [pltpu.VMEM((SEQ, LANES), f32), pltpu.VMEM((SEQ, LANES), f32)]
    if biased:
        in_specs.append(pl.BlockSpec((1, 2, SPAN), lambda p, s: (first + p, 0, 0)))
        args.append(g)
        scratch += [pltpu.VMEM((SEQ, 2 * LANES), f32)] * 2
        out_specs = [
            pl.BlockSpec((3, SEQ, LANES), lambda p, s: (0, s, first + p)),
            pl.BlockSpec((1, 2, SPAN), lambda p, s: (p, 0, 0)),
        ]
        out_shape = [
            jax.ShapeDtypeStruct((3, tokens, INNER), bf16),
            jax.ShapeDtypeStruct((pairs, 2, SPAN), f32),
        ]
    else:
        out_specs = [block(0), pl.BlockSpec((2, SEQ, LANES), lambda p, s: (0, s, p))]
        out_shape = [
            jax.ShapeDtypeStruct((tokens, INNER), bf16),
            jax.ShapeDtypeStruct((2, tokens, INNER), bf16),
        ]
    aliases = {}
    if into is not None:
        after = [into, *after]
        aliases = {0: 0}
    return pl.pallas_call(
        partial(attend_backward_kernel, ranges, biased, len(after)),
        grid=(pairs, sequences),
        in_specs=[pl.BlockSpec(memory_space=pl.ANY)] * len(after) + in_specs,
        out_specs=out_specs,
        out_shape=out_shape,
        scratch_shapes=scratch,
        input_output_aliases=aliases,
        compiler_params=pltpu.CompilerParams(vmem_limit_bytes=VMEM_LIMIT),
        cost_estimate=LIGHT,
    )(*after, *args)


def shares(core, value, keep_ref, send_ref, *at):
    rows, cols = value.shape
    parts = value.astype(bf16).reshape(2, 2, rows // 4, cols)
    for y in range(2):
        place = (y,) + at
        keep_ref[place] = jnp.where(core == 0, parts[y, 0], parts[y, 1])
        send_ref[place] = jnp.where(core == 0, parts[y, 1], parts[y, 0])


def place_pieces(where_ref, full, own, core, y, x, yc, xc):
    shard = where_ref[0]
    rows, cols = own.shape
    half = cols // 2

    def at(index):
        return pl.ds(pl.multiple_of(index * rows, rows), rows)

    full[at(shard), :] = own[...]
    full[at(shard ^ 1), :] = core[...]
    for bit in range(2):

        @pl.when(where_ref[1] == bit)
        def _():
            mine = slice(bit * half, (bit + 1) * half)
            other = slice((1 - bit) * half, (2 - bit) * half)
            full[at(shard ^ 2), mine] = y[...]
            full[at(shard ^ 2), other] = x[...]
            full[at(shard ^ 3), mine] = yc[...]
            full[at(shard ^ 3), other] = xc[...]


def whole_spec(array):
    return pl.BlockSpec(
        array.shape, lambda i, c: (0,) * array.ndim, pipeline_mode=pl.Buffered(1)
    )


def normed_rows(x, gain):
    factor = lax.rsqrt(jnp.mean(x * x, -1, keepdims=True) + eps)
    return (x * factor * gain).astype(bf16)


def first_kernel(where_ref, x_ref, onehot_ref, valid_ref, *refs):
    pieces_in = refs[:6]
    full, gains_ref, g_ref, n_ref, qkv_ref = refs[6:]

    @pl.when(pl.program_id(0) == 0)
    def _():
        place_pieces(where_ref, full, *pieces_in)
        small = full[:, 4 * INNER : 4 * INNER + LANES].astype(f32).T
        gains_ref[...] = small[0:8]
        table = small[16:32].astype(bf16)
        bias = jnp.where(valid_ref[...] > 0, dot_nn(table, onehot_ref[...]), masked_score)
        for pair in range(PAIRS):
            g_ref[pair] = bias[2 * pair : 2 * pair + 2]

    normed = normed_rows(x_ref[...].astype(f32), gains_ref[0:1, :])
    n_ref[...] = normed
    for part in range(3):
        columns = slice(part * D, (part + 1) * D)
        qkv_ref[:, columns] = dot_nn(normed, full[:, columns]).astype(bf16)


def first_step(where, x, pieces_in, onehot, valid):
    tokens = x.shape[0]
    width = pieces_in[0].shape[1]
    block = pl.BlockSpec((ROWS, D), lambda i, c: (i, 0))
    return pl.pallas_call(
        first_kernel,
        grid_spec=pltpu.PrefetchScalarGridSpec(
            num_scalar_prefetch=1,
            grid=(tokens // ROWS,),
            in_specs=[block, whole_spec(onehot), whole_spec(valid)]
            + [whole_spec(p) for p in pieces_in],
            out_specs=[
                pl.BlockSpec((D, width), lambda i, c: (0, 0)),
                pl.BlockSpec((8, D), lambda i, c: (0, 0)),
                pl.BlockSpec((PAIRS, 2, SPAN), lambda i, c: (0, 0, 0)),
                block,
                pl.BlockSpec((ROWS, 3 * INNER), lambda i, c: (i, 0)),
            ],
        ),
        out_shape=[
            jax.ShapeDtypeStruct((D, width), bf16),
            jax.ShapeDtypeStruct((8, D), f32),
            jax.ShapeDtypeStruct((PAIRS, 2, SPAN), f32),
            jax.ShapeDtypeStruct((tokens, D), bf16),
            jax.ShapeDtypeStruct((tokens, 3 * INNER), bf16),
        ],
        compiler_params=pltpu.CompilerParams(vmem_limit_bytes=VMEM_LIMIT),
        cost_estimate=LIGHT,
    )(where, x, onehot, valid, *pieces_in)


def encoder_kernel(waits, where_ref, *refs):
    refs = refs[waits:]
    x_ref, pieces_in = refs[0], refs[1:7]
    full, kv_ref = refs[7:]

    @pl.when(pl.program_id(0) == 0)
    def _():
        place_pieces(where_ref, full, *pieces_in)

    for part in range(2):
        columns = slice(part * D, (part + 1) * D)
        kv_ref[:, columns] = dot_nn(x_ref[...], full[:, columns]).astype(bf16)


def encoder_step(where, x, pieces_in, after):
    tokens = x.shape[0]
    width = pieces_in[0].shape[1]
    return pl.pallas_call(
        partial(encoder_kernel, len(after)),
        grid_spec=pltpu.PrefetchScalarGridSpec(
            num_scalar_prefetch=1,
            grid=(tokens // ROWS,),
            in_specs=[pl.BlockSpec(memory_space=pl.ANY)] * len(after)
            + [pl.BlockSpec((ROWS, D), lambda i, c: (i, 0))]
            + [whole_spec(p) for p in pieces_in],
            out_specs=[
                pl.BlockSpec((D, width), lambda i, c: (0, 0)),
                pl.BlockSpec((ROWS, 2 * INNER), lambda i, c: (i, 0)),
            ],
        ),
        out_shape=[
            jax.ShapeDtypeStruct((D, width), bf16),
            jax.ShapeDtypeStruct((tokens, 2 * INNER), bf16),
        ],
        compiler_params=pltpu.CompilerParams(vmem_limit_bytes=VMEM_LIMIT),
        cost_estimate=LIGHT,
    )(where, *after, x, *pieces_in)


def middle_kernel(x_ref, attn_ref, out_w_ref, gain_ref, q_w_ref, first_ref, n_ref, cq_ref):
    first = x_ref[...].astype(f32) + dot_nn(attn_ref[...], out_w_ref[...])
    first_ref[...] = first
    normed = normed_rows(first, gain_ref[...])
    n_ref[...] = normed
    cq_ref[...] = dot_nn(normed, q_w_ref[...]).astype(bf16)


def middle_step(x, attn, w_self, gain, w_cross):
    tokens = x.shape[0]
    block = pl.BlockSpec((ROWS, D), lambda i: (i, 0))
    return pl.pallas_call(
        middle_kernel,
        grid=(tokens // ROWS,),
        in_specs=[
            block,
            block,
            pl.BlockSpec((D, D), lambda i: (0, 3)),
            pl.BlockSpec((1, D), lambda i: (0, 0)),
            pl.BlockSpec((D, D), lambda i: (0, 2)),
        ],
        out_specs=[block] * 3,
        out_shape=[
            jax.ShapeDtypeStruct((tokens, D), f32),
            jax.ShapeDtypeStruct((tokens, D), bf16),
            jax.ShapeDtypeStruct((tokens, D), bf16),
        ],
        compiler_params=pltpu.CompilerParams(vmem_limit_bytes=VMEM_LIMIT),
        cost_estimate=LIGHT,
    )(x, attn, w_self, gain, w_cross)


def shares(core, value, keep_ref, send_ref, *at):
    rows, cols = value.shape
    parts = value.astype(bf16).reshape(2, 2, rows // 4, cols)
    columns = slice(0, cols)
    for y in range(2):
        place = (y,) + at + (slice(None), columns)
        keep_ref[place] = jnp.where(core == 0, parts[y, 0], parts[y, 1])
        send_ref[place] = jnp.where(core == 0, parts[y, 1], parts[y, 0])


def feed_forward_kernel(
    where_ref, x1_ref, attn_ref, w2_ref, gain_ref, dout_ref,
    own_g, own_u, core_g, core_u, y_in, x_in, yc_in, xc_in,
    own_o, core_o, y_o, x_o, yc_o, xc_o,
    layer_ref, gx_ref, gx16_ref, gk_ref, gs_ref, ok_ref, os_ref,
    wg, wu, wo, n3, n3t, acc, dn, hid, dgate, dup,
):
    step = pl.program_id(0)
    shard, across = where_ref[0], where_ref[1]
    tokens = x1_ref.shape[0]
    chunks = tokens // ROWS
    rows_in = own_g.shape[0]

    def at(index):
        return pl.ds(pl.multiple_of(index * rows_in, rows_in), rows_in)

    wg[at(shard), :] = own_g[...]
    wu[at(shard), :] = own_u[...]
    wg[at(shard ^ 1), :] = core_g[...]
    wu[at(shard ^ 1), :] = core_u[...]

    @pl.when(across == 0)
    def _():
        wg[at(shard ^ 2), :] = y_in[...]
        wu[at(shard ^ 2), :] = x_in[...]
        wg[at(shard ^ 3), :] = yc_in[...]
        wu[at(shard ^ 3), :] = xc_in[...]

    @pl.when(across == 1)
    def _():
        wg[at(shard ^ 2), :] = x_in[...]
        wu[at(shard ^ 2), :] = y_in[...]
        wg[at(shard ^ 3), :] = xc_in[...]
        wu[at(shard ^ 3), :] = yc_in[...]

    half = D // 2
    for turn, whole in ((0, own_o), (1, core_o)):

        @pl.when(step == turn)
        def _():
            wo[...] = whole[...]

    for turn, near, far in ((2, y_o, x_o), (3, yc_o, xc_o)):
        for bit in range(2):

            @pl.when((step == turn) & (across == bit))
            def _():
                wo[:, bit * half : (bit + 1) * half] = near[...]
                wo[:, (1 - bit) * half : (2 - bit) * half] = far[...]

    @pl.when(step == 0)
    def _():
        gain = gain_ref[...]
        for chunk in range(chunks):
            rows = slice(chunk * ROWS, (chunk + 1) * ROWS)
            x = x1_ref[rows, :] + dot_nn(attn_ref[rows, :], w2_ref[...])
            gx_ref[rows, :] = x
            normed = normed_rows(x, gain)
            n3[rows, :] = normed
            n3t[:, rows] = normed.T
            acc[rows, :] = jnp.zeros((ROWS, D), f32)
            dn[rows, :] = jnp.zeros((ROWS, D), f32)

    c = math.sqrt(2.0 / math.pi)
    for chunk in range(chunks):
        rows = slice(chunk * ROWS, (chunk + 1) * ROWS)
        normed = n3[rows, :]
        gate = dot_nn(normed, wg[...])
        up = dot_nn(normed, wu[...])
        dhidden = dot_nt(dout_ref[rows, :], wo[...]).astype(bf16).astype(f32)
        square = gate * gate
        t = jnp.tanh(c * gate * (1.0 + 0.044715 * square))
        mid = 0.5 * (1.0 + t)
        act = gate * mid
        slope = mid + (0.5 * c) * gate * (1.0 - t * t) * (1.0 + (3.0 * 0.044715) * square)
        hid[rows, :] = (act * up).astype(bf16)
        dgate[rows, :] = (dhidden * up * slope).astype(bf16)
        dup[rows, :] = (dhidden * act).astype(bf16)
        acc[rows, :] += dot_nn(hid[rows, :], wo[...])
        dn[rows, :] += dot_nt(dgate[rows, :], wg[...]) + dot_nt(dup[rows, :], wu[...])
    core = shard % 2
    shares(core, dot_nn(n3t[...], dgate[...]), gk_ref, gs_ref, 0)
    shares(core, dot_nn(n3t[...], dup[...]), gk_ref, gs_ref, 1)
    out_grad = dot_tn(hid[...], dout_ref[...]).astype(bf16)

    @pl.when(step % 2 == 0)
    def _():
        ok_ref[0] = out_grad

    @pl.when(step % 2 == 1)
    def _():
        os_ref[0] = out_grad

    @pl.when(step == pl.num_programs(0) - 1)
    def _():
        gain = gain_ref[...]
        for chunk in range(chunks):
            rows = slice(chunk * ROWS, (chunk + 1) * ROWS)
            x = gx_ref[rows, :]
            layer_ref[rows, :] = (x + acc[rows, :]).astype(bf16)
            factor = lax.rsqrt(jnp.mean(x * x, -1, keepdims=True) + eps)
            d = dn[rows, :]
            weighted = d * gain
            back = factor * weighted - x * (
                factor * factor * factor * jnp.mean(weighted * x, -1, keepdims=True)
            )
            gx = dout_ref[rows, :].astype(f32) + back
            gx_ref[rows, :] = gx
            gx16_ref[rows, :] = gx.astype(bf16)


def feed_forward(where, x1, attn, w_cross, gain, dout, in_pieces, out_pieces):
    tokens = x1.shape[0]
    steps = FF // FF_BLOCK
    one = pl.Buffered(1)
    rows_in = in_pieces[0].shape[0]

    def whole(width=D):
        return pl.BlockSpec((tokens, width), lambda f, c: (0, 0), pipeline_mode=one)

    def streamed(at):
        return pl.BlockSpec((rows_in, FF_BLOCK), lambda f, c: (0, at + (c[0] ^ f)))

    resident = pl.BlockSpec((tokens, D), lambda f, c: (0, 0))
    in_share = pl.BlockSpec((2, 2, D // 4, FF_BLOCK), lambda f, c: (0, 0, 0, c[0] ^ f))
    out_share = pl.BlockSpec((1, FF_BLOCK, D), lambda f, c: ((c[0] ^ f) // 2, 0, 0))
    in_type = jax.ShapeDtypeStruct((2, 2, D // 4, FF), bf16)
    out_type = jax.ShapeDtypeStruct((2, FF_BLOCK, D), bf16)
    own_i, core_i, *halves_i = in_pieces
    return pl.pallas_call(
        feed_forward_kernel,
        grid_spec=pltpu.PrefetchScalarGridSpec(
            num_scalar_prefetch=1,
            grid=(steps,),
            in_specs=[
                whole(),
                whole(),
                pl.BlockSpec((D, D), lambda f, c: (0, 3), pipeline_mode=one),
                pl.BlockSpec((1, D), lambda f, c: (0, 0)),
                whole(),
                streamed(0), streamed(steps), streamed(0), streamed(steps),
                streamed(0), streamed(0), streamed(0), streamed(0),
            ]
            + [whole_spec(p) for p in out_pieces],
            out_specs=[resident, resident, resident, in_share, in_share, out_share, out_share],
            scratch_shapes=[
                pltpu.VMEM((D, FF_BLOCK), bf16),
                pltpu.VMEM((D, FF_BLOCK), bf16),
                pltpu.VMEM((FF_BLOCK, D), bf16),
                pltpu.VMEM((tokens, D), bf16),
                pltpu.VMEM((D, tokens), bf16),
                pltpu.VMEM((tokens, D), f32),
                pltpu.VMEM((tokens, D), f32),
                pltpu.VMEM((tokens, FF_BLOCK), bf16),
                pltpu.VMEM((tokens, FF_BLOCK), bf16),
                pltpu.VMEM((tokens, FF_BLOCK), bf16),
            ],
        ),
        out_shape=[
            jax.ShapeDtypeStruct((tokens, D), bf16),
            jax.ShapeDtypeStruct((tokens, D), f32),
            jax.ShapeDtypeStruct((tokens, D), bf16),
            in_type, in_type, out_type, out_type,
        ],
        compiler_params=pltpu.CompilerParams(vmem_limit_bytes=VMEM_LIMIT),
        cost_estimate=LIGHT,
    )(where, x1, attn, w_cross, gain, dout, own_i, own_i, core_i, core_i, *halves_i, *out_pieces)


def weight_grad_kernel(counts, firsts, waits, core_ref, *refs):
    refs = refs[waits:]
    terms = len(counts)
    lefts, rights = refs[0:terms], refs[terms : 2 * terms]
    refs = refs[2 * terms :]
    second = firsts is not None
    if second:
        tiny_ref, keep_ref, send_ref, keep2_ref, send2_ref, left_t = refs
    else:
        keep_ref, send_ref, left_t = refs
    step = pl.program_id(0)
    core = core_ref[0] % 2
    at = 0
    for left, right, count in zip(lefts, rights, counts):

        @pl.when(step == at)
        def _():
            left_t[...] = left[...].T

        @pl.when((step >= at) & (step < at + count))
        def _():
            block = right[...] if len(right.shape) == 2 else right[0]
            value = dot_nn(left_t[...], block)
            if not second:
                shares(core, value, keep_ref, send_ref)
            else:

                @pl.when(step < firsts)
                def _():
                    shares(core, value, keep_ref, send_ref)

                @pl.when(step >= firsts)
                def _():
                    shares(core, value, keep2_ref, send2_ref)
                    tiny = tiny_ref[...]
                    for y in range(2):
                        keep2_ref[y, :, D:] = jnp.where(core == 0, tiny[y, 0], tiny[y, 1])
                        send2_ref[y, :, D:] = jnp.where(core == 0, tiny[y, 1], tiny[y, 0])

        at += count


def weight_grad(where, terms, tiny=None, after=()):
    tokens = terms[0][0].shape[0]
    counts = []
    rights = []
    at = 0
    for _, right in terms:
        deep = right.ndim == 3
        count = right.shape[0] if deep else 1

        def place(j, c, at=at, count=count, deep=deep):
            return (jnp.clip(j - at, 0, count - 1), 0, 0) if deep else (0, 0)

        rights.append(pl.BlockSpec((1, tokens, D) if deep else (tokens, D), place))
        counts.append(count)
        at += count
    firsts = None if tiny is None else at - 1
    blocks = at if tiny is None else at - 1
    share = pl.BlockSpec((2, D // 4, D), lambda j, c: (0, 0, jnp.minimum(j, blocks - 1)))
    out_specs = [share, share]
    out_shape = [jax.ShapeDtypeStruct((2, D // 4, blocks * D), bf16)] * 2
    extra_specs, extra = [], []
    if tiny is not None:
        extra_specs, extra = [pl.BlockSpec(tiny.shape, lambda j, c: (0, 0, 0, 0))], [tiny]
        wide = D + tiny.shape[-1]
        out_specs += [pl.BlockSpec((2, D // 4, wide), lambda j, c: (0, 0, 0))] * 2
        out_shape += [jax.ShapeDtypeStruct((2, D // 4, wide), bf16)] * 2
    return pl.pallas_call(
        partial(weight_grad_kernel, counts, firsts, len(after)),
        grid_spec=pltpu.PrefetchScalarGridSpec(
            num_scalar_prefetch=1,
            grid=(at,),
            in_specs=[pl.BlockSpec(memory_space=pl.ANY)] * len(after)
            + [pl.BlockSpec((tokens, D), lambda j, c: (0, 0))] * len(terms)
            + rights
            + extra_specs,
            out_specs=out_specs,
            scratch_shapes=[pltpu.VMEM((D, tokens), bf16)],
        ),
        out_shape=out_shape,
        compiler_params=pltpu.CompilerParams(vmem_limit_bytes=VMEM_LIMIT),
        cost_estimate=LIGHT,
    )(where, *after, *[left for left, _ in terms], *[right for _, right in terms], *extra)


def norm_back_kernel(normed, onward, waits, *refs):
    refs = refs[waits:]
    grad_ref, w_ref = refs[:2]
    total = None
    for part in range(grad_ref.shape[0]):
        term = dot_nt(grad_ref[part], w_ref[:, part * D : (part + 1) * D])
        total = term if total is None else total + term
    if not normed:
        refs[2][...] = total.astype(refs[2].dtype)
        return
    x_ref, gain_ref, up_ref = refs[2:5]
    refs = refs[5:]
    if onward:
        next_ref, out_ref, gain_grad_ref, out16_ref, onward_ref = refs
    else:
        out_ref, gain_grad_ref = refs
    x = x_ref[...].astype(f32)
    factor = lax.rsqrt(jnp.mean(x * x, -1, keepdims=True) + eps)
    weighted = total * gain_ref[...]
    grad_gain = jnp.sum(total * x * factor, axis=0, keepdims=True)

    @pl.when(pl.program_id(0) == 0)
    def _():
        gain_grad_ref[...] = jnp.zeros_like(gain_grad_ref)

    gain_grad_ref[...] += grad_gain
    scale = factor * factor * factor * jnp.mean(weighted * x, -1, keepdims=True)
    out = up_ref[...] + factor * weighted - x * scale
    out_ref[...] = out
    if onward:
        out16 = out.astype(bf16)
        out16_ref[...] = out16
        onward_ref[...] = dot_nt(out16, next_ref[...]).astype(bf16)


def norm_back(
    grads, w, w_at, x=None, gain=None, upstream=None, w_next=None, next_at=0, after=(), kind=f32
):
    if grads.ndim == 2:
        grads = grads[None]
    parts, tokens, _ = grads.shape
    block = pl.BlockSpec((ROWS, D), lambda i: (i, 0))
    row = pl.BlockSpec((1, D), lambda i: (0, 0))
    in_specs = [pl.BlockSpec(memory_space=pl.ANY)] * len(after)
    in_specs += [
        pl.BlockSpec((parts, ROWS, D), lambda i: (0, i, 0)),
        pl.BlockSpec((D, parts * D), lambda i: (0, w_at)),
    ]
    args = [*after, grads, w]
    wide = jax.ShapeDtypeStruct((tokens, D), kind)
    half = jax.ShapeDtypeStruct((tokens, D), bf16)
    out_specs, out_shape = [block], [wide]
    if x is not None:
        in_specs += [block, row, block]
        args += [x, gain, upstream]
        out_specs.append(row)
        out_shape.append(jax.ShapeDtypeStruct((1, D), f32))
        if w_next is not None:
            in_specs.append(pl.BlockSpec((D, D), lambda i: (0, next_at)))
            args.append(w_next)
            out_specs += [block, block]
            out_shape += [half, half]
    return pl.pallas_call(
        partial(norm_back_kernel, x is not None, w_next is not None, len(after)),
        grid=(tokens // ROWS,),
        in_specs=in_specs,
        out_specs=out_specs,
        out_shape=out_shape,
        compiler_params=pltpu.CompilerParams(vmem_limit_bytes=VMEM_LIMIT),
        cost_estimate=LIGHT,
    )(*args)


def exchange(array, axis, size, bit):
    return lax.ppermute(array, axis, [(i, i ^ bit) for i in range(size)])


def part_of(array, dim, index):
    half = array.shape[dim] // 2
    return lax.dynamic_slice_in_dim(array, index * half, half, dim)


def tie(value, *others):
    return lax.optimization_barrier((value, *others))[0]


def meet(done, *moves):
    *gots, done = lax.optimization_barrier((*[m.got for m in moves], done))
    for move, got in zip(moves, gots):
        move.got = got
    return done


class Gather:
    def __init__(self, own, sizes, *after):
        self.sizes = sizes
        self.own = own
        half = part_of(own, 1, lax.axis_index("rep") % 2)
        if after:
            half = tie(half, *after)
        self.half = half
        self.got = exchange(half, "shard", sizes[0], 2)

    def cross(self):
        self.y = self.got
        self.got = exchange(self.y, "rep", self.sizes[1], 1)
        self.core = exchange(tie(self.own, self.y), "shard", self.sizes[0], 1)
        self.yc = exchange(self.y, "shard", self.sizes[0], 1)

    def pieces(self):
        self.x = self.got
        xc = exchange(self.x, "shard", self.sizes[0], 1)
        return self.own, self.core, self.y, self.x, self.yc, xc


class Chain:
    def __init__(self, keep, send, sizes, dims, order):
        self.shards, self.reps = sizes
        self.bits = [1 << b for b in range(self.reps.bit_length() - 1)]
        self.dims = [dims[min(i, len(dims) - 1)] for i in range(len(self.bits))]
        steps = []
        for name in order:
            if name == "y":
                steps.append(("shard", 2, 0))
            else:
                steps += [("rep", bit, dim) for bit, dim in zip(self.bits, self.dims)]
        self.steps = steps
        self.kept = [keep]
        self.got = exchange(send, "shard", self.shards, 1)
        self.sent = send
        self.at = 0

    def own(self):
        while self.at < len(self.steps):
            self.advance()
        total = self.got.astype(f32)
        for part in self.kept:
            total = total + part.astype(f32)
        return total.astype(bf16)

    def advance(self):
        axis, bit, dim = self.steps[self.at]
        self.at += 1
        mine = (lax.axis_index(axis) // bit) % 2
        size = self.shards if axis == "shard" else self.reps
        parts = self.kept + [self.got]
        total = None
        for part in parts:
            term = part_of(part, dim, 1 - mine).astype(f32)
            total = term if total is None else total + term
        self.sent = total.astype(bf16)
        self.kept = [part_of(part, dim, mine) for part in parts]
        self.got = exchange(self.sent, axis, size, bit)
        return self.got


class Spread:
    def __init__(self, own, sizes, bits, dims):
        self.own = own
        self.reps = sizes[1]
        self.left = list(zip(bits, dims))
        self.got = None
        self.advance()

    def pair(self):
        bit, _ = self.now
        mine = (lax.axis_index("rep") // bit) % 2
        low = jnp.where(mine == 0, self.own, self.got)
        high = jnp.where(mine == 0, self.got, self.own)
        return low, high

    def advance(self):
        if self.got is not None:
            self.own = jnp.concatenate(self.pair(), axis=self.now[1])
        self.now = self.left.pop()
        self.got = exchange(self.own, "rep", self.reps, self.now[0])


def together(*moves):
    gots = lax.optimization_barrier(tuple(m.got for m in moves))
    for move, got in zip(moves, gots):
        move.got = got


def unpack_kernel(where_ref, own_ref, got_ref, w_ref, in_ref, out_ref, sum_ref):
    mine = where_ref[1]
    half, _, rows, cols = own_ref.shape
    out_rows = out_ref.shape[0] // (2 * half)
    total = jnp.zeros((rows, LANES), f32)
    for blocks_ref, first in ((own_ref, mine * half), (got_ref, (1 - mine) * half)):
        for block in range(half):
            at = first + block
            for part in range(2):
                place = pl.ds(pl.multiple_of(part * FF + at * cols, cols), cols)
                value = blocks_ref[block, part].astype(f32)
                in_ref[:, place] = value
                product = value * w_ref[:, place].astype(f32)
                for lane in range(0, cols, LANES):
                    total = total + product[:, lane : lane + LANES]
            place = pl.ds(pl.multiple_of(at * out_rows, out_rows), out_rows)
            for group in range(D // cols):
                out_ref[place, group * cols : (group + 1) * cols] = blocks_ref[
                    block, 2, group * out_rows : (group + 1) * out_rows, :
                ].astype(f32)
    row = jnp.broadcast_to(jnp.sum(total, axis=1, keepdims=True), (rows, LANES)).T
    sum_ref[...] = row[0:8]


def unpack(where, own, got, w):
    rows = own.shape[2]

    def whole(shape):
        return pl.BlockSpec(shape, lambda i, c: (0,) * len(shape))

    outs = [
        jax.ShapeDtypeStruct((rows, 2 * FF), f32),
        jax.ShapeDtypeStruct((FF * rows // D, D), f32),
        jax.ShapeDtypeStruct((8, rows), f32),
    ]
    return pl.pallas_call(
        unpack_kernel,
        grid_spec=pltpu.PrefetchScalarGridSpec(
            num_scalar_prefetch=1,
            grid=(1,),
            in_specs=[whole(own.shape), whole(got.shape), whole(w.shape)],
            out_specs=[whole(o.shape) for o in outs],
        ),
        out_shape=outs,
        compiler_params=pltpu.CompilerParams(vmem_limit_bytes=VMEM_LIMIT),
        cost_estimate=LIGHT,
    )(where, own, got, w)


def bias_rows(shards):
    lane = np.arange(SPAN)
    distance = np.where(lane < SEQ, SEQ - LANES - lane, 2 * SEQ - lane)
    bucket = np.zeros(SPAN, np.int64)
    for edge in bucket_edges:
        bucket += distance >= edge
    valid = (distance >= 0) & (distance < SEQ)
    onehot = np.zeros((SPAN, NUM_BUCKETS), np.float32)
    onehot[np.arange(SPAN)[valid], bucket[valid]] = 1.0
    own = NUM_BUCKETS // shards
    rows = np.arange(NUM_BUCKETS) // own * (D // shards) + np.arange(NUM_BUCKETS) % own
    placed = np.zeros((D, SPAN), np.float32)
    placed[rows] = onehot.T
    return onehot, placed, valid[None].astype(np.float32)


def local(
    sizes,
    hidden_in,
    enc_states,
    dec_segments,
    enc_segments,
    out_grad,
    gains,
    rel_table,
    self_qkv,
    self_out,
    cross_q,
    cross_kv,
    cross_out,
    ff_in,
    ff_out,
):
    shards, reps = sizes
    own_rows = D // shards
    own_buckets = NUM_BUCKETS // shards
    width = reps.bit_length() - 1
    shard = lax.axis_index("shard")
    where = jnp.stack([shard, lax.axis_index("rep") % 2]).astype(jnp.int32)
    small = jnp.concatenate(
        [
            gains.T,
            jnp.zeros((own_rows, 13), bf16),
            jnp.pad(rel_table, ((0, own_rows - own_buckets), (0, 2 * LANES - 16 - HEADS))),
        ],
        axis=1,
    )
    self_set = Gather(jnp.concatenate([self_qkv, self_out, small], axis=1), sizes)
    self_set.cross()
    cross_set = Gather(
        jnp.concatenate([cross_kv, cross_q, cross_out], axis=1), sizes, self_set.y
    )
    self_pieces = self_set.pieces()

    lane = jnp.arange(LANES, dtype=jnp.int32)[None, :]
    dec_ids = dec_segments[:, None]
    enc_ids = enc_segments[:, None]
    ones = ((lane % HEAD_DIM >= 2) & (lane % HEAD_DIM <= 4)).astype(f32)

    def key_extra(ids):
        return jnp.where(lane < 2, jnp.where(lane != ids, masked_score, 0.0), ones).astype(bf16)

    q_extra = ((lane < 2) & (lane == dec_ids)).astype(bf16)
    self_extra = key_extra(dec_ids)
    cross_extra = key_extra(enc_ids)
    onehot, placed, valid = bias_rows(shards)
    w_self, gains_all, g, normed_one, qkv = first_step(
        where, hidden_in, self_pieces, placed.astype(bf16), valid
    )
    meet(normed_one, cross_set)
    cross_set.cross()
    out_set = Gather(ff_out, sizes, cross_set.y)
    in_set = Gather(ff_in, sizes, cross_set.y)
    attn_one, lows_one = attend_forward(
        qkv, 0, qkv, PAIRS, qkv, 2 * PAIRS, q_extra, self_extra, g, SELF_RANGES,
        after=[out_set.half, in_set.half],
    )
    meet(attn_one, cross_set, out_set, in_set)
    cross_pieces = cross_set.pieces()
    out_set.cross()
    in_set.cross()
    w_cross, ckv = encoder_step(where, enc_states, cross_pieces, [attn_one])
    first, normed_two, cq = middle_step(hidden_in, attn_one, w_self, gains_all[1:2], w_cross)
    attn_two, lows_two = attend_forward(
        cq, 0, ckv, 0, ckv, PAIRS, q_extra, cross_extra, None, CROSS_RANGES
    )
    meet(attn_two, out_set, in_set)
    ff_out_pieces = out_set.pieces()
    ff_in_pieces = in_set.pieces()
    layer_out, grad_second, out_two, in_keep, in_send, out_keep, out_send = feed_forward(
        where, first, attn_two, w_cross, gains_all[2:3], out_grad, ff_in_pieces, ff_out_pieces
    )
    ff_in_chain = Chain(in_keep, in_send, sizes, [3], "yr")
    ff_out_chain = Chain(out_keep, out_send, sizes, [1], "ry")
    (grad_attn_two,) = norm_back(out_two, w_cross, 3, kind=bf16, after=[layer_out])
    meet(grad_attn_two, ff_in_chain, ff_out_chain)
    ff_out_chain.advance()
    ff_in_chain.advance()
    grad_cq, grad_ckv = attend_backward(
        cq, 0, ckv, 0, ckv, PAIRS, q_extra, cross_extra, lows_two, attn_two, grad_attn_two,
        None, CROSS_RANGES, after=[ff_in_chain.sent, ff_out_chain.sent],
    )
    meet(grad_cq, ff_out_chain)
    ff_out_chain.advance()
    grad_first, _, out_one, grad_attn_one = norm_back(
        grad_cq, w_cross, 2, first, gains_all[1:2], grad_second, w_self, 3,
        after=[ff_out_chain.sent],
    )
    meet(grad_attn_one, ff_in_chain, ff_out_chain)
    ff_in_chain.advance()
    ff_out_chain.advance()
    cross_keep, cross_send = weight_grad(
        where,
        [(enc_states, grad_ckv), (normed_two, grad_cq), (attn_two, out_two), (attn_one, out_one)],
        after=[ff_in_chain.sent, ff_out_chain.sent],
    )
    cross_send = meet(cross_send, ff_in_chain, ff_out_chain)
    ff_in_chain.advance()
    ff_out_chain.advance()
    cross_chain = Chain(cross_keep, cross_send, sizes, [2, 1], "yr")
    (enc_grad,) = norm_back(
        grad_ckv, w_cross, 0, after=[cross_keep, ff_in_chain.sent, ff_out_chain.sent]
    )
    meet(enc_grad, cross_chain, ff_in_chain, ff_out_chain)
    cross_chain.advance()
    ff_in_chain.advance()
    out_own = ff_out_chain.own()[0]
    backward = partial(
        attend_backward, qkv, 0, qkv, PAIRS, qkv, 2 * PAIRS, q_extra, self_extra, lows_one,
        attn_one, grad_attn_one, g, SELF_RANGES, pairs=PAIRS // 2,
    )
    some_qkv, some_rel = backward(after=[cross_chain.sent, ff_in_chain.sent, out_own])
    some_qkv = meet(some_qkv, ff_in_chain)
    in_own = ff_in_chain.own()[0]
    rows, columns = in_own.shape[1:]
    out_rows = out_own.shape[0]
    out_own = out_own.reshape(out_rows, -1, columns).transpose(1, 0, 2).reshape(1, rows, columns)
    bits = ff_in_chain.bits
    blocks = Spread(
        jnp.concatenate([in_own, out_own], axis=0)[None], sizes, bits, [0] * len(bits)
    )
    grad_qkv, more_rel = backward(after=[blocks.own], first=PAIRS // 2, into=some_qkv)
    rel_part = jnp.concatenate([some_rel, more_rel], axis=0)
    grad_qkv = meet(grad_qkv, cross_chain, blocks)
    cross_chain.advance()
    blocks.advance()
    table_part = jnp.einsum(
        "hu,ub->bh",
        rel_part.reshape(HEADS, SPAN),
        onehot,
        precision=lax.Precision.HIGHEST,
        preferred_element_type=f32,
    )
    tiny = table_part.reshape(2, 2, own_buckets, HEADS).astype(bf16)
    tiny = jnp.pad(tiny, ((0, 0), (0, 0), (0, own_rows - own_buckets), (0, 2 * LANES - HEADS)))
    self_keep, self_send, last_keep, last_send = weight_grad(
        where, [(normed_one, grad_qkv)], tiny=tiny, after=[blocks.own, cross_chain.sent]
    )
    self_send = meet(self_send, blocks, cross_chain)
    blocks.advance()
    cross_chain.advance()
    self_chain = Chain(self_keep, self_send, sizes, [2, 1], "yr")
    last_chain = Chain(last_keep, last_send, sizes, [2, 1], "ry")
    self_chain.advance()
    last_chain.advance()
    in_grad, _ = norm_back(
        grad_qkv, w_self, 0, hidden_in, gains_all[0:1], grad_first,
        after=[self_chain.sent, last_chain.sent, cross_chain.sent, blocks.own],
    )
    meet(in_grad, self_chain, last_chain, cross_chain)
    self_chain.advance()
    last_chain.advance()
    cross_chain.advance()
    cross_spread = None
    while last_chain.at < len(last_chain.steps):
        if last_chain.at == 3:
            together(self_chain, last_chain, cross_spread or cross_chain, blocks)
        else:
            together(self_chain, last_chain, cross_spread or cross_chain)
        if cross_spread is not None:
            if cross_spread.left:
                cross_spread.advance()
        elif cross_chain.at < len(cross_chain.steps):
            cross_chain.advance()
        else:
            cross_spread = Spread(cross_chain.own(), sizes, cross_chain.bits, cross_chain.dims)
        self_chain.advance()
        last_chain.advance()
    together(self_chain, last_chain, cross_spread)
    if cross_spread.left:
        cross_spread.advance()
    self_width = self_chain.got.shape[2]
    self_spread = Spread(
        jnp.concatenate([self_chain.own(), last_chain.own()], axis=2),
        sizes, self_chain.bits, self_chain.dims,
    )
    while self_spread.left:
        if cross_spread.left:
            together(self_spread, cross_spread)
            cross_spread.advance()
        self_spread.advance()
    low, high = self_spread.pair()
    low, high = low[0], high[0]
    self_grad = jnp.concatenate(
        [low[:, :self_width], high[:, :self_width], low[:, self_width:], high[:, self_width:]],
        axis=1,
    ).astype(f32)
    cross_grad = jnp.concatenate(cross_spread.pair(), axis=2)[0].astype(f32)

    if reps == 8:
        ff_in_grad, ff_out_grad, in_sums = unpack(where, blocks.own, blocks.got, ff_in)
        in_sums = in_sums[0]
    else:
        while blocks.left:
            blocks.advance()
        spread = jnp.concatenate(blocks.pair(), axis=0)
        in_grads = spread[:, :2].transpose(2, 1, 0, 3)
        ff_in_grad = in_grads.reshape(own_rows, 2 * FF).astype(f32)
        out_grads = spread[:, 2].reshape(reps, -1, out_rows, columns).transpose(0, 2, 1, 3)
        ff_out_grad = out_grads.reshape(ff_out.shape).astype(f32)
        in_sums = jnp.sum(ff_in.astype(f32) * ff_in_grad, axis=1)

    self_qkv_grad = self_grad[:, : 3 * INNER]
    cross_query_gradient = cross_grad[:, 2 * INNER : 3 * INNER]

    sums = jnp.stack(
        [
            jnp.sum(self_qkv.astype(f32) * self_qkv_grad, axis=1),
            jnp.sum(cross_q.astype(f32) * cross_query_gradient, axis=1),
            in_sums,
        ]
    )
    gains_grad = sums / gains.astype(f32)
    rel_table_grad = self_grad[:own_buckets, 3 * INNER : 3 * INNER + HEADS]
    return (
        layer_out,
        in_grad,
        enc_grad,
        gains_grad,
        rel_table_grad,
        self_qkv_grad,
        cross_grad[:, 3 * INNER + D :],
        cross_query_gradient,
        cross_grad[:, : 2 * INNER],
        cross_grad[:, 3 * INNER : 3 * INNER + D],
        ff_in_grad,
        ff_out_grad,
    )


def solution(mesh):
    tokens = P(("rep", "shard"), None)
    ids = P(("rep", "shard"))
    rows = P("shard", None)
    columns = P(None, "shard")
    in_specs = (tokens, tokens, ids, ids, tokens, columns) + (rows,) * 8
    out_specs = (tokens, tokens, tokens, columns) + (rows,) * 8
    sizes = (mesh.shape["shard"], mesh.shape["rep"])
    return jax.shard_map(
        partial(local, sizes), mesh=mesh, in_specs=in_specs, out_specs=out_specs, check_vma=False
    )
```

```python
from functools import partial
import math

import jax
import jax.numpy as jnp
import numpy as np
from jax import lax
from jax.experimental import pallas as pl
from jax.experimental.pallas import tpu as pltpu
from jax.sharding import PartitionSpec as P

HEADS = 12
HEAD_DIM = 64
FF = 2048
NUM_BUCKETS = 32
SEQ = 512
D = 768
INNER = HEADS * HEAD_DIM
PAIRS = HEADS // 2
LANES = 128
SPAN = SEQ + LANES
FF_BLOCK = 512
ROWS = 256

eps = 1e-06
masked_score = -1e30
bf16 = jnp.bfloat16
f32 = jnp.float32
VMEM_LIMIT = 56 * 1024 * 1024
LIGHT = pl.CostEstimate(flops=1000000, bytes_accessed=100000, transcendentals=0)

bucket_edges = np.array(
    list(range(1, 16)) + [int(math.ceil(16.0 * 8.0 ** ((b - 16) / 16.0))) for b in range(16, 32)],
    dtype=np.int32,
)

SELF_RANGES = ((0, 128), (0, 256), (0, 384), (128, 512))
CROSS_RANGES = ((0, 384), (0, 512), (0, 512), (128, 512))


def dot_nn(a, b):
    return lax.dot_general(a, b, (((1,), (0,)), ((), ())), preferred_element_type=f32)


def dot_nt(a, b):
    return lax.dot_general(a, b, (((1,), (1,)), ((), ())), preferred_element_type=f32)


def dot_tn(a, b):
    return lax.dot_general(a, b, (((0,), (0,)), ((), ())), preferred_element_type=f32)


def half_masks():
    lane = lax.broadcasted_iota(jnp.int32, (1, LANES), 1)
    low = (lane < HEAD_DIM).astype(f32)
    return low.astype(bf16), (1.0 - low).astype(bf16)


def pieces(value):
    lane = lax.broadcasted_iota(jnp.int32, value.shape, 1) % HEAD_DIM
    high = value.astype(bf16).astype(f32)
    rest = value - high
    middle = rest.astype(bf16).astype(f32)
    last = rest - middle
    return jnp.where(
        lane == 2, high, jnp.where(lane == 3, middle, jnp.where(lane == 4, last, 0.0))
    )


def stacked(block, low, high):
    return jnp.concatenate([block * low, block * high], axis=0)


def toeplitz(row):
    wide = jnp.broadcast_to(row, (LANES, SPAN))
    return pltpu.roll(wide, 0, 1, stride=1, stride_axis=0)[:, :SEQ]


def attend_forward_kernel(ranges, biased, waits, *refs):
    refs = refs[waits:]
    if biased:
        q_ref, k_ref, v_ref, qa_ref, ka_ref, g_ref, o_ref, l_ref, slab = refs

        @pl.when(pl.program_id(1) == 0)
        def _():
            slab[0:LANES] = toeplitz(g_ref[0, 0:1, :])
            slab[LANES : 2 * LANES] = toeplitz(g_ref[0, 1:2, :])
    else:
        q_ref, k_ref, v_ref, qa_ref, ka_ref, o_ref, l_ref = refs
    low, high = half_masks()
    keys = jnp.concatenate([k_ref[...], ka_ref[...]], axis=1)
    values = jnp.concatenate([v_ref[...], jnp.ones((SEQ, LANES), bf16)], axis=1)
    lane = lax.broadcasted_iota(jnp.int32, (LANES, LANES), 1)
    for block, (start, stop) in enumerate(ranges):
        rows = slice(block * LANES, (block + 1) * LANES)
        extra = qa_ref[rows, :]
        left = jnp.concatenate(
            [stacked(q_ref[rows, :], low, high), jnp.concatenate([extra, extra], axis=0)], axis=1
        )
        scores = dot_nt(left, keys[start:stop])
        if biased:
            scores = scores + slab[:, SEQ - (stop - start) :]
        top = jnp.max(scores, axis=1, keepdims=True)
        expd = jnp.exp(scores - top)
        mixed = dot_nn(expd.astype(bf16), values[start:stop])
        total = mixed[:, LANES:]
        mixed = mixed[:, :LANES] / total
        o_ref[rows, :] = jnp.where(lane < HEAD_DIM, mixed[:LANES], mixed[LANES:]).astype(bf16)
        negative = pieces(-(top + jnp.log(total)))
        l_ref[rows, :] = jnp.where(lane < HEAD_DIM, negative[:LANES], negative[LANES:]).astype(bf16)


def attend_forward(q, q_at, k, k_at, v, v_at, q_extra, k_extra, g, ranges, after=()):
    tokens = q.shape[0]
    sequences = tokens // SEQ
    biased = g is not None

    def block(at):
        return pl.BlockSpec((SEQ, LANES), lambda p, s: (s, at + p))

    shared = pl.BlockSpec((SEQ, LANES), lambda p, s: (s, 0))
    in_specs = [block(q_at), block(k_at), block(v_at), shared, shared]
    args = [q, k, v, q_extra, k_extra]
    scratch = []
    if biased:
        in_specs.append(pl.BlockSpec((1, 2, SPAN), lambda p, s: (p, 0, 0)))
        args.append(g)
        scratch.append(pltpu.VMEM((2 * LANES, SEQ), f32))
    seen = sum(stop - start for start, stop in ranges)
    return pl.pallas_call(
        partial(attend_forward_kernel, ranges, biased, len(after)),
        grid=(PAIRS, sequences),
        in_specs=[pl.BlockSpec(memory_space=pl.ANY)] * len(after) + in_specs,
        out_specs=[block(0), block(0)],
        out_shape=[jax.ShapeDtypeStruct((tokens, INNER), bf16)] * 2,
        scratch_shapes=scratch,
        compiler_params=pltpu.CompilerParams(vmem_limit_bytes=VMEM_LIMIT),
        cost_estimate=LIGHT,
    )(*after, *args)


def attend_backward_kernel(ranges, biased, waits, *refs):
    refs = refs[waits:]
    if biased:
        (q_ref, k_ref, v_ref, qa_ref, ka_ref, l_ref, o_ref, d_ref, g_ref) = refs[:9]
        out_ref, rel_ref, dk, dv, slab, dslab = refs[9:]

        @pl.when(pl.program_id(1) == 0)
        def _():
            slab[:, 0:LANES] = toeplitz(g_ref[0, 0:1, :]).T
            slab[:, LANES : 2 * LANES] = toeplitz(g_ref[0, 1:2, :]).T
            dslab[...] = jnp.zeros_like(dslab)
    else:
        (q_ref, k_ref, v_ref, qa_ref, ka_ref, l_ref, o_ref, d_ref) = refs[:8]
        dq_ref, out_ref, dk, dv = refs[8:]
    low, high = half_masks()
    low_lane = lax.broadcasted_iota(jnp.int32, (LANES, LANES), 1) < HEAD_DIM
    low_row = lax.broadcasted_iota(jnp.int32, (LANES, LANES), 0) < HEAD_DIM
    keys = jnp.concatenate([k_ref[...], ka_ref[...]], axis=1)
    values = jnp.concatenate([v_ref[...], ka_ref[...]], axis=1)
    keys_t = k_ref[...].T
    dk[...] = jnp.zeros_like(dk)
    dv[...] = jnp.zeros_like(dv)
    for block, (start, stop) in enumerate(ranges):
        rows = slice(block * LANES, (block + 1) * LANES)
        seen = slice(start, stop)
        q2 = stacked(q_ref[rows, :], low, high)
        extra = qa_ref[rows, :]
        totals = l_ref[rows, :]
        q_right = jnp.concatenate(
            [q2, jnp.concatenate([extra + totals * low, extra + totals * high], axis=0)], axis=1
        )
        scores = dot_nt(keys[seen], q_right)
        if biased:
            scores = scores + slab[SEQ - (stop - start) :, :]
        probs = jnp.exp(scores)
        grad = d_ref[rows, :]
        d2 = stacked(grad, low, high)
        product = grad.astype(f32) * o_ref[rows, :].astype(f32)
        sum_low = jnp.sum(jnp.where(low_lane, product, 0.0), axis=1, keepdims=True)
        sum_high = jnp.sum(jnp.where(low_lane, 0.0, product), axis=1, keepdims=True)
        delta = pieces(
            -jnp.concatenate(
                [
                    jnp.broadcast_to(sum_low, (LANES, LANES)),
                    jnp.broadcast_to(sum_high, (LANES, LANES)),
                ],
                axis=0,
            )
        ).astype(bf16)
        lows = jnp.concatenate([delta[:LANES] * low, delta[LANES:] * high], axis=0)
        d_right = jnp.concatenate([d2, lows], axis=1)
        grad_scores = probs * dot_nt(values[seen], d_right)
        probs16 = probs.astype(bf16)
        scores16 = grad_scores.astype(bf16)
        dv[seen, :] += dot_nn(probs16, d2)
        dk[seen, :] += dot_nn(scores16, q2)
        dq = dot_nn(keys_t[:, seen], scores16)
        dq = jnp.where(low_row, dq[:, :LANES], dq[:, LANES:]).T.astype(bf16)
        if biased:
            out_ref[0, rows, :] = dq
            dslab[SEQ - (stop - start) :, :] += grad_scores
        else:
            dq_ref[rows, :] = dq
    first = 1 if biased else 0
    out_ref[first] = dk[...].astype(bf16)
    out_ref[first + 1] = dv[...].astype(bf16)
    if biased:

        @pl.when(pl.program_id(1) == pl.num_programs(1) - 1)
        def _():
            for head in range(2):
                square = dslab[:, head * LANES : (head + 1) * LANES].T
                wide = jnp.concatenate([square, jnp.zeros((LANES, LANES), f32)], axis=1)
                half = LANES // 2
                while half >= 1:
                    wide = wide[:half] + pltpu.roll(wide[half:], SPAN - half, 1)
                    half //= 2
                rel_ref[0, head : head + 1, :] = wide


def attend_backward(q, q_at, k, k_at, v, v_at, q_extra, k_extra, lows, mixed, grad, g, ranges, after=(),
                    first=0, pairs=PAIRS, into=None):
    tokens = q.shape[0]
    sequences = tokens // SEQ
    biased = g is not None

    def block(at):
        return pl.BlockSpec((SEQ, LANES), lambda p, s: (s, at + first + p))

    shared = pl.BlockSpec((SEQ, LANES), lambda p, s: (s, 0))
    in_specs = [block(q_at), block(k_at), block(v_at), shared, shared, block(0), block(0), block(0)]
    args = [q, k, v, q_extra, k_extra, lows, mixed, grad]
    scratch = [pltpu.VMEM((SEQ, LANES), f32), pltpu.VMEM((SEQ, LANES), f32)]
    if biased:
        in_specs.append(pl.BlockSpec((1, 2, SPAN), lambda p, s: (first + p, 0, 0)))
        args.append(g)
        scratch += [pltpu.VMEM((SEQ, 2 * LANES), f32)] * 2
        out_specs = [
            pl.BlockSpec((3, SEQ, LANES), lambda p, s: (0, s, first + p)),
            pl.BlockSpec((1, 2, SPAN), lambda p, s: (p, 0, 0)),
        ]
        out_shape = [
            jax.ShapeDtypeStruct((3, tokens, INNER), bf16),
            jax.ShapeDtypeStruct((pairs, 2, SPAN), f32),
        ]
    else:
        out_specs = [block(0), pl.BlockSpec((2, SEQ, LANES), lambda p, s: (0, s, p))]
        out_shape = [
            jax.ShapeDtypeStruct((tokens, INNER), bf16),
            jax.ShapeDtypeStruct((2, tokens, INNER), bf16),
        ]
    aliases = {}
    if into is not None:
        after = [into, *after]
        aliases = {0: 0}
    return pl.pallas_call(
        partial(attend_backward_kernel, ranges, biased, len(after)),
        grid=(pairs, sequences),
        in_specs=[pl.BlockSpec(memory_space=pl.ANY)] * len(after) + in_specs,
        out_specs=out_specs,
        out_shape=out_shape,
        scratch_shapes=scratch,
        input_output_aliases=aliases,
        compiler_params=pltpu.CompilerParams(vmem_limit_bytes=VMEM_LIMIT),
        cost_estimate=LIGHT,
    )(*after, *args)


def shares(core, value, keep_ref, send_ref, *at):
    rows, cols = value.shape
    parts = value.astype(bf16).reshape(2, 2, rows // 4, cols)
    for y in range(2):
        place = (y,) + at
        keep_ref[place] = jnp.where(core == 0, parts[y, 0], parts[y, 1])
        send_ref[place] = jnp.where(core == 0, parts[y, 1], parts[y, 0])


def place_pieces(where_ref, full, own, core, y, x, yc, xc):
    shard = where_ref[0]
    rows, cols = own.shape
    half = cols // 2

    def at(index):
        return pl.ds(pl.multiple_of(index * rows, rows), rows)

    full[at(shard), :] = own[...]
    full[at(shard ^ 1), :] = core[...]
    for bit in range(2):

        @pl.when(where_ref[1] == bit)
        def _():
            mine = slice(bit * half, (bit + 1) * half)
            other = slice((1 - bit) * half, (2 - bit) * half)
            full[at(shard ^ 2), mine] = y[...]
            full[at(shard ^ 2), other] = x[...]
            full[at(shard ^ 3), mine] = yc[...]
            full[at(shard ^ 3), other] = xc[...]


def whole_spec(array):
    return pl.BlockSpec(
        array.shape, lambda i, c: (0,) * array.ndim, pipeline_mode=pl.Buffered(1)
    )


def normed_rows(x, gain):
    factor = lax.rsqrt(jnp.mean(x * x, -1, keepdims=True) + eps)
    return (x * factor * gain).astype(bf16)


def first_kernel(where_ref, x_ref, onehot_ref, valid_ref, *refs):
    pieces_in = refs[:6]
    full, gains_ref, g_ref, n_ref, qkv_ref = refs[6:]

    @pl.when(pl.program_id(0) == 0)
    def _():
        place_pieces(where_ref, full, *pieces_in)
        small = full[:, 3 * INNER : 3 * INNER + LANES].astype(f32).T
        gains_ref[...] = small[0:8]
        table = small[16:32].astype(bf16)
        bias = jnp.where(valid_ref[...] > 0, dot_nn(table, onehot_ref[...]), masked_score)
        for pair in range(PAIRS):
            g_ref[pair] = bias[2 * pair : 2 * pair + 2]

    normed = normed_rows(x_ref[...].astype(f32), gains_ref[0:1, :])
    n_ref[...] = normed
    for part in range(3):
        columns = slice(part * D, (part + 1) * D)
        qkv_ref[:, columns] = dot_nn(normed, full[:, columns]).astype(bf16)


def first_step(where, x, pieces_in, onehot, valid):
    tokens = x.shape[0]
    width = pieces_in[0].shape[1]
    block = pl.BlockSpec((ROWS, D), lambda i, c: (i, 0))
    return pl.pallas_call(
        first_kernel,
        grid_spec=pltpu.PrefetchScalarGridSpec(
            num_scalar_prefetch=1,
            grid=(tokens // ROWS,),
            in_specs=[block, whole_spec(onehot), whole_spec(valid)]
            + [whole_spec(p) for p in pieces_in],
            out_specs=[
                pl.BlockSpec((D, width), lambda i, c: (0, 0)),
                pl.BlockSpec((8, D), lambda i, c: (0, 0)),
                pl.BlockSpec((PAIRS, 2, SPAN), lambda i, c: (0, 0, 0)),
                block,
                pl.BlockSpec((ROWS, 3 * INNER), lambda i, c: (i, 0)),
            ],
        ),
        out_shape=[
            jax.ShapeDtypeStruct((D, width), bf16),
            jax.ShapeDtypeStruct((8, D), f32),
            jax.ShapeDtypeStruct((PAIRS, 2, SPAN), f32),
            jax.ShapeDtypeStruct((tokens, D), bf16),
            jax.ShapeDtypeStruct((tokens, 3 * INNER), bf16),
        ],
        compiler_params=pltpu.CompilerParams(vmem_limit_bytes=VMEM_LIMIT),
        cost_estimate=LIGHT,
    )(where, x, onehot, valid, *pieces_in)


def encoder_kernel(waits, where_ref, *refs):
    refs = refs[waits:]
    x_ref, pieces_in = refs[0], refs[1:7]
    full, kv_ref = refs[7:]

    @pl.when(pl.program_id(0) == 0)
    def _():
        place_pieces(where_ref, full, *pieces_in)

    for part in range(2):
        columns = slice(part * D, (part + 1) * D)
        kv_ref[:, columns] = dot_nn(x_ref[...], full[:, columns]).astype(bf16)


def encoder_step(where, x, pieces_in, after):
    tokens = x.shape[0]
    width = pieces_in[0].shape[1]
    return pl.pallas_call(
        partial(encoder_kernel, len(after)),
        grid_spec=pltpu.PrefetchScalarGridSpec(
            num_scalar_prefetch=1,
            grid=(tokens // ROWS,),
            in_specs=[pl.BlockSpec(memory_space=pl.ANY)] * len(after)
            + [pl.BlockSpec((ROWS, D), lambda i, c: (i, 0))]
            + [whole_spec(p) for p in pieces_in],
            out_specs=[
                pl.BlockSpec((D, width), lambda i, c: (0, 0)),
                pl.BlockSpec((ROWS, 2 * INNER), lambda i, c: (i, 0)),
            ],
        ),
        out_shape=[
            jax.ShapeDtypeStruct((D, width), bf16),
            jax.ShapeDtypeStruct((tokens, 2 * INNER), bf16),
        ],
        compiler_params=pltpu.CompilerParams(vmem_limit_bytes=VMEM_LIMIT),
        cost_estimate=LIGHT,
    )(where, *after, x, *pieces_in)


def middle_kernel(x_ref, attn_ref, out_w_ref, gain_ref, q_w_ref, first_ref, n_ref, cq_ref):
    first = x_ref[...].astype(f32) + dot_nn(attn_ref[...], out_w_ref[...])
    first_ref[...] = first
    normed = normed_rows(first, gain_ref[...])
    n_ref[...] = normed
    cq_ref[...] = dot_nn(normed, q_w_ref[...]).astype(bf16)


def middle_step(x, attn, gain, w_cross):
    tokens = x.shape[0]
    block = pl.BlockSpec((ROWS, D), lambda i: (i, 0))
    return pl.pallas_call(
        middle_kernel,
        grid=(tokens // ROWS,),
        in_specs=[
            block,
            block,
            pl.BlockSpec((D, D), lambda i: (0, 4)),
            pl.BlockSpec((1, D), lambda i: (0, 0)),
            pl.BlockSpec((D, D), lambda i: (0, 2)),
        ],
        out_specs=[block] * 3,
        out_shape=[
            jax.ShapeDtypeStruct((tokens, D), f32),
            jax.ShapeDtypeStruct((tokens, D), bf16),
            jax.ShapeDtypeStruct((tokens, D), bf16),
        ],
        compiler_params=pltpu.CompilerParams(vmem_limit_bytes=VMEM_LIMIT),
        cost_estimate=LIGHT,
    )(x, attn, w_cross, gain, w_cross)


def shares(core, value, keep_ref, send_ref, *at, start=0):
    rows, cols = value.shape
    parts = value.astype(bf16).reshape(2, 2, rows // 4, cols)
    columns = slice(start, start + cols)
    for y in range(2):
        place = (y,) + at + (slice(None), columns)
        keep_ref[place] = jnp.where(core == 0, parts[y, 0], parts[y, 1])
        send_ref[place] = jnp.where(core == 0, parts[y, 1], parts[y, 0])


def feed_forward_kernel(
    where_ref, x1_ref, attn_ref, w2_ref, gain_ref, dout_ref,
    own_g, own_u, core_g, core_u, y_in, x_in, yc_in, xc_in,
    own_o, core_o, y_o, x_o, yc_o, xc_o,
    layer_ref, gx_ref, gx16_ref, gk_ref, gs_ref, ok_ref, os_ref,
    wg, wu, wo, n3, n3t, acc, dn, hid, dgate, dup,
):
    step = pl.program_id(0)
    shard, across = where_ref[0], where_ref[1]
    tokens = x1_ref.shape[0]
    chunks = tokens // ROWS
    rows_in = own_g.shape[0]

    def at(index):
        return pl.ds(pl.multiple_of(index * rows_in, rows_in), rows_in)

    wg[at(shard), :] = own_g[...]
    wu[at(shard), :] = own_u[...]
    wg[at(shard ^ 1), :] = core_g[...]
    wu[at(shard ^ 1), :] = core_u[...]

    @pl.when(across == 0)
    def _():
        wg[at(shard ^ 2), :] = y_in[...]
        wu[at(shard ^ 2), :] = x_in[...]
        wg[at(shard ^ 3), :] = yc_in[...]
        wu[at(shard ^ 3), :] = xc_in[...]

    @pl.when(across == 1)
    def _():
        wg[at(shard ^ 2), :] = x_in[...]
        wu[at(shard ^ 2), :] = y_in[...]
        wg[at(shard ^ 3), :] = xc_in[...]
        wu[at(shard ^ 3), :] = yc_in[...]

    half = D // 2
    for turn, whole in ((0, own_o), (1, core_o)):

        @pl.when(step == turn)
        def _():
            wo[...] = whole[...]

    for turn, near, far in ((2, y_o, x_o), (3, yc_o, xc_o)):
        for bit in range(2):

            @pl.when((step == turn) & (across == bit))
            def _():
                wo[:, bit * half : (bit + 1) * half] = near[...]
                wo[:, (1 - bit) * half : (2 - bit) * half] = far[...]

    @pl.when(step == 0)
    def _():
        gain = gain_ref[...]
        for chunk in range(chunks):
            rows = slice(chunk * ROWS, (chunk + 1) * ROWS)
            x = x1_ref[rows, :] + dot_nn(attn_ref[rows, :], w2_ref[...])
            gx_ref[rows, :] = x
            normed = normed_rows(x, gain)
            n3[rows, :] = normed
            n3t[:, rows] = normed.T
            acc[rows, :] = jnp.zeros((ROWS, D), f32)
            dn[rows, :] = jnp.zeros((ROWS, D), f32)

    c = math.sqrt(2.0 / math.pi)
    for chunk in range(chunks):
        rows = slice(chunk * ROWS, (chunk + 1) * ROWS)
        normed = n3[rows, :]
        gate = dot_nn(normed, wg[...])
        up = dot_nn(normed, wu[...])
        dhidden = dot_nt(dout_ref[rows, :], wo[...]).astype(bf16).astype(f32)
        square = gate * gate
        t = jnp.tanh(c * gate * (1.0 + 0.044715 * square))
        mid = 0.5 * (1.0 + t)
        act = gate * mid
        slope = mid + (0.5 * c) * gate * (1.0 - t * t) * (1.0 + (3.0 * 0.044715) * square)
        hid[rows, :] = (act * up).astype(bf16)
        dgate[rows, :] = (dhidden * up * slope).astype(bf16)
        dup[rows, :] = (dhidden * act).astype(bf16)
        acc[rows, :] += dot_nn(hid[rows, :], wo[...])
        dn[rows, :] += dot_nt(dgate[rows, :], wg[...]) + dot_nt(dup[rows, :], wu[...])
    core = shard % 2
    for part, grads in enumerate((dgate, dup)):
        for start in range(0, FF_BLOCK, ROWS):
            value = dot_nn(n3t[...], grads[:, start : start + ROWS])
            shares(core, value, gk_ref, gs_ref, part, start=start)
    out_grad = dot_tn(hid[...], dout_ref[...]).astype(bf16)

    @pl.when(step % 2 == 0)
    def _():
        ok_ref[0] = out_grad

    @pl.when(step % 2 == 1)
    def _():
        os_ref[0] = out_grad

    @pl.when(step == pl.num_programs(0) - 1)
    def _():
        gain = gain_ref[...]
        for chunk in range(chunks):
            rows = slice(chunk * ROWS, (chunk + 1) * ROWS)
            x = gx_ref[rows, :]
            layer_ref[rows, :] = (x + acc[rows, :]).astype(bf16)
            factor = lax.rsqrt(jnp.mean(x * x, -1, keepdims=True) + eps)
            d = dn[rows, :]
            weighted = d * gain
            back = factor * weighted - x * (
                factor * factor * factor * jnp.mean(weighted * x, -1, keepdims=True)
            )
            gx = dout_ref[rows, :].astype(f32) + back
            gx_ref[rows, :] = gx
            gx16_ref[rows, :] = gx.astype(bf16)


def feed_forward(where, x1, attn, w_cross, gain, dout, in_pieces, out_pieces):
    tokens = x1.shape[0]
    steps = FF // FF_BLOCK
    one = pl.Buffered(1)
    rows_in = in_pieces[0].shape[0]

    def whole(width=D):
        return pl.BlockSpec((tokens, width), lambda f, c: (0, 0), pipeline_mode=one)

    def streamed(at):
        return pl.BlockSpec((rows_in, FF_BLOCK), lambda f, c: (0, at + (c[0] ^ f)))

    resident = pl.BlockSpec((tokens, D), lambda f, c: (0, 0))
    in_share = pl.BlockSpec((2, 2, D // 4, FF_BLOCK), lambda f, c: (0, 0, 0, c[0] ^ f))
    out_share = pl.BlockSpec((1, FF_BLOCK, D), lambda f, c: ((c[0] ^ f) // 2, 0, 0))
    in_type = jax.ShapeDtypeStruct((2, 2, D // 4, FF), bf16)
    out_type = jax.ShapeDtypeStruct((2, FF_BLOCK, D), bf16)
    own_i, core_i, *halves_i = in_pieces
    return pl.pallas_call(
        feed_forward_kernel,
        grid_spec=pltpu.PrefetchScalarGridSpec(
            num_scalar_prefetch=1,
            grid=(steps,),
            in_specs=[
                whole(),
                whole(),
                pl.BlockSpec((D, D), lambda f, c: (0, 3), pipeline_mode=one),
                pl.BlockSpec((1, D), lambda f, c: (0, 0)),
                whole(),
                streamed(0), streamed(steps), streamed(0), streamed(steps),
                streamed(0), streamed(0), streamed(0), streamed(0),
            ]
            + [whole_spec(p) for p in out_pieces],
            out_specs=[resident, resident, resident, in_share, in_share, out_share, out_share],
            scratch_shapes=[
                pltpu.VMEM((D, FF_BLOCK), bf16),
                pltpu.VMEM((D, FF_BLOCK), bf16),
                pltpu.VMEM((FF_BLOCK, D), bf16),
                pltpu.VMEM((tokens, D), bf16),
                pltpu.VMEM((D, tokens), bf16),
                pltpu.VMEM((tokens, D), f32),
                pltpu.VMEM((tokens, D), f32),
                pltpu.VMEM((tokens, FF_BLOCK), bf16),
                pltpu.VMEM((tokens, FF_BLOCK), bf16),
                pltpu.VMEM((tokens, FF_BLOCK), bf16),
            ],
        ),
        out_shape=[
            jax.ShapeDtypeStruct((tokens, D), bf16),
            jax.ShapeDtypeStruct((tokens, D), f32),
            jax.ShapeDtypeStruct((tokens, D), bf16),
            in_type, in_type, out_type, out_type,
        ],
        compiler_params=pltpu.CompilerParams(vmem_limit_bytes=VMEM_LIMIT),
        cost_estimate=LIGHT,
    )(where, x1, attn, w_cross, gain, dout, own_i, own_i, core_i, core_i, *halves_i, *out_pieces)


def weight_grad_kernel(counts, firsts, waits, core_ref, *refs):
    refs = refs[waits:]
    terms = len(counts)
    lefts, rights = refs[0:terms], refs[terms : 2 * terms]
    refs = refs[2 * terms :]
    second = firsts is not None
    if second:
        tiny_ref, keep_ref, send_ref, keep2_ref, send2_ref, left_t = refs
    else:
        keep_ref, send_ref, left_t = refs
    step = pl.program_id(0)
    core = core_ref[0] % 2
    at = 0
    for left, right, count in zip(lefts, rights, counts):

        @pl.when(step == at)
        def _():
            left_t[...] = left[...].T

        def product(keep, send):
            for start in range(0, D, ROWS):
                columns = slice(start, start + ROWS)
                block = right[:, columns] if len(right.shape) == 2 else right[0, :, columns]
                shares(core, dot_nn(left_t[...], block), keep, send, start=start)

        @pl.when((step >= at) & (step < (firsts if second else at + count)))
        def _():
            product(keep_ref, send_ref)

        if second:

            @pl.when(step >= firsts)
            def _():
                product(keep2_ref, send2_ref)
                tiny = tiny_ref[...]
                for y in range(2):
                    keep2_ref[y, :, D:] = jnp.where(core == 0, tiny[y, 0], tiny[y, 1])
                    send2_ref[y, :, D:] = jnp.where(core == 0, tiny[y, 1], tiny[y, 0])

        at += count


def weight_grad(where, terms, tiny=None, after=()):
    tokens = terms[0][0].shape[0]
    counts = []
    rights = []
    at = 0
    for _, right in terms:
        deep = right.ndim == 3
        count = right.shape[0] if deep else 1

        def place(j, c, at=at, count=count, deep=deep):
            return (jnp.clip(j - at, 0, count - 1), 0, 0) if deep else (0, 0)

        rights.append(pl.BlockSpec((1, tokens, D) if deep else (tokens, D), place))
        counts.append(count)
        at += count
    firsts = None if tiny is None else at - 1
    blocks = at if tiny is None else at - 1
    share = pl.BlockSpec((2, D // 4, D), lambda j, c: (0, 0, jnp.minimum(j, blocks - 1)))
    out_specs = [share, share]
    out_shape = [jax.ShapeDtypeStruct((2, D // 4, blocks * D), bf16)] * 2
    extra_specs, extra = [], []
    if tiny is not None:
        extra_specs, extra = [pl.BlockSpec(tiny.shape, lambda j, c: (0, 0, 0, 0))], [tiny]
        wide = D + tiny.shape[-1]
        out_specs += [pl.BlockSpec((2, D // 4, wide), lambda j, c: (0, 0, 0))] * 2
        out_shape += [jax.ShapeDtypeStruct((2, D // 4, wide), bf16)] * 2
    return pl.pallas_call(
        partial(weight_grad_kernel, counts, firsts, len(after)),
        grid_spec=pltpu.PrefetchScalarGridSpec(
            num_scalar_prefetch=1,
            grid=(at,),
            in_specs=[pl.BlockSpec(memory_space=pl.ANY)] * len(after)
            + [pl.BlockSpec((tokens, D), lambda j, c: (0, 0))] * len(terms)
            + rights
            + extra_specs,
            out_specs=out_specs,
            scratch_shapes=[pltpu.VMEM((D, tokens), bf16)],
        ),
        out_shape=out_shape,
        compiler_params=pltpu.CompilerParams(vmem_limit_bytes=VMEM_LIMIT),
        cost_estimate=LIGHT,
    )(where, *after, *[left for left, _ in terms], *[right for _, right in terms], *extra)


def norm_back_kernel(normed, onward, waits, *refs):
    refs = refs[waits:]
    grad_ref, w_ref = refs[:2]
    total = None
    for part in range(grad_ref.shape[0]):
        term = dot_nt(grad_ref[part], w_ref[:, part * D : (part + 1) * D])
        total = term if total is None else total + term
    if not normed:
        refs[2][...] = total.astype(refs[2].dtype)
        return
    x_ref, gain_ref, up_ref = refs[2:5]
    refs = refs[5:]
    if onward:
        next_ref, out_ref, gain_grad_ref, out16_ref, onward_ref = refs
    else:
        out_ref, gain_grad_ref = refs
    x = x_ref[...].astype(f32)
    factor = lax.rsqrt(jnp.mean(x * x, -1, keepdims=True) + eps)
    weighted = total * gain_ref[...]
    grad_gain = jnp.sum(total * x * factor, axis=0, keepdims=True)

    @pl.when(pl.program_id(0) == 0)
    def _():
        gain_grad_ref[...] = jnp.zeros_like(gain_grad_ref)

    gain_grad_ref[...] += grad_gain
    scale = factor * factor * factor * jnp.mean(weighted * x, -1, keepdims=True)
    out = up_ref[...] + factor * weighted - x * scale
    out_ref[...] = out
    if onward:
        out16 = out.astype(bf16)
        out16_ref[...] = out16
        onward_ref[...] = dot_nt(out16, next_ref[...]).astype(bf16)


def norm_back(
    grads, w, w_at, x=None, gain=None, upstream=None, w_next=None, next_at=0, after=(), kind=f32
):
    if grads.ndim == 2:
        grads = grads[None]
    parts, tokens, _ = grads.shape
    block = pl.BlockSpec((ROWS, D), lambda i: (i, 0))
    row = pl.BlockSpec((1, D), lambda i: (0, 0))
    in_specs = [pl.BlockSpec(memory_space=pl.ANY)] * len(after)
    in_specs += [
        pl.BlockSpec((parts, ROWS, D), lambda i: (0, i, 0)),
        pl.BlockSpec((D, parts * D), lambda i: (0, w_at)),
    ]
    args = [*after, grads, w]
    wide = jax.ShapeDtypeStruct((tokens, D), kind)
    half = jax.ShapeDtypeStruct((tokens, D), bf16)
    out_specs, out_shape = [block], [wide]
    if x is not None:
        in_specs += [block, row, block]
        args += [x, gain, upstream]
        out_specs.append(row)
        out_shape.append(jax.ShapeDtypeStruct((1, D), f32))
        if w_next is not None:
            in_specs.append(pl.BlockSpec((D, D), lambda i: (0, next_at)))
            args.append(w_next)
            out_specs += [block, block]
            out_shape += [half, half]
    return pl.pallas_call(
        partial(norm_back_kernel, x is not None, w_next is not None, len(after)),
        grid=(tokens // ROWS,),
        in_specs=in_specs,
        out_specs=out_specs,
        out_shape=out_shape,
        compiler_params=pltpu.CompilerParams(vmem_limit_bytes=VMEM_LIMIT),
        cost_estimate=LIGHT,
    )(*args)


def exchange(array, axis, size, bit):
    return lax.ppermute(array, axis, [(i, i ^ bit) for i in range(size)])


def part_of(array, dim, index):
    half = array.shape[dim] // 2
    return lax.dynamic_slice_in_dim(array, index * half, half, dim)


def tie(value, *others):
    return lax.optimization_barrier((value, *others))[0]


def meet(done, *moves):
    *gots, done = lax.optimization_barrier((*[m.got for m in moves], done))
    for move, got in zip(moves, gots):
        move.got = got
    return done


class Gather:
    def __init__(self, own, sizes, *after):
        self.sizes = sizes
        self.own = own
        half = part_of(own, 1, lax.axis_index("rep") % 2)
        if after:
            half = tie(half, *after)
        self.half = half
        self.got = exchange(half, "shard", sizes[0], 2)

    def cross(self):
        self.y = self.got
        self.got = exchange(self.y, "rep", self.sizes[1], 1)
        self.core = exchange(tie(self.own, self.y), "shard", self.sizes[0], 1)
        self.yc = exchange(self.y, "shard", self.sizes[0], 1)

    def pieces(self):
        self.x = self.got
        xc = exchange(self.x, "shard", self.sizes[0], 1)
        return self.own, self.core, self.y, self.x, self.yc, xc


class Chain:
    def __init__(self, keep, send, sizes, dims, order, turned=False):
        self.shards, self.reps = sizes
        self.bits = [1 << b for b in range(self.reps.bit_length() - 1)]
        self.dims = [dims[min(i, len(dims) - 1)] for i in range(len(self.bits))]
        if turned:
            self.bits[:2] = self.bits[1::-1]
            self.dims[:2] = self.dims[1::-1]
        steps = []
        for name in order:
            if name == "y":
                steps.append(("shard", 2, 0))
            else:
                steps += [("rep", bit, dim) for bit, dim in zip(self.bits, self.dims)]
        self.steps = steps
        self.kept = keep
        self.got = exchange(send, "shard", self.shards, 1)
        self.sent = send
        self.at = 0

    def own(self):
        while self.at < len(self.steps):
            self.advance()
        return (self.kept.astype(f32) + self.got.astype(f32)).astype(bf16)

    def advance(self):
        axis, bit, dim = self.steps[self.at]
        self.at += 1
        mine = (lax.axis_index(axis) // bit) % 2
        size = self.shards if axis == "shard" else self.reps
        def half(index):
            kept, got = (part_of(part, dim, index).astype(f32) for part in (self.kept, self.got))
            return lax.optimization_barrier((kept + got).astype(bf16))

        self.sent = half(1 - mine)
        self.kept = half(mine)
        self.got = exchange(self.sent, axis, size, bit)
        return self.got


class Spread:
    def __init__(self, own, sizes, bits, dims):
        self.own = own
        self.reps = sizes[1]
        self.left = list(zip(bits, dims))
        self.got = None
        self.advance()

    def pair(self):
        bit, _ = self.now
        mine = (lax.axis_index("rep") // bit) % 2
        low = jnp.where(mine == 0, self.own, self.got)
        high = jnp.where(mine == 0, self.got, self.own)
        return low, high

    def advance(self):
        if self.got is not None:
            self.own = jnp.concatenate(self.pair(), axis=self.now[1])
        self.now = self.left.pop()
        self.got = exchange(self.own, "rep", self.reps, self.now[0])


def together(*moves):
    gots = lax.optimization_barrier(tuple(m.got for m in moves))
    for move, got in zip(moves, gots):
        move.got = got


def unpack_kernel(where_ref, own_ref, got_ref, w_ref, in_ref, out_ref, sum_ref):
    mine = where_ref[2]
    half, _, rows, cols = own_ref.shape
    out_rows = out_ref.shape[0] // (2 * half)
    total = jnp.zeros((rows, LANES), f32)
    for blocks_ref, bit in ((own_ref, mine), (got_ref, 1 - mine)):
        for block in range(half):
            at = block // 2 * 4 + bit * 2 + block % 2
            for part in range(2):
                place = pl.ds(pl.multiple_of(part * FF + at * cols, cols), cols)
                value = blocks_ref[block, part].astype(f32)
                in_ref[:, place] = value
                product = value * w_ref[:, place].astype(f32)
                for lane in range(0, cols, LANES):
                    total = total + product[:, lane : lane + LANES]
            place = pl.ds(pl.multiple_of(at * out_rows, out_rows), out_rows)
            for group in range(D // cols):
                out_ref[place, group * cols : (group + 1) * cols] = blocks_ref[
                    block, 2, group * out_rows : (group + 1) * out_rows, :
                ].astype(f32)
    row = jnp.broadcast_to(jnp.sum(total, axis=1, keepdims=True), (rows, LANES)).T
    sum_ref[...] = row[0:8]


def unpack(where, own, got, w):
    rows = own.shape[2]

    def whole(shape):
        return pl.BlockSpec(shape, lambda i, c: (0,) * len(shape))

    outs = [
        jax.ShapeDtypeStruct((rows, 2 * FF), f32),
        jax.ShapeDtypeStruct((FF * rows // D, D), f32),
        jax.ShapeDtypeStruct((8, rows), f32),
    ]
    return pl.pallas_call(
        unpack_kernel,
        grid_spec=pltpu.PrefetchScalarGridSpec(
            num_scalar_prefetch=1,
            grid=(1,),
            in_specs=[whole(own.shape), whole(got.shape), whole(w.shape)],
            out_specs=[whole(o.shape) for o in outs],
        ),
        out_shape=outs,
        compiler_params=pltpu.CompilerParams(vmem_limit_bytes=VMEM_LIMIT),
        cost_estimate=LIGHT,
    )(where, own, got, w)


def bias_rows(shards):
    lane = np.arange(SPAN)
    distance = np.where(lane < SEQ, SEQ - LANES - lane, 2 * SEQ - lane)
    bucket = np.zeros(SPAN, np.int64)
    for edge in bucket_edges:
        bucket += distance >= edge
    valid = (distance >= 0) & (distance < SEQ)
    onehot = np.zeros((SPAN, NUM_BUCKETS), np.float32)
    onehot[np.arange(SPAN)[valid], bucket[valid]] = 1.0
    own = NUM_BUCKETS // shards
    rows = np.arange(NUM_BUCKETS) // own * (D // shards) + np.arange(NUM_BUCKETS) % own
    placed = np.zeros((D, SPAN), np.float32)
    placed[rows] = onehot.T
    return onehot, placed, valid[None].astype(np.float32)


def local(
    sizes,
    hidden_in,
    enc_states,
    dec_segments,
    enc_segments,
    out_grad,
    gains,
    rel_table,
    self_qkv,
    self_out,
    cross_q,
    cross_kv,
    cross_out,
    ff_in,
    ff_out,
):
    shards, reps = sizes
    own_rows = D // shards
    own_buckets = NUM_BUCKETS // shards
    width = reps.bit_length() - 1
    shard = lax.axis_index("shard")
    rep = lax.axis_index("rep")
    where = jnp.stack([shard, rep % 2, rep // 2 % 2]).astype(jnp.int32)
    small = jnp.concatenate(
        [
            gains.T,
            jnp.zeros((own_rows, 13), bf16),
            jnp.pad(rel_table, ((0, own_rows - own_buckets), (0, 2 * LANES - 16 - HEADS))),
        ],
        axis=1,
    )
    self_set = Gather(jnp.concatenate([self_qkv, small], axis=1), sizes)
    self_set.cross()
    cross_set = Gather(
        jnp.concatenate([cross_kv, cross_q, cross_out, self_out], axis=1), sizes, self_set.y
    )
    self_pieces = self_set.pieces()

    lane = jnp.arange(LANES, dtype=jnp.int32)[None, :]
    dec_ids = dec_segments[:, None]
    enc_ids = enc_segments[:, None]
    ones = ((lane % HEAD_DIM >= 2) & (lane % HEAD_DIM <= 4)).astype(f32)

    def key_extra(ids):
        return jnp.where(lane < 2, jnp.where(lane != ids, masked_score, 0.0), ones).astype(bf16)

    q_extra = ((lane < 2) & (lane == dec_ids)).astype(bf16)
    self_extra = key_extra(dec_ids)
    cross_extra = key_extra(enc_ids)
    onehot, placed, valid = bias_rows(shards)
    w_self, gains_all, g, normed_one, qkv = first_step(
        where, hidden_in, self_pieces, placed.astype(bf16), valid
    )
    meet(normed_one, cross_set)
    cross_set.cross()
    out_set = Gather(ff_out, sizes, cross_set.y)
    in_set = Gather(ff_in, sizes, cross_set.y)
    attn_one, lows_one = attend_forward(
        qkv, 0, qkv, PAIRS, qkv, 2 * PAIRS, q_extra, self_extra, g, SELF_RANGES,
        after=[out_set.half, in_set.half],
    )
    meet(attn_one, cross_set, out_set, in_set)
    cross_pieces = cross_set.pieces()
    out_set.cross()
    in_set.cross()
    w_cross, ckv = encoder_step(where, enc_states, cross_pieces, [attn_one])
    first, normed_two, cq = middle_step(hidden_in, attn_one, gains_all[1:2], w_cross)
    attn_two, lows_two = attend_forward(
        cq, 0, ckv, 0, ckv, PAIRS, q_extra, cross_extra, None, CROSS_RANGES
    )
    meet(attn_two, out_set, in_set)
    ff_out_pieces = out_set.pieces()
    ff_in_pieces = in_set.pieces()
    layer_out, grad_second, out_two, in_keep, in_send, out_keep, out_send = feed_forward(
        where, first, attn_two, w_cross, gains_all[2:3], out_grad, ff_in_pieces, ff_out_pieces
    )
    ff_in_chain = Chain(in_keep, in_send, sizes, [3], "yr")
    ff_out_chain = Chain(out_keep, out_send, sizes, [1], "ry")
    (grad_attn_two,) = norm_back(out_two, w_cross, 3, kind=bf16, after=[layer_out])
    meet(grad_attn_two, ff_in_chain, ff_out_chain)
    ff_out_chain.advance()
    ff_in_chain.advance()
    grad_cq, grad_ckv = attend_backward(
        cq, 0, ckv, 0, ckv, PAIRS, q_extra, cross_extra, lows_two, attn_two, grad_attn_two,
        None, CROSS_RANGES, after=[ff_in_chain.sent, ff_out_chain.sent],
    )
    meet(grad_cq, ff_out_chain)
    ff_out_chain.advance()
    grad_first, _, out_one, grad_attn_one = norm_back(
        grad_cq, w_cross, 2, first, gains_all[1:2], grad_second, w_cross, 4,
        after=[ff_out_chain.sent],
    )
    meet(grad_attn_one, ff_in_chain, ff_out_chain)
    ff_in_chain.advance()
    ff_out_chain.advance()
    cross_keep, cross_send = weight_grad(
        where,
        [(enc_states, grad_ckv), (normed_two, grad_cq), (attn_two, out_two), (attn_one, out_one)],
        after=[ff_in_chain.sent, ff_out_chain.sent],
    )
    cross_send = meet(cross_send, ff_in_chain, ff_out_chain)
    ff_in_chain.advance()
    ff_out_chain.advance()
    cross_chain = Chain(cross_keep, cross_send, sizes, [2, 1], "yr", turned=True)
    (enc_grad,) = norm_back(
        grad_ckv, w_cross, 0, after=[cross_keep, ff_in_chain.sent, ff_out_chain.sent]
    )
    meet(enc_grad, cross_chain, ff_in_chain, ff_out_chain)
    cross_chain.advance()
    ff_in_chain.advance()
    out_own = ff_out_chain.own()[0]
    backward = partial(
        attend_backward, qkv, 0, qkv, PAIRS, qkv, 2 * PAIRS, q_extra, self_extra, lows_one,
        attn_one, grad_attn_one, g, SELF_RANGES, pairs=PAIRS // 2,
    )
    some_qkv, some_rel = backward(after=[cross_chain.sent, ff_in_chain.sent, out_own])
    some_qkv = meet(some_qkv, ff_in_chain)
    in_own = ff_in_chain.own()[0]
    rows, columns = in_own.shape[1:]
    out_rows = out_own.shape[0]
    out_own = out_own.reshape(out_rows, -1, columns).transpose(1, 0, 2).reshape(1, rows, columns)
    bits = [2, 1, 4] if reps == 8 else ff_in_chain.bits
    blocks = Spread(
        jnp.concatenate([in_own, out_own], axis=0)[None], sizes, bits, [0] * len(bits)
    )
    grad_qkv, more_rel = backward(after=[blocks.own], first=PAIRS // 2, into=some_qkv)
    rel_part = jnp.concatenate([some_rel, more_rel], axis=0)
    grad_qkv = meet(grad_qkv, cross_chain, blocks)
    cross_chain.advance()
    blocks.advance()
    table_part = jnp.einsum(
        "hu,ub->bh",
        rel_part.reshape(HEADS, SPAN),
        onehot,
        precision=lax.Precision.HIGHEST,
        preferred_element_type=f32,
    )
    tiny = table_part.reshape(2, 2, own_buckets, HEADS).astype(bf16)
    tiny = jnp.pad(tiny, ((0, 0), (0, 0), (0, own_rows - own_buckets), (0, 2 * LANES - HEADS)))
    self_keep, self_send, last_keep, last_send = weight_grad(
        where, [(normed_one, grad_qkv)], tiny=tiny, after=[blocks.own, cross_chain.sent]
    )
    self_send = meet(self_send, blocks, cross_chain)
    blocks.advance()
    cross_chain.advance()
    self_chain = Chain(self_keep, self_send, sizes, [2, 1], "yr")
    last_chain = Chain(last_keep, last_send, sizes, [2, 1], "ry")
    self_chain.advance()
    last_chain.advance()
    in_grad, _ = norm_back(
        grad_qkv, w_self, 0, hidden_in, gains_all[0:1], grad_first,
        after=[self_chain.sent, last_chain.sent, cross_chain.sent, blocks.own],
    )
    meet(in_grad, self_chain, last_chain, cross_chain)
    self_chain.advance()
    last_chain.advance()
    cross_chain.advance()
    cross_spread = None
    while last_chain.at < len(last_chain.steps):
        if last_chain.at == 3:
            together(self_chain, last_chain, cross_chain, blocks)
            cross_spread = Spread(cross_chain.own(), sizes, cross_chain.bits, cross_chain.dims)
        else:
            together(self_chain, last_chain)
        self_chain.advance()
        last_chain.advance()
    together(self_chain, last_chain, cross_spread)
    if cross_spread.left:
        cross_spread.advance()
    self_width = self_chain.got.shape[2]
    self_spread = Spread(
        jnp.concatenate([self_chain.own(), last_chain.own()], axis=2),
        sizes, self_chain.bits, self_chain.dims,
    )
    while self_spread.left:
        if cross_spread.left:
            together(self_spread, cross_spread)
            cross_spread.advance()
        self_spread.advance()
    low, high = self_spread.pair()
    low, high = low[0], high[0]
    self_grad = jnp.concatenate(
        [low[:, :self_width], high[:, :self_width], low[:, self_width:], high[:, self_width:]],
        axis=1,
    ).astype(f32)
    cross_grad = jnp.concatenate(cross_spread.pair(), axis=cross_spread.now[1])[0].astype(f32)

    if reps == 8:
        ff_in_grad, ff_out_grad, in_sums = unpack(where, blocks.own, blocks.got, ff_in)
        in_sums = in_sums[0]
    else:
        while blocks.left:
            blocks.advance()
        spread = jnp.concatenate(blocks.pair(), axis=0)
        in_grads = spread[:, :2].transpose(2, 1, 0, 3)
        ff_in_grad = in_grads.reshape(own_rows, 2 * FF).astype(f32)
        out_grads = spread[:, 2].reshape(reps, -1, out_rows, columns).transpose(0, 2, 1, 3)
        ff_out_grad = out_grads.reshape(ff_out.shape).astype(f32)
        in_sums = jnp.sum(ff_in.astype(f32) * ff_in_grad, axis=1)

    self_qkv_grad = self_grad[:, : 3 * INNER]
    cross_query_gradient = cross_grad[:, 2 * INNER : 3 * INNER]

    sums = jnp.stack(
        [
            jnp.sum(self_qkv.astype(f32) * self_qkv_grad, axis=1),
            jnp.sum(cross_q.astype(f32) * cross_query_gradient, axis=1),
            in_sums,
        ]
    )
    gains_grad = sums / gains.astype(f32)
    rel_table_grad = self_grad[:own_buckets, 3 * INNER : 3 * INNER + HEADS]
    return (
        layer_out,
        in_grad,
        enc_grad,
        gains_grad,
        rel_table_grad,
        self_qkv_grad,
        cross_grad[:, 3 * INNER + D :],
        cross_query_gradient,
        cross_grad[:, : 2 * INNER],
        cross_grad[:, 3 * INNER : 3 * INNER + D],
        ff_in_grad,
        ff_out_grad,
    )


def solution(mesh):
    tokens = P(("rep", "shard"), None)
    ids = P(("rep", "shard"))
    rows = P("shard", None)
    columns = P(None, "shard")
    in_specs = (tokens, tokens, ids, ids, tokens, columns) + (rows,) * 8
    out_specs = (tokens, tokens, tokens, columns) + (rows,) * 8
    sizes = (mesh.shape["shard"], mesh.shape["rep"])
    return jax.shard_map(
        partial(local, sizes), mesh=mesh, in_specs=in_specs, out_specs=out_specs, check_vma=False
    )
```

```python
from functools import partial
import math

import jax
import jax.numpy as jnp
import numpy as np
from jax import lax
from jax.experimental import pallas as pl
from jax.experimental.pallas import tpu as pltpu
from jax.sharding import PartitionSpec as P

HEADS = 12
HEAD_DIM = 64
FF = 2048
NUM_BUCKETS = 32
SEQ = 512
D = 768
INNER = HEADS * HEAD_DIM
PAIRS = HEADS // 2
LANES = 128
SPAN = SEQ + LANES
GROUP = 3
WIDE = GROUP * LANES
FF_BLOCK = 512
ROWS = 256

eps = 1e-06
masked_score = -1e30
bf16 = jnp.bfloat16
f32 = jnp.float32
VMEM_LIMIT = 56 * 1024 * 1024
LIGHT = pl.CostEstimate(flops=1000000, bytes_accessed=100000, transcendentals=0)

bucket_edges = np.array(
    list(range(1, 16)) + [int(math.ceil(16.0 * 8.0 ** ((b - 16) / 16.0))) for b in range(16, 32)],
    dtype=np.int32,
)

SELF_RANGES = ((0, 128), (0, 256), (0, 384), (128, 512))
CROSS_RANGES = ((0, 384), (0, 512), (0, 512), (128, 512))


def dot_nn(a, b):
    return lax.dot_general(a, b, (((1,), (0,)), ((), ())), preferred_element_type=f32)


def dot_nt(a, b):
    return lax.dot_general(a, b, (((1,), (1,)), ((), ())), preferred_element_type=f32)


def dot_tn(a, b):
    return lax.dot_general(a, b, (((0,), (0,)), ((), ())), preferred_element_type=f32)


def half_masks():
    lane = lax.broadcasted_iota(jnp.int32, (1, LANES), 1)
    low = (lane < HEAD_DIM).astype(f32)
    return low.astype(bf16), (1.0 - low).astype(bf16)


def pieces(value):
    lane = lax.broadcasted_iota(jnp.int32, value.shape, 1) % HEAD_DIM
    high = value.astype(bf16).astype(f32)
    rest = value - high
    middle = rest.astype(bf16).astype(f32)
    last = rest - middle
    return jnp.where(
        lane == 2, high, jnp.where(lane == 3, middle, jnp.where(lane == 4, last, 0.0))
    )


def stacked(block, low, high):
    return jnp.concatenate([block * low, block * high], axis=0)


def toeplitz(row):
    wide = jnp.broadcast_to(row, (LANES, SPAN))
    return pltpu.roll(wide, 0, 1, stride=1, stride_axis=0)[:, :SEQ]


def by_pair(kernel, kinds, waits, *refs):
    for pair in range(GROUP):
        lanes = slice(pair * LANES, (pair + 1) * LANES)
        views = []
        for kind, ref in zip(kinds, refs[waits:]):
            if kind == "L":
                ref = ref.at[:, lanes]
            elif kind == "T":
                ref = ref.at[:, :, lanes]
            elif kind == "G":
                ref = ref.at[pair : pair + 1]
            elif kind == "X":
                ref = ref.at[pair]
            views.append(ref)
        kernel(*views)


def attend_forward_kernel(ranges, biased, *refs):
    if biased:
        q_ref, k_ref, v_ref, qa_ref, ka_ref, g_ref, o_ref, l_ref, slab = refs

        @pl.when(pl.program_id(1) == 0)
        def _():
            slab[0:LANES] = toeplitz(g_ref[0, 0:1, :])
            slab[LANES : 2 * LANES] = toeplitz(g_ref[0, 1:2, :])
    else:
        q_ref, k_ref, v_ref, qa_ref, ka_ref, o_ref, l_ref = refs
    low, high = half_masks()
    keys = jnp.concatenate([k_ref[...], ka_ref[...]], axis=1)
    values = jnp.concatenate([v_ref[...], jnp.ones((SEQ, LANES), bf16)], axis=1)
    lane = lax.broadcasted_iota(jnp.int32, (LANES, LANES), 1)
    blocks = [
        (slice(i * LANES, (i + 1) * LANES), slice(start, stop), slice(SEQ - (stop - start), SEQ))
        for i, (start, stop) in enumerate(ranges)
    ]
    scores = []
    for rows, seen, columns in blocks:
        extra = qa_ref[rows, :]
        left = jnp.concatenate(
            [stacked(q_ref[rows, :], low, high), jnp.concatenate([extra, extra], axis=0)], axis=1
        )
        score = dot_nt(left, keys[seen])
        scores.append(score + slab[:, columns] if biased else score)
    tops = [jnp.max(score, axis=1, keepdims=True) for score in scores]
    expds = [jnp.exp(score - top).astype(bf16) for score, top in zip(scores, tops)]
    mixes = [dot_nn(expd, values[seen]) for expd, (_, seen, _) in zip(expds, blocks)]
    outs = []
    for mixed, top in zip(mixes, tops):
        total = mixed[:, LANES:]
        mixed = mixed[:, :LANES] / total
        negative = pieces(-(top + jnp.log(total)))
        outs.append(
            (
                jnp.where(lane < HEAD_DIM, mixed[:LANES], mixed[LANES:]).astype(bf16),
                jnp.where(lane < HEAD_DIM, negative[:LANES], negative[LANES:]).astype(bf16),
            )
        )
    for (rows, _, _), (out, lows) in zip(blocks, outs):
        o_ref[rows, :] = out
        l_ref[rows, :] = lows


def attend_forward(q, q_at, k, k_at, v, v_at, q_extra, k_extra, g, ranges, after=()):
    tokens = q.shape[0]
    sequences = tokens // SEQ
    biased = g is not None

    def block(at):
        return pl.BlockSpec((SEQ, WIDE), lambda p, s: (s, at // GROUP + p))

    shared = pl.BlockSpec((SEQ, LANES), lambda p, s: (s, 0))
    in_specs = [block(q_at), block(k_at), block(v_at), shared, shared]
    args = [q, k, v, q_extra, k_extra]
    scratch = []
    if biased:
        in_specs.append(pl.BlockSpec((GROUP, 2, SPAN), lambda p, s: (p, 0, 0)))
        args.append(g)
        scratch.append(pltpu.VMEM((GROUP, 2 * LANES, SEQ), f32))
    seen = sum(stop - start for start, stop in ranges)
    return pl.pallas_call(
        partial(
            by_pair,
            partial(attend_forward_kernel, ranges, biased),
            "LLLSSGLLX" if biased else "LLLSSLL",
            len(after),
        ),
        grid=(PAIRS // GROUP, sequences),
        in_specs=[pl.BlockSpec(memory_space=pl.ANY)] * len(after) + in_specs,
        out_specs=[block(0), block(0)],
        out_shape=[jax.ShapeDtypeStruct((tokens, INNER), bf16)] * 2,
        scratch_shapes=scratch,
        compiler_params=pltpu.CompilerParams(vmem_limit_bytes=VMEM_LIMIT),
        cost_estimate=LIGHT,
    )(*after, *args)


def attend_backward_kernel(ranges, biased, *refs):
    if biased:
        (q_ref, k_ref, v_ref, qa_ref, ka_ref, l_ref, o_ref, d_ref, g_ref) = refs[:9]
        out_ref, rel_ref, dk, dv, slab, dslab = refs[9:]

        @pl.when(pl.program_id(1) == 0)
        def _():
            slab[:, 0:LANES] = toeplitz(g_ref[0, 0:1, :]).T
            slab[:, LANES : 2 * LANES] = toeplitz(g_ref[0, 1:2, :]).T
            dslab[...] = jnp.zeros_like(dslab)
    else:
        (q_ref, k_ref, v_ref, qa_ref, ka_ref, l_ref, o_ref, d_ref) = refs[:8]
        dq_ref, out_ref, dk, dv = refs[8:]
    low, high = half_masks()
    low_lane = lax.broadcasted_iota(jnp.int32, (LANES, LANES), 1) < HEAD_DIM
    low_row = lax.broadcasted_iota(jnp.int32, (LANES, LANES), 0) < HEAD_DIM
    keys = jnp.concatenate([k_ref[...], ka_ref[...]], axis=1)
    values = jnp.concatenate([v_ref[...], ka_ref[...]], axis=1)
    keys_t = k_ref[...].T
    blocks = [
        (slice(i * LANES, (i + 1) * LANES), slice(start, stop), slice(SEQ - (stop - start), SEQ))
        for i, (start, stop) in enumerate(ranges)
    ]
    rights = []
    for rows, _, _ in blocks:
        q2 = stacked(q_ref[rows, :], low, high)
        extra = qa_ref[rows, :]
        totals = l_ref[rows, :]
        q_right = jnp.concatenate(
            [q2, jnp.concatenate([extra + totals * low, extra + totals * high], axis=0)], axis=1
        )
        grad = d_ref[rows, :]
        d2 = stacked(grad, low, high)
        product = grad.astype(f32) * o_ref[rows, :].astype(f32)
        sum_low = jnp.sum(jnp.where(low_lane, product, 0.0), axis=1, keepdims=True)
        sum_high = jnp.sum(jnp.where(low_lane, 0.0, product), axis=1, keepdims=True)
        delta = pieces(
            -jnp.concatenate(
                [
                    jnp.broadcast_to(sum_low, (LANES, LANES)),
                    jnp.broadcast_to(sum_high, (LANES, LANES)),
                ],
                axis=0,
            )
        ).astype(bf16)
        lows = jnp.concatenate([delta[:LANES] * low, delta[LANES:] * high], axis=0)
        rights.append((q2, q_right, d2, jnp.concatenate([d2, lows], axis=1)))
    scores = [
        dot_nt(keys[seen], q_right) for (_, seen, _), (_, q_right, _, _) in zip(blocks, rights)
    ]
    if biased:
        scores = [score + slab[columns, :] for (_, _, columns), score in zip(blocks, scores)]
    grads = [
        dot_nt(values[seen], d_right) for (_, seen, _), (_, _, _, d_right) in zip(blocks, rights)
    ]
    probs = [jnp.exp(score) for score in scores]
    grads = [prob * grad for prob, grad in zip(probs, grads)]
    probs = [prob.astype(bf16) for prob in probs]
    grads16 = [grad.astype(bf16) for grad in grads]
    dvs = [dot_nn(prob, right[2]) for prob, right in zip(probs, rights)]
    dks = [dot_nn(grad, right[0]) for grad, right in zip(grads16, rights)]
    dqs = [dot_nn(keys_t[:, seen], grad) for (_, seen, _), grad in zip(blocks, grads16)]
    dk[...] = jnp.zeros_like(dk)
    dv[...] = jnp.zeros_like(dv)
    for (_, seen, _), dv_here, dk_here in zip(blocks, dvs, dks):
        dv[seen, :] += dv_here
        dk[seen, :] += dk_here
    for (rows, _, columns), dq, grad in zip(blocks, dqs, grads):
        dq = jnp.where(low_row, dq[:, :LANES], dq[:, LANES:]).T.astype(bf16)
        if biased:
            out_ref[0, rows, :] = dq
            dslab[columns, :] += grad
        else:
            dq_ref[rows, :] = dq
    first = 1 if biased else 0
    out_ref[first] = dk[...].astype(bf16)
    out_ref[first + 1] = dv[...].astype(bf16)
    if biased:

        @pl.when(pl.program_id(1) == pl.num_programs(1) - 1)
        def _():
            for head in range(2):
                square = dslab[:, head * LANES : (head + 1) * LANES].T
                wide = jnp.concatenate([square, jnp.zeros((LANES, LANES), f32)], axis=1)
                half = LANES // 2
                while half >= 1:
                    wide = wide[:half] + pltpu.roll(wide[half:], SPAN - half, 1)
                    half //= 2
                rel_ref[0, head : head + 1, :] = wide


def attend_backward(q, q_at, k, k_at, v, v_at, q_extra, k_extra, lows, mixed, grad, g, ranges, after=(),
                    first=0, pairs=PAIRS, into=None):
    tokens = q.shape[0]
    sequences = tokens // SEQ
    biased = g is not None

    def block(at):
        return pl.BlockSpec((SEQ, WIDE), lambda p, s: (s, (at + first) // GROUP + p))

    shared = pl.BlockSpec((SEQ, LANES), lambda p, s: (s, 0))
    in_specs = [block(q_at), block(k_at), block(v_at), shared, shared, block(0), block(0), block(0)]
    args = [q, k, v, q_extra, k_extra, lows, mixed, grad]
    scratch = [pltpu.VMEM((GROUP, SEQ, LANES), f32)] * 2
    if biased:
        in_specs.append(pl.BlockSpec((GROUP, 2, SPAN), lambda p, s: (first // GROUP + p, 0, 0)))
        args.append(g)
        scratch += [pltpu.VMEM((GROUP, SEQ, 2 * LANES), f32)] * 2
        out_specs = [
            pl.BlockSpec((3, SEQ, WIDE), lambda p, s: (0, s, first // GROUP + p)),
            pl.BlockSpec((GROUP, 2, SPAN), lambda p, s: (p, 0, 0)),
        ]
        out_shape = [
            jax.ShapeDtypeStruct((3, tokens, INNER), bf16),
            jax.ShapeDtypeStruct((pairs, 2, SPAN), f32),
        ]
    else:
        out_specs = [block(0), pl.BlockSpec((2, SEQ, WIDE), lambda p, s: (0, s, p))]
        out_shape = [
            jax.ShapeDtypeStruct((tokens, INNER), bf16),
            jax.ShapeDtypeStruct((2, tokens, INNER), bf16),
        ]
    aliases = {}
    if into is not None:
        after = [into, *after]
        aliases = {0: 0}
    return pl.pallas_call(
        partial(
            by_pair,
            partial(attend_backward_kernel, ranges, biased),
            "LLLSSLLLGTGXXXX" if biased else "LLLSSLLLLTXX",
            len(after),
        ),
        grid=(pairs // GROUP, sequences),
        in_specs=[pl.BlockSpec(memory_space=pl.ANY)] * len(after) + in_specs,
        out_specs=out_specs,
        out_shape=out_shape,
        scratch_shapes=scratch,
        input_output_aliases=aliases,
        compiler_params=pltpu.CompilerParams(vmem_limit_bytes=VMEM_LIMIT),
        cost_estimate=LIGHT,
    )(*after, *args)


def shares(core, value, keep_ref, send_ref, *at):
    rows, cols = value.shape
    parts = value.astype(bf16).reshape(2, 2, rows // 4, cols)
    for y in range(2):
        place = (y,) + at
        keep_ref[place] = jnp.where(core == 0, parts[y, 0], parts[y, 1])
        send_ref[place] = jnp.where(core == 0, parts[y, 1], parts[y, 0])


def place_pieces(where_ref, full, own, core, y, x, yc, xc):
    shard = where_ref[0]
    rows, cols = own.shape
    half = cols // 2

    def at(index):
        return pl.ds(pl.multiple_of(index * rows, rows), rows)

    full[at(shard), :] = own[...]
    full[at(shard ^ 1), :] = core[...]
    for bit in range(2):

        @pl.when(where_ref[1] == bit)
        def _():
            mine = slice(bit * half, (bit + 1) * half)
            other = slice((1 - bit) * half, (2 - bit) * half)
            full[at(shard ^ 2), mine] = y[...]
            full[at(shard ^ 2), other] = x[...]
            full[at(shard ^ 3), mine] = yc[...]
            full[at(shard ^ 3), other] = xc[...]


def whole_spec(array):
    return pl.BlockSpec(
        array.shape, lambda i, c: (0,) * array.ndim, pipeline_mode=pl.Buffered(1)
    )


def normed_rows(x, gain):
    factor = lax.rsqrt(jnp.mean(x * x, -1, keepdims=True) + eps)
    return (x * factor * gain).astype(bf16)


def first_kernel(where_ref, x_ref, onehot_ref, valid_ref, *refs):
    pieces_in = refs[:6]
    full, gains_ref, g_ref, n_ref, qkv_ref = refs[6:]

    @pl.when(pl.program_id(0) == 0)
    def _():
        place_pieces(where_ref, full, *pieces_in)
        small = full[:, 3 * INNER : 3 * INNER + LANES].astype(f32).T
        gains_ref[...] = small[0:8]
        table = small[16:32].astype(bf16)
        bias = jnp.where(valid_ref[...] > 0, dot_nn(table, onehot_ref[...]), masked_score)
        for pair in range(PAIRS):
            g_ref[pair] = bias[2 * pair : 2 * pair + 2]

    normed = normed_rows(x_ref[...].astype(f32), gains_ref[0:1, :])
    n_ref[...] = normed
    for part in range(3):
        columns = slice(part * D, (part + 1) * D)
        qkv_ref[:, columns] = dot_nn(normed, full[:, columns]).astype(bf16)


def first_step(where, x, pieces_in, onehot, valid):
    tokens = x.shape[0]
    width = pieces_in[0].shape[1]
    block = pl.BlockSpec((ROWS, D), lambda i, c: (i, 0))
    return pl.pallas_call(
        first_kernel,
        grid_spec=pltpu.PrefetchScalarGridSpec(
            num_scalar_prefetch=1,
            grid=(tokens // ROWS,),
            in_specs=[block, whole_spec(onehot), whole_spec(valid)]
            + [whole_spec(p) for p in pieces_in],
            out_specs=[
                pl.BlockSpec((D, width), lambda i, c: (0, 0)),
                pl.BlockSpec((8, D), lambda i, c: (0, 0)),
                pl.BlockSpec((PAIRS, 2, SPAN), lambda i, c: (0, 0, 0)),
                block,
                pl.BlockSpec((ROWS, 3 * INNER), lambda i, c: (i, 0)),
            ],
        ),
        out_shape=[
            jax.ShapeDtypeStruct((D, width), bf16),
            jax.ShapeDtypeStruct((8, D), f32),
            jax.ShapeDtypeStruct((PAIRS, 2, SPAN), f32),
            jax.ShapeDtypeStruct((tokens, D), bf16),
            jax.ShapeDtypeStruct((tokens, 3 * INNER), bf16),
        ],
        compiler_params=pltpu.CompilerParams(vmem_limit_bytes=VMEM_LIMIT),
        cost_estimate=LIGHT,
    )(where, x, onehot, valid, *pieces_in)


def encoder_kernel(waits, where_ref, *refs):
    refs = refs[waits:]
    x_ref, pieces_in = refs[0], refs[1:7]
    full, kv_ref = refs[7:]

    @pl.when(pl.program_id(0) == 0)
    def _():
        place_pieces(where_ref, full, *pieces_in)

    for part in range(2):
        columns = slice(part * D, (part + 1) * D)
        kv_ref[:, columns] = dot_nn(x_ref[...], full[:, columns]).astype(bf16)


def encoder_step(where, x, pieces_in, after):
    tokens = x.shape[0]
    width = pieces_in[0].shape[1]
    return pl.pallas_call(
        partial(encoder_kernel, len(after)),
        grid_spec=pltpu.PrefetchScalarGridSpec(
            num_scalar_prefetch=1,
            grid=(tokens // ROWS,),
            in_specs=[pl.BlockSpec(memory_space=pl.ANY)] * len(after)
            + [pl.BlockSpec((ROWS, D), lambda i, c: (i, 0))]
            + [whole_spec(p) for p in pieces_in],
            out_specs=[
                pl.BlockSpec((D, width), lambda i, c: (0, 0)),
                pl.BlockSpec((ROWS, 2 * INNER), lambda i, c: (i, 0)),
            ],
        ),
        out_shape=[
            jax.ShapeDtypeStruct((D, width), bf16),
            jax.ShapeDtypeStruct((tokens, 2 * INNER), bf16),
        ],
        compiler_params=pltpu.CompilerParams(vmem_limit_bytes=VMEM_LIMIT),
        cost_estimate=LIGHT,
    )(where, *after, x, *pieces_in)


def middle_kernel(x_ref, attn_ref, out_w_ref, gain_ref, q_w_ref, first_ref, n_ref, cq_ref):
    first = x_ref[...].astype(f32) + dot_nn(attn_ref[...], out_w_ref[...])
    first_ref[...] = first
    normed = normed_rows(first, gain_ref[...])
    n_ref[...] = normed
    cq_ref[...] = dot_nn(normed, q_w_ref[...]).astype(bf16)


def middle_step(x, attn, gain, w_cross):
    tokens = x.shape[0]
    block = pl.BlockSpec((ROWS, D), lambda i: (i, 0))
    return pl.pallas_call(
        middle_kernel,
        grid=(tokens // ROWS,),
        in_specs=[
            block,
            block,
            pl.BlockSpec((D, D), lambda i: (0, 4)),
            pl.BlockSpec((1, D), lambda i: (0, 0)),
            pl.BlockSpec((D, D), lambda i: (0, 2)),
        ],
        out_specs=[block] * 3,
        out_shape=[
            jax.ShapeDtypeStruct((tokens, D), f32),
            jax.ShapeDtypeStruct((tokens, D), bf16),
            jax.ShapeDtypeStruct((tokens, D), bf16),
        ],
        compiler_params=pltpu.CompilerParams(vmem_limit_bytes=VMEM_LIMIT),
        cost_estimate=LIGHT,
    )(x, attn, w_cross, gain, w_cross)


def shares(core, value, keep_ref, send_ref, *at, start=0):
    rows, cols = value.shape
    parts = value.astype(bf16).reshape(2, 2, rows // 4, cols)
    columns = slice(start, start + cols)
    for y in range(2):
        place = (y,) + at + (slice(None), columns)
        keep_ref[place] = jnp.where(core == 0, parts[y, 0], parts[y, 1])
        send_ref[place] = jnp.where(core == 0, parts[y, 1], parts[y, 0])


def feed_forward_kernel(
    where_ref, x1_ref, attn_ref, w2_ref, gain_ref, dout_ref,
    own_g, own_u, core_g, core_u, y_in, x_in, yc_in, xc_in,
    own_o, core_o, y_o, x_o, yc_o, xc_o,
    layer_ref, gx_ref, gx16_ref, gk_ref, gs_ref, ok_ref, os_ref,
    wg, wu, wo, n3, n3t, acc, dn, hid, dgate, dup,
):
    step = pl.program_id(0)
    shard, across = where_ref[0], where_ref[1]
    tokens = x1_ref.shape[0]
    chunks = tokens // ROWS
    rows_in = own_g.shape[0]

    def at(index):
        return pl.ds(pl.multiple_of(index * rows_in, rows_in), rows_in)

    wg[at(shard), :] = own_g[...]
    wu[at(shard), :] = own_u[...]
    wg[at(shard ^ 1), :] = core_g[...]
    wu[at(shard ^ 1), :] = core_u[...]

    @pl.when(across == 0)
    def _():
        wg[at(shard ^ 2), :] = y_in[...]
        wu[at(shard ^ 2), :] = x_in[...]
        wg[at(shard ^ 3), :] = yc_in[...]
        wu[at(shard ^ 3), :] = xc_in[...]

    @pl.when(across == 1)
    def _():
        wg[at(shard ^ 2), :] = x_in[...]
        wu[at(shard ^ 2), :] = y_in[...]
        wg[at(shard ^ 3), :] = xc_in[...]
        wu[at(shard ^ 3), :] = yc_in[...]

    half = D // 2
    for turn, whole in ((0, own_o), (1, core_o)):

        @pl.when(step == turn)
        def _():
            wo[...] = whole[...]

    for turn, near, far in ((2, y_o, x_o), (3, yc_o, xc_o)):
        for bit in range(2):

            @pl.when((step == turn) & (across == bit))
            def _():
                wo[:, bit * half : (bit + 1) * half] = near[...]
                wo[:, (1 - bit) * half : (2 - bit) * half] = far[...]

    @pl.when(step == 0)
    def _():
        gain = gain_ref[...]
        for chunk in range(chunks):
            rows = slice(chunk * ROWS, (chunk + 1) * ROWS)
            x = x1_ref[rows, :] + dot_nn(attn_ref[rows, :], w2_ref[...])
            gx_ref[rows, :] = x
            normed = normed_rows(x, gain)
            n3[rows, :] = normed
            n3t[:, rows] = normed.T
            acc[rows, :] = jnp.zeros((ROWS, D), f32)
            dn[rows, :] = jnp.zeros((ROWS, D), f32)

    c = math.sqrt(2.0 / math.pi)
    for chunk in range(chunks):
        rows = slice(chunk * ROWS, (chunk + 1) * ROWS)
        normed = n3[rows, :]
        gate = dot_nn(normed, wg[...])
        up = dot_nn(normed, wu[...])
        dhidden = dot_nt(dout_ref[rows, :], wo[...]).astype(bf16).astype(f32)
        square = gate * gate
        t = jnp.tanh(c * gate * (1.0 + 0.044715 * square))
        mid = 0.5 * (1.0 + t)
        act = gate * mid
        slope = mid + (0.5 * c) * gate * (1.0 - t * t) * (1.0 + (3.0 * 0.044715) * square)
        hid[rows, :] = (act * up).astype(bf16)
        dgate[rows, :] = (dhidden * up * slope).astype(bf16)
        dup[rows, :] = (dhidden * act).astype(bf16)
        acc[rows, :] += dot_nn(hid[rows, :], wo[...])
        dn[rows, :] += dot_nt(dgate[rows, :], wg[...]) + dot_nt(dup[rows, :], wu[...])
    core = shard % 2
    for part, grads in enumerate((dgate, dup)):
        for start in range(0, FF_BLOCK, ROWS):
            value = dot_nn(n3t[...], grads[:, start : start + ROWS])
            shares(core, value, gk_ref, gs_ref, part, start=start)
    out_grad = dot_tn(hid[...], dout_ref[...]).astype(bf16)

    @pl.when(step % 2 == 0)
    def _():
        ok_ref[0] = out_grad

    @pl.when(step % 2 == 1)
    def _():
        os_ref[0] = out_grad

    @pl.when(step == pl.num_programs(0) - 1)
    def _():
        gain = gain_ref[...]
        for chunk in range(chunks):
            rows = slice(chunk * ROWS, (chunk + 1) * ROWS)
            x = gx_ref[rows, :]
            layer_ref[rows, :] = (x + acc[rows, :]).astype(bf16)
            factor = lax.rsqrt(jnp.mean(x * x, -1, keepdims=True) + eps)
            d = dn[rows, :]
            weighted = d * gain
            back = factor * weighted - x * (
                factor * factor * factor * jnp.mean(weighted * x, -1, keepdims=True)
            )
            gx = dout_ref[rows, :].astype(f32) + back
            gx_ref[rows, :] = gx
            gx16_ref[rows, :] = gx.astype(bf16)


def feed_forward(where, x1, attn, w_cross, gain, dout, in_pieces, out_pieces):
    tokens = x1.shape[0]
    steps = FF // FF_BLOCK
    one = pl.Buffered(1)
    rows_in = in_pieces[0].shape[0]

    def whole(width=D):
        return pl.BlockSpec((tokens, width), lambda f, c: (0, 0), pipeline_mode=one)

    def streamed(at):
        return pl.BlockSpec((rows_in, FF_BLOCK), lambda f, c: (0, at + (c[0] ^ f)))

    resident = pl.BlockSpec((tokens, D), lambda f, c: (0, 0))
    in_share = pl.BlockSpec((2, 2, D // 4, FF_BLOCK), lambda f, c: (0, 0, 0, c[0] ^ f))
    out_share = pl.BlockSpec((1, FF_BLOCK, D), lambda f, c: ((c[0] ^ f) // 2, 0, 0))
    in_type = jax.ShapeDtypeStruct((2, 2, D // 4, FF), bf16)
    out_type = jax.ShapeDtypeStruct((2, FF_BLOCK, D), bf16)
    own_i, core_i, *halves_i = in_pieces
    return pl.pallas_call(
        feed_forward_kernel,
        grid_spec=pltpu.PrefetchScalarGridSpec(
            num_scalar_prefetch=1,
            grid=(steps,),
            in_specs=[
                whole(),
                whole(),
                pl.BlockSpec((D, D), lambda f, c: (0, 3), pipeline_mode=one),
                pl.BlockSpec((1, D), lambda f, c: (0, 0)),
                whole(),
                streamed(0), streamed(steps), streamed(0), streamed(steps),
                streamed(0), streamed(0), streamed(0), streamed(0),
            ]
            + [whole_spec(p) for p in out_pieces],
            out_specs=[resident, resident, resident, in_share, in_share, out_share, out_share],
            scratch_shapes=[
                pltpu.VMEM((D, FF_BLOCK), bf16),
                pltpu.VMEM((D, FF_BLOCK), bf16),
                pltpu.VMEM((FF_BLOCK, D), bf16),
                pltpu.VMEM((tokens, D), bf16),
                pltpu.VMEM((D, tokens), bf16),
                pltpu.VMEM((tokens, D), f32),
                pltpu.VMEM((tokens, D), f32),
                pltpu.VMEM((tokens, FF_BLOCK), bf16),
                pltpu.VMEM((tokens, FF_BLOCK), bf16),
                pltpu.VMEM((tokens, FF_BLOCK), bf16),
            ],
        ),
        out_shape=[
            jax.ShapeDtypeStruct((tokens, D), bf16),
            jax.ShapeDtypeStruct((tokens, D), f32),
            jax.ShapeDtypeStruct((tokens, D), bf16),
            in_type, in_type, out_type, out_type,
        ],
        compiler_params=pltpu.CompilerParams(vmem_limit_bytes=VMEM_LIMIT),
        cost_estimate=LIGHT,
    )(where, x1, attn, w_cross, gain, dout, own_i, own_i, core_i, core_i, *halves_i, *out_pieces)


def weight_grad_kernel(counts, firsts, waits, core_ref, *refs):
    refs = refs[waits:]
    terms = len(counts)
    lefts, rights = refs[0:terms], refs[terms : 2 * terms]
    refs = refs[2 * terms :]
    second = firsts is not None
    if second:
        tiny_ref, keep_ref, send_ref, keep2_ref, send2_ref = refs
    else:
        keep_ref, send_ref = refs
    step = pl.program_id(0)
    core = core_ref[0] % 2
    at = 0
    for left, right, count in zip(lefts, rights, counts):

        def product(keep, send):
            for start in range(0, D, ROWS):
                columns = slice(start, start + ROWS)
                block = right[:, columns] if len(right.shape) == 2 else right[0, :, columns]
                shares(core, dot_tn(left[...], block), keep, send, start=start)

        @pl.when((step >= at) & (step < (firsts if second else at + count)))
        def _():
            product(keep_ref, send_ref)

        if second:

            @pl.when(step >= firsts)
            def _():
                product(keep2_ref, send2_ref)
                tiny = tiny_ref[...]
                for y in range(2):
                    keep2_ref[y, :, D:] = jnp.where(core == 0, tiny[y, 0], tiny[y, 1])
                    send2_ref[y, :, D:] = jnp.where(core == 0, tiny[y, 1], tiny[y, 0])

        at += count


def weight_grad(where, terms, tiny=None, after=()):
    tokens = terms[0][0].shape[0]
    counts = []
    rights = []
    at = 0
    for _, right in terms:
        deep = right.ndim == 3
        count = right.shape[0] if deep else 1

        def place(j, c, at=at, count=count, deep=deep):
            return (jnp.clip(j - at, 0, count - 1), 0, 0) if deep else (0, 0)

        rights.append(pl.BlockSpec((1, tokens, D) if deep else (tokens, D), place))
        counts.append(count)
        at += count
    firsts = None if tiny is None else at - 1
    blocks = at if tiny is None else at - 1
    share = pl.BlockSpec((2, D // 4, D), lambda j, c: (0, 0, jnp.minimum(j, blocks - 1)))
    out_specs = [share, share]
    out_shape = [jax.ShapeDtypeStruct((2, D // 4, blocks * D), bf16)] * 2
    extra_specs, extra = [], []
    if tiny is not None:
        extra_specs, extra = [pl.BlockSpec(tiny.shape, lambda j, c: (0, 0, 0, 0))], [tiny]
        wide = D + tiny.shape[-1]
        out_specs += [pl.BlockSpec((2, D // 4, wide), lambda j, c: (0, 0, 0))] * 2
        out_shape += [jax.ShapeDtypeStruct((2, D // 4, wide), bf16)] * 2
    return pl.pallas_call(
        partial(weight_grad_kernel, counts, firsts, len(after)),
        grid_spec=pltpu.PrefetchScalarGridSpec(
            num_scalar_prefetch=1,
            grid=(at,),
            in_specs=[pl.BlockSpec(memory_space=pl.ANY)] * len(after)
            + [pl.BlockSpec((tokens, D), lambda j, c: (0, 0))] * len(terms)
            + rights
            + extra_specs,
            out_specs=out_specs,
        ),
        out_shape=out_shape,
        compiler_params=pltpu.CompilerParams(vmem_limit_bytes=VMEM_LIMIT),
        cost_estimate=LIGHT,
    )(where, *after, *[left for left, _ in terms], *[right for _, right in terms], *extra)


def norm_back_kernel(normed, onward, waits, *refs):
    refs = refs[waits:]
    grad_ref, w_ref = refs[:2]
    total = None
    for part in range(grad_ref.shape[0]):
        term = dot_nt(grad_ref[part], w_ref[:, part * D : (part + 1) * D])
        total = term if total is None else total + term
    if not normed:
        refs[2][...] = total.astype(refs[2].dtype)
        return
    x_ref, gain_ref, up_ref = refs[2:5]
    refs = refs[5:]
    if onward:
        next_ref, out_ref, gain_grad_ref, out16_ref, onward_ref = refs
    else:
        out_ref, gain_grad_ref = refs
    x = x_ref[...].astype(f32)
    factor = lax.rsqrt(jnp.mean(x * x, -1, keepdims=True) + eps)
    weighted = total * gain_ref[...]
    grad_gain = jnp.sum(total * x * factor, axis=0, keepdims=True)

    @pl.when(pl.program_id(0) == 0)
    def _():
        gain_grad_ref[...] = jnp.zeros_like(gain_grad_ref)

    gain_grad_ref[...] += grad_gain
    scale = factor * factor * factor * jnp.mean(weighted * x, -1, keepdims=True)
    out = up_ref[...] + factor * weighted - x * scale
    out_ref[...] = out
    if onward:
        out16 = out.astype(bf16)
        out16_ref[...] = out16
        onward_ref[...] = dot_nt(out16, next_ref[...]).astype(bf16)


def norm_back(
    grads, w, w_at, x=None, gain=None, upstream=None, w_next=None, next_at=0, after=(), kind=f32
):
    if grads.ndim == 2:
        grads = grads[None]
    parts, tokens, _ = grads.shape
    block = pl.BlockSpec((ROWS, D), lambda i: (i, 0))
    row = pl.BlockSpec((1, D), lambda i: (0, 0))
    in_specs = [pl.BlockSpec(memory_space=pl.ANY)] * len(after)
    in_specs += [
        pl.BlockSpec((parts, ROWS, D), lambda i: (0, i, 0)),
        pl.BlockSpec((D, parts * D), lambda i: (0, w_at)),
    ]
    args = [*after, grads, w]
    wide = jax.ShapeDtypeStruct((tokens, D), kind)
    half = jax.ShapeDtypeStruct((tokens, D), bf16)
    out_specs, out_shape = [block], [wide]
    if x is not None:
        in_specs += [block, row, block]
        args += [x, gain, upstream]
        out_specs.append(row)
        out_shape.append(jax.ShapeDtypeStruct((1, D), f32))
        if w_next is not None:
            in_specs.append(pl.BlockSpec((D, D), lambda i: (0, next_at)))
            args.append(w_next)
            out_specs += [block, block]
            out_shape += [half, half]
    return pl.pallas_call(
        partial(norm_back_kernel, x is not None, w_next is not None, len(after)),
        grid=(tokens // ROWS,),
        in_specs=in_specs,
        out_specs=out_specs,
        out_shape=out_shape,
        compiler_params=pltpu.CompilerParams(vmem_limit_bytes=VMEM_LIMIT),
        cost_estimate=LIGHT,
    )(*args)


def exchange(array, axis, size, bit):
    return lax.ppermute(array, axis, [(i, i ^ bit) for i in range(size)])


def part_of(array, dim, index):
    half = array.shape[dim] // 2
    return lax.dynamic_slice_in_dim(array, index * half, half, dim)


def tie(value, *others):
    return lax.optimization_barrier((value, *others))[0]


def meet(done, *moves):
    *gots, done = lax.optimization_barrier((*[m.got for m in moves], done))
    for move, got in zip(moves, gots):
        move.got = got
    return done


class Gather:
    def __init__(self, own, sizes, *after):
        self.sizes = sizes
        self.own = own
        half = part_of(own, 1, lax.axis_index("rep") % 2)
        if after:
            half = tie(half, *after)
        self.half = half
        self.got = exchange(half, "shard", sizes[0], 2)

    def cross(self):
        self.y = self.got
        self.got = exchange(self.y, "rep", self.sizes[1], 1)
        self.core = exchange(tie(self.own, self.y), "shard", self.sizes[0], 1)
        self.yc = exchange(self.y, "shard", self.sizes[0], 1)

    def pieces(self):
        self.x = self.got
        xc = exchange(self.x, "shard", self.sizes[0], 1)
        return self.own, self.core, self.y, self.x, self.yc, xc


class Chain:
    def __init__(self, keep, send, sizes, dims, order, turned=False):
        self.shards, self.reps = sizes
        self.bits = [1 << b for b in range(self.reps.bit_length() - 1)]
        self.dims = [dims[min(i, len(dims) - 1)] for i in range(len(self.bits))]
        if turned:
            self.bits[:2] = self.bits[1::-1]
            self.dims[:2] = self.dims[1::-1]
        steps = []
        for name in order:
            if name == "y":
                steps.append(("shard", 2, 0))
            else:
                steps += [("rep", bit, dim) for bit, dim in zip(self.bits, self.dims)]
        self.steps = steps
        self.kept = keep
        self.got = exchange(send, "shard", self.shards, 1)
        self.sent = send
        self.at = 0

    def own(self):
        while self.at < len(self.steps):
            self.advance()
        return (self.kept.astype(f32) + self.got.astype(f32)).astype(bf16)

    def advance(self):
        axis, bit, dim = self.steps[self.at]
        self.at += 1
        mine = (lax.axis_index(axis) // bit) % 2
        size = self.shards if axis == "shard" else self.reps
        def half(index):
            kept, got = (part_of(part, dim, index).astype(f32) for part in (self.kept, self.got))
            return lax.optimization_barrier((kept + got).astype(bf16))

        self.sent = half(1 - mine)
        self.kept = half(mine)
        self.got = exchange(self.sent, axis, size, bit)
        return self.got


class Spread:
    def __init__(self, own, sizes, bits, dims):
        self.own = own
        self.reps = sizes[1]
        self.left = list(zip(bits, dims))
        self.got = None
        self.advance()

    def pair(self):
        bit, _ = self.now
        mine = (lax.axis_index("rep") // bit) % 2
        low = jnp.where(mine == 0, self.own, self.got)
        high = jnp.where(mine == 0, self.got, self.own)
        return low, high

    def advance(self):
        if self.got is not None:
            self.own = jnp.concatenate(self.pair(), axis=self.now[1])
        self.now = self.left.pop()
        self.got = exchange(self.own, "rep", self.reps, self.now[0])


def together(*moves):
    gots = lax.optimization_barrier(tuple(m.got for m in moves))
    for move, got in zip(moves, gots):
        move.got = got


def unpack_kernel(where_ref, own_ref, got_ref, w_ref, in_ref, out_ref, sum_ref):
    mine = where_ref[2]
    half, _, rows, cols = own_ref.shape
    out_rows = out_ref.shape[0] // (2 * half)
    total = jnp.zeros((rows, LANES), f32)
    for blocks_ref, bit in ((own_ref, mine), (got_ref, 1 - mine)):
        for block in range(half):
            at = block // 2 * 4 + bit * 2 + block % 2
            for part in range(2):
                place = pl.ds(pl.multiple_of(part * FF + at * cols, cols), cols)
                value = blocks_ref[block, part].astype(f32)
                in_ref[:, place] = value
                product = value * w_ref[:, place].astype(f32)
                for lane in range(0, cols, LANES):
                    total = total + product[:, lane : lane + LANES]
            place = pl.ds(pl.multiple_of(at * out_rows, out_rows), out_rows)
            for group in range(D // cols):
                out_ref[place, group * cols : (group + 1) * cols] = blocks_ref[
                    block, 2, group * out_rows : (group + 1) * out_rows, :
                ].astype(f32)
    row = jnp.broadcast_to(jnp.sum(total, axis=1, keepdims=True), (rows, LANES)).T
    sum_ref[...] = row[0:8]


def unpack(where, own, got, w):
    rows = own.shape[2]

    def whole(shape):
        return pl.BlockSpec(shape, lambda i, c: (0,) * len(shape))

    outs = [
        jax.ShapeDtypeStruct((rows, 2 * FF), f32),
        jax.ShapeDtypeStruct((FF * rows // D, D), f32),
        jax.ShapeDtypeStruct((8, rows), f32),
    ]
    return pl.pallas_call(
        unpack_kernel,
        grid_spec=pltpu.PrefetchScalarGridSpec(
            num_scalar_prefetch=1,
            grid=(1,),
            in_specs=[whole(own.shape), whole(got.shape), whole(w.shape)],
            out_specs=[whole(o.shape) for o in outs],
        ),
        out_shape=outs,
        compiler_params=pltpu.CompilerParams(vmem_limit_bytes=VMEM_LIMIT),
        cost_estimate=LIGHT,
    )(where, own, got, w)


def bias_rows(shards):
    lane = np.arange(SPAN)
    distance = np.where(lane < SEQ, SEQ - LANES - lane, 2 * SEQ - lane)
    bucket = np.zeros(SPAN, np.int64)
    for edge in bucket_edges:
        bucket += distance >= edge
    valid = (distance >= 0) & (distance < SEQ)
    onehot = np.zeros((SPAN, NUM_BUCKETS), np.float32)
    onehot[np.arange(SPAN)[valid], bucket[valid]] = 1.0
    own = NUM_BUCKETS // shards
    rows = np.arange(NUM_BUCKETS) // own * (D // shards) + np.arange(NUM_BUCKETS) % own
    placed = np.zeros((D, SPAN), np.float32)
    placed[rows] = onehot.T
    return onehot, placed, valid[None].astype(np.float32)


def local(
    sizes,
    hidden_in,
    enc_states,
    dec_segments,
    enc_segments,
    out_grad,
    gains,
    rel_table,
    self_qkv,
    self_out,
    cross_q,
    cross_kv,
    cross_out,
    ff_in,
    ff_out,
):
    shards, reps = sizes
    own_rows = D // shards
    own_buckets = NUM_BUCKETS // shards
    width = reps.bit_length() - 1
    shard = lax.axis_index("shard")
    rep = lax.axis_index("rep")
    where = jnp.stack([shard, rep % 2, rep // 2 % 2]).astype(jnp.int32)
    small = jnp.concatenate(
        [
            gains.T,
            jnp.zeros((own_rows, 13), bf16),
            jnp.pad(rel_table, ((0, own_rows - own_buckets), (0, 2 * LANES - 16 - HEADS))),
        ],
        axis=1,
    )
    self_set = Gather(jnp.concatenate([self_qkv, small], axis=1), sizes)
    self_set.cross()
    cross_set = Gather(
        jnp.concatenate([cross_kv, cross_q, cross_out, self_out], axis=1), sizes, self_set.y
    )
    self_pieces = self_set.pieces()

    lane = jnp.arange(LANES, dtype=jnp.int32)[None, :]
    dec_ids = dec_segments[:, None]
    enc_ids = enc_segments[:, None]
    ones = ((lane % HEAD_DIM >= 2) & (lane % HEAD_DIM <= 4)).astype(f32)

    def key_extra(ids):
        return jnp.where(lane < 2, jnp.where(lane != ids, masked_score, 0.0), ones).astype(bf16)

    q_extra = ((lane < 2) & (lane == dec_ids)).astype(bf16)
    self_extra = key_extra(dec_ids)
    cross_extra = key_extra(enc_ids)
    onehot, placed, valid = bias_rows(shards)
    w_self, gains_all, g, normed_one, qkv = first_step(
        where, hidden_in, self_pieces, placed.astype(bf16), valid
    )
    meet(normed_one, cross_set)
    cross_set.cross()
    out_set = Gather(ff_out, sizes, cross_set.y)
    in_set = Gather(ff_in, sizes, cross_set.y)
    attn_one, lows_one = attend_forward(
        qkv, 0, qkv, PAIRS, qkv, 2 * PAIRS, q_extra, self_extra, g, SELF_RANGES,
        after=[out_set.half, in_set.half],
    )
    meet(attn_one, cross_set, out_set, in_set)
    cross_pieces = cross_set.pieces()
    out_set.cross()
    in_set.cross()
    w_cross, ckv = encoder_step(where, enc_states, cross_pieces, [attn_one])
    first, normed_two, cq = middle_step(hidden_in, attn_one, gains_all[1:2], w_cross)
    attn_two, lows_two = attend_forward(
        cq, 0, ckv, 0, ckv, PAIRS, q_extra, cross_extra, None, CROSS_RANGES
    )
    meet(attn_two, out_set, in_set)
    ff_out_pieces = out_set.pieces()
    ff_in_pieces = in_set.pieces()
    layer_out, grad_second, out_two, in_keep, in_send, out_keep, out_send = feed_forward(
        where, first, attn_two, w_cross, gains_all[2:3], out_grad, ff_in_pieces, ff_out_pieces
    )
    ff_in_chain = Chain(in_keep, in_send, sizes, [3], "yr")
    ff_out_chain = Chain(out_keep, out_send, sizes, [1], "ry")
    (grad_attn_two,) = norm_back(out_two, w_cross, 3, kind=bf16, after=[layer_out])
    meet(grad_attn_two, ff_in_chain, ff_out_chain)
    ff_out_chain.advance()
    ff_in_chain.advance()
    grad_cq, grad_ckv = attend_backward(
        cq, 0, ckv, 0, ckv, PAIRS, q_extra, cross_extra, lows_two, attn_two, grad_attn_two,
        None, CROSS_RANGES, after=[ff_in_chain.sent, ff_out_chain.sent],
    )
    meet(grad_cq, ff_out_chain)
    ff_out_chain.advance()
    grad_first, _, out_one, grad_attn_one = norm_back(
        grad_cq, w_cross, 2, first, gains_all[1:2], grad_second, w_cross, 4,
        after=[ff_out_chain.sent],
    )
    meet(grad_attn_one, ff_in_chain, ff_out_chain)
    ff_in_chain.advance()
    ff_out_chain.advance()
    cross_keep, cross_send = weight_grad(
        where,
        [(enc_states, grad_ckv), (normed_two, grad_cq), (attn_two, out_two), (attn_one, out_one)],
        after=[ff_in_chain.sent, ff_out_chain.sent],
    )
    cross_send = meet(cross_send, ff_in_chain, ff_out_chain)
    ff_in_chain.advance()
    ff_out_chain.advance()
    cross_chain = Chain(cross_keep, cross_send, sizes, [2, 1], "yr", turned=True)
    (enc_grad,) = norm_back(
        grad_ckv, w_cross, 0, after=[cross_keep, ff_in_chain.sent, ff_out_chain.sent]
    )
    meet(enc_grad, cross_chain, ff_in_chain, ff_out_chain)
    cross_chain.advance()
    ff_in_chain.advance()
    out_own = ff_out_chain.own()[0]
    backward = partial(
        attend_backward, qkv, 0, qkv, PAIRS, qkv, 2 * PAIRS, q_extra, self_extra, lows_one,
        attn_one, grad_attn_one, g, SELF_RANGES, pairs=PAIRS // 2,
    )
    some_qkv, some_rel = backward(after=[cross_chain.sent, ff_in_chain.sent, out_own])
    some_qkv = meet(some_qkv, ff_in_chain)
    in_own = ff_in_chain.own()[0]
    rows, columns = in_own.shape[1:]
    out_rows = out_own.shape[0]
    out_own = out_own.reshape(out_rows, -1, columns).transpose(1, 0, 2).reshape(1, rows, columns)
    bits = [2, 1, 4] if reps == 8 else ff_in_chain.bits
    blocks = Spread(
        jnp.concatenate([in_own, out_own], axis=0)[None], sizes, bits, [0] * len(bits)
    )
    grad_qkv, more_rel = backward(after=[blocks.own], first=PAIRS // 2, into=some_qkv)
    rel_part = jnp.concatenate([some_rel, more_rel], axis=0)
    grad_qkv = meet(grad_qkv, cross_chain, blocks)
    cross_chain.advance()
    blocks.advance()
    table_part = jnp.einsum(
        "hu,ub->bh",
        rel_part.reshape(HEADS, SPAN),
        onehot,
        precision=lax.Precision.HIGHEST,
        preferred_element_type=f32,
    )
    tiny = table_part.reshape(2, 2, own_buckets, HEADS).astype(bf16)
    tiny = jnp.pad(tiny, ((0, 0), (0, 0), (0, own_rows - own_buckets), (0, 2 * LANES - HEADS)))
    self_keep, self_send, last_keep, last_send = weight_grad(
        where, [(normed_one, grad_qkv)], tiny=tiny, after=[blocks.own, cross_chain.sent]
    )
    self_send = meet(self_send, blocks, cross_chain)
    blocks.advance()
    cross_chain.advance()
    self_chain = Chain(self_keep, self_send, sizes, [2, 1], "yr")
    last_chain = Chain(last_keep, last_send, sizes, [2, 1], "ry")
    self_chain.advance()
    last_chain.advance()
    in_grad, _ = norm_back(
        grad_qkv, w_self, 0, hidden_in, gains_all[0:1], grad_first,
        after=[self_chain.sent, last_chain.sent, cross_chain.sent, blocks.own],
    )
    meet(in_grad, self_chain, last_chain, cross_chain)
    self_chain.advance()
    last_chain.advance()
    cross_chain.advance()
    cross_spread = None
    while last_chain.at < len(last_chain.steps):
        if last_chain.at == 3:
            together(self_chain, last_chain, cross_chain, blocks)
            cross_spread = Spread(cross_chain.own(), sizes, cross_chain.bits, cross_chain.dims)
        else:
            together(self_chain, last_chain)
        self_chain.advance()
        last_chain.advance()
    together(self_chain, last_chain, cross_spread)
    if cross_spread.left:
        cross_spread.advance()
    self_width = self_chain.got.shape[2]
    self_spread = Spread(
        jnp.concatenate([self_chain.own(), last_chain.own()], axis=2),
        sizes, self_chain.bits, self_chain.dims,
    )
    while self_spread.left:
        if cross_spread.left:
            together(self_spread, cross_spread)
            cross_spread.advance()
        self_spread.advance()
    low, high = self_spread.pair()
    low, high = low[0], high[0]
    self_grad = jnp.concatenate(
        [low[:, :self_width], high[:, :self_width], low[:, self_width:], high[:, self_width:]],
        axis=1,
    ).astype(f32)
    cross_grad = jnp.concatenate(cross_spread.pair(), axis=cross_spread.now[1])[0].astype(f32)

    if reps == 8:
        ff_in_grad, ff_out_grad, in_sums = unpack(where, blocks.own, blocks.got, ff_in)
        in_sums = in_sums[0]
    else:
        while blocks.left:
            blocks.advance()
        spread = jnp.concatenate(blocks.pair(), axis=0)
        in_grads = spread[:, :2].transpose(2, 1, 0, 3)
        ff_in_grad = in_grads.reshape(own_rows, 2 * FF).astype(f32)
        out_grads = spread[:, 2].reshape(reps, -1, out_rows, columns).transpose(0, 2, 1, 3)
        ff_out_grad = out_grads.reshape(ff_out.shape).astype(f32)
        in_sums = jnp.sum(ff_in.astype(f32) * ff_in_grad, axis=1)

    self_qkv_grad = self_grad[:, : 3 * INNER]
    cross_query_gradient = cross_grad[:, 2 * INNER : 3 * INNER]

    sums = jnp.stack(
        [
            jnp.sum(self_qkv.astype(f32) * self_qkv_grad, axis=1),
            jnp.sum(cross_q.astype(f32) * cross_query_gradient, axis=1),
            in_sums,
        ]
    )
    gains_grad = sums / gains.astype(f32)
    rel_table_grad = self_grad[:own_buckets, 3 * INNER : 3 * INNER + HEADS]
    return (
        layer_out,
        in_grad,
        enc_grad,
        gains_grad,
        rel_table_grad,
        self_qkv_grad,
        cross_grad[:, 3 * INNER + D :],
        cross_query_gradient,
        cross_grad[:, : 2 * INNER],
        cross_grad[:, 3 * INNER : 3 * INNER + D],
        ff_in_grad,
        ff_out_grad,
    )


def solution(mesh):
    tokens = P(("rep", "shard"), None)
    ids = P(("rep", "shard"))
    rows = P("shard", None)
    columns = P(None, "shard")
    in_specs = (tokens, tokens, ids, ids, tokens, columns) + (rows,) * 8
    out_specs = (tokens, tokens, tokens, columns) + (rows,) * 8
    sizes = (mesh.shape["shard"], mesh.shape["rep"])
    return jax.shard_map(
        partial(local, sizes), mesh=mesh, in_specs=in_specs, out_specs=out_specs, check_vma=False
    )
```

```python
from functools import partial
import math

import jax
import jax.numpy as jnp
import numpy as np
from jax import lax
from jax.experimental import pallas as pl
from jax.experimental.pallas import tpu as pltpu
from jax.sharding import PartitionSpec as P

HEADS = 12
HEAD_DIM = 64
FF = 2048
NUM_BUCKETS = 32
SEQ = 512
D = 768
INNER = HEADS * HEAD_DIM
PAIRS = HEADS // 2
LANES = 128
SPAN = SEQ + LANES
GROUP = 3
WIDE = GROUP * LANES
FF_BLOCK = 512
ROWS = 256

eps = 1e-06
masked_score = -1e30
bf16 = jnp.bfloat16
f32 = jnp.float32
VMEM_LIMIT = 56 * 1024 * 1024
LIGHT = pl.CostEstimate(flops=1000000, bytes_accessed=100000, transcendentals=0)

bucket_edges = np.array(
    list(range(1, 16)) + [int(math.ceil(16.0 * 8.0 ** ((b - 16) / 16.0))) for b in range(16, 32)],
    dtype=np.int32,
)

SELF_RANGES = ((0, 128), (0, 256), (0, 384), (128, 512))
CROSS_RANGES = ((0, 384), (0, 512), (0, 512), (128, 512))


def dot_nn(a, b):
    return lax.dot_general(a, b, (((1,), (0,)), ((), ())), preferred_element_type=f32)


def dot_nt(a, b):
    return lax.dot_general(a, b, (((1,), (1,)), ((), ())), preferred_element_type=f32)


def dot_tn(a, b):
    return lax.dot_general(a, b, (((0,), (0,)), ((), ())), preferred_element_type=f32)


def half_masks():
    lane = lax.broadcasted_iota(jnp.int32, (1, LANES), 1)
    low = (lane < HEAD_DIM).astype(f32)
    return low.astype(bf16), (1.0 - low).astype(bf16)


def pieces(value):
    lane = lax.broadcasted_iota(jnp.int32, value.shape, 1) % HEAD_DIM
    high = value.astype(bf16).astype(f32)
    rest = value - high
    middle = rest.astype(bf16).astype(f32)
    last = rest - middle
    return jnp.where(
        lane == 2, high, jnp.where(lane == 3, middle, jnp.where(lane == 4, last, 0.0))
    )


def stacked(block, low, high):
    return jnp.concatenate([block * low, block * high], axis=0)


def toeplitz(row):
    wide = jnp.broadcast_to(row, (LANES, SPAN))
    return pltpu.roll(wide, 0, 1, stride=1, stride_axis=0)[:, :SEQ]


def by_pair(kernel, kinds, waits, *refs):
    for pair in range(GROUP):
        lanes = slice(pair * LANES, (pair + 1) * LANES)
        views = []
        for kind, ref in zip(kinds, refs[waits:]):
            if kind == "L":
                ref = ref.at[:, lanes]
            elif kind == "T":
                ref = ref.at[:, :, lanes]
            elif kind == "G":
                ref = ref.at[pair : pair + 1]
            elif kind == "X":
                ref = ref.at[pair]
            views.append(ref)
        kernel(*views)


def attend_forward_kernel(ranges, biased, *refs):
    if biased:
        q_ref, k_ref, v_ref, qa_ref, ka_ref, g_ref, o_ref, l_ref, slab = refs

        @pl.when(pl.program_id(1) == 0)
        def _():
            slab[0:LANES] = toeplitz(g_ref[0, 0:1, :])
            slab[LANES : 2 * LANES] = toeplitz(g_ref[0, 1:2, :])
    else:
        q_ref, k_ref, v_ref, qa_ref, ka_ref, o_ref, l_ref = refs
    low, high = half_masks()
    keys = jnp.concatenate([k_ref[...], ka_ref[...]], axis=1)
    values = jnp.concatenate([v_ref[...], jnp.ones((SEQ, LANES), bf16)], axis=1)
    lane = lax.broadcasted_iota(jnp.int32, (LANES, LANES), 1)
    blocks = [
        (slice(i * LANES, (i + 1) * LANES), slice(start, stop), slice(SEQ - (stop - start), SEQ))
        for i, (start, stop) in enumerate(ranges)
    ]
    scores = []
    for rows, seen, columns in blocks:
        extra = qa_ref[rows, :]
        left = jnp.concatenate(
            [stacked(q_ref[rows, :], low, high), jnp.concatenate([extra, extra], axis=0)], axis=1
        )
        score = dot_nt(left, keys[seen])
        scores.append(score + slab[:, columns] if biased else score)
    tops = [jnp.max(score, axis=1, keepdims=True) for score in scores]
    expds = [jnp.exp(score - top).astype(bf16) for score, top in zip(scores, tops)]
    mixes = [dot_nn(expd, values[seen]) for expd, (_, seen, _) in zip(expds, blocks)]
    outs = []
    for mixed, top in zip(mixes, tops):
        total = mixed[:, LANES:]
        mixed = mixed[:, :LANES] / total
        negative = pieces(-(top + jnp.log(total)))
        outs.append(
            (
                jnp.where(lane < HEAD_DIM, mixed[:LANES], mixed[LANES:]).astype(bf16),
                jnp.where(lane < HEAD_DIM, negative[:LANES], negative[LANES:]).astype(bf16),
            )
        )
    for (rows, _, _), (out, lows) in zip(blocks, outs):
        o_ref[rows, :] = out
        l_ref[rows, :] = lows


def attend_forward(q, q_at, k, k_at, v, v_at, q_extra, k_extra, g, ranges, after=()):
    tokens = q.shape[0]
    sequences = tokens // SEQ
    biased = g is not None

    def block(at):
        return pl.BlockSpec((SEQ, WIDE), lambda p, s: (s, at // GROUP + p))

    shared = pl.BlockSpec((SEQ, LANES), lambda p, s: (s, 0))
    in_specs = [block(q_at), block(k_at), block(v_at), shared, shared]
    args = [q, k, v, q_extra, k_extra]
    scratch = []
    if biased:
        in_specs.append(pl.BlockSpec((GROUP, 2, SPAN), lambda p, s: (p, 0, 0)))
        args.append(g)
        scratch.append(pltpu.VMEM((GROUP, 2 * LANES, SEQ), f32))
    seen = sum(stop - start for start, stop in ranges)
    return pl.pallas_call(
        partial(
            by_pair,
            partial(attend_forward_kernel, ranges, biased),
            "LLLSSGLLX" if biased else "LLLSSLL",
            len(after),
        ),
        grid=(PAIRS // GROUP, sequences),
        in_specs=[pl.BlockSpec(memory_space=pl.ANY)] * len(after) + in_specs,
        out_specs=[block(0), block(0)],
        out_shape=[jax.ShapeDtypeStruct((tokens, INNER), bf16)] * 2,
        scratch_shapes=scratch,
        compiler_params=pltpu.CompilerParams(vmem_limit_bytes=VMEM_LIMIT),
        cost_estimate=LIGHT,
    )(*after, *args)


def attend_backward_kernel(ranges, biased, *refs):
    if biased:
        (q_ref, k_ref, v_ref, qa_ref, ka_ref, l_ref, o_ref, d_ref, g_ref) = refs[:9]
        out_ref, rel_ref, dk, dv, slab, dslab = refs[9:]

        @pl.when(pl.program_id(1) == 0)
        def _():
            slab[:, 0:LANES] = toeplitz(g_ref[0, 0:1, :]).T
            slab[:, LANES : 2 * LANES] = toeplitz(g_ref[0, 1:2, :]).T
            dslab[...] = jnp.zeros_like(dslab)
    else:
        (q_ref, k_ref, v_ref, qa_ref, ka_ref, l_ref, o_ref, d_ref) = refs[:8]
        dq_ref, out_ref, dk, dv = refs[8:]
    low, high = half_masks()
    low_lane = lax.broadcasted_iota(jnp.int32, (LANES, LANES), 1) < HEAD_DIM
    low_row = lax.broadcasted_iota(jnp.int32, (LANES, LANES), 0) < HEAD_DIM
    keys = jnp.concatenate([k_ref[...], ka_ref[...]], axis=1)
    values = jnp.concatenate([v_ref[...], ka_ref[...]], axis=1)
    keys_t = k_ref[...].T
    blocks = [
        (slice(i * LANES, (i + 1) * LANES), slice(start, stop), slice(SEQ - (stop - start), SEQ))
        for i, (start, stop) in enumerate(ranges)
    ]
    rights = []
    for rows, _, _ in blocks:
        q2 = stacked(q_ref[rows, :], low, high)
        extra = qa_ref[rows, :]
        totals = l_ref[rows, :]
        q_right = jnp.concatenate(
            [q2, jnp.concatenate([extra + totals * low, extra + totals * high], axis=0)], axis=1
        )
        grad = d_ref[rows, :]
        d2 = stacked(grad, low, high)
        product = grad.astype(f32) * o_ref[rows, :].astype(f32)
        sum_low = jnp.sum(jnp.where(low_lane, product, 0.0), axis=1, keepdims=True)
        sum_high = jnp.sum(jnp.where(low_lane, 0.0, product), axis=1, keepdims=True)
        delta = pieces(
            -jnp.concatenate(
                [
                    jnp.broadcast_to(sum_low, (LANES, LANES)),
                    jnp.broadcast_to(sum_high, (LANES, LANES)),
                ],
                axis=0,
            )
        ).astype(bf16)
        lows = jnp.concatenate([delta[:LANES] * low, delta[LANES:] * high], axis=0)
        rights.append((q2, q_right, d2, jnp.concatenate([d2, lows], axis=1)))
    scores = [
        dot_nt(keys[seen], q_right) for (_, seen, _), (_, q_right, _, _) in zip(blocks, rights)
    ]
    if biased:
        scores = [score + slab[columns, :] for (_, _, columns), score in zip(blocks, scores)]
    grads = [
        dot_nt(values[seen], d_right) for (_, seen, _), (_, _, _, d_right) in zip(blocks, rights)
    ]
    probs = [jnp.exp(score) for score in scores]
    grads = [prob * grad for prob, grad in zip(probs, grads)]
    probs = [prob.astype(bf16) for prob in probs]
    grads16 = [grad.astype(bf16) for grad in grads]
    dvs = [dot_nn(prob, right[2]) for prob, right in zip(probs, rights)]
    dks = [dot_nn(grad, right[0]) for grad, right in zip(grads16, rights)]
    dqs = [dot_nn(keys_t[:, seen], grad) for (_, seen, _), grad in zip(blocks, grads16)]
    dk[...] = jnp.zeros_like(dk)
    dv[...] = jnp.zeros_like(dv)
    for (_, seen, _), dv_here, dk_here in zip(blocks, dvs, dks):
        dv[seen, :] += dv_here
        dk[seen, :] += dk_here
    for (rows, _, columns), dq, grad in zip(blocks, dqs, grads):
        dq = jnp.where(low_row, dq[:, :LANES], dq[:, LANES:]).T.astype(bf16)
        if biased:
            out_ref[0, rows, :] = dq
            dslab[columns, :] += grad
        else:
            dq_ref[rows, :] = dq
    first = 1 if biased else 0
    out_ref[first] = dk[...].astype(bf16)
    out_ref[first + 1] = dv[...].astype(bf16)
    if biased:

        @pl.when(pl.program_id(1) == pl.num_programs(1) - 1)
        def _():
            for head in range(2):
                square = dslab[:, head * LANES : (head + 1) * LANES].T
                wide = jnp.concatenate([square, jnp.zeros((LANES, LANES), f32)], axis=1)
                half = LANES // 2
                while half >= 1:
                    wide = wide[:half] + pltpu.roll(wide[half:], SPAN - half, 1)
                    half //= 2
                rel_ref[0, head : head + 1, :] = wide


def attend_backward(q, q_at, k, k_at, v, v_at, q_extra, k_extra, lows, mixed, grad, g, ranges, after=(),
                    first=0, pairs=PAIRS, into=None):
    tokens = q.shape[0]
    sequences = tokens // SEQ
    biased = g is not None

    def block(at):
        return pl.BlockSpec((SEQ, WIDE), lambda p, s: (s, (at + first) // GROUP + p))

    shared = pl.BlockSpec((SEQ, LANES), lambda p, s: (s, 0))
    in_specs = [block(q_at), block(k_at), block(v_at), shared, shared, block(0), block(0), block(0)]
    args = [q, k, v, q_extra, k_extra, lows, mixed, grad]
    scratch = [pltpu.VMEM((GROUP, SEQ, LANES), f32)] * 2
    if biased:
        in_specs.append(pl.BlockSpec((GROUP, 2, SPAN), lambda p, s: (first // GROUP + p, 0, 0)))
        args.append(g)
        scratch += [pltpu.VMEM((GROUP, SEQ, 2 * LANES), f32)] * 2
        out_specs = [
            pl.BlockSpec((3, SEQ, WIDE), lambda p, s: (0, s, first // GROUP + p)),
            pl.BlockSpec((GROUP, 2, SPAN), lambda p, s: (p, 0, 0)),
        ]
        out_shape = [
            jax.ShapeDtypeStruct((3, tokens, INNER), bf16),
            jax.ShapeDtypeStruct((pairs, 2, SPAN), f32),
        ]
    else:
        out_specs = [block(0), pl.BlockSpec((2, SEQ, WIDE), lambda p, s: (0, s, p))]
        out_shape = [
            jax.ShapeDtypeStruct((tokens, INNER), bf16),
            jax.ShapeDtypeStruct((2, tokens, INNER), bf16),
        ]
    aliases = {}
    if into is not None:
        after = [into, *after]
        aliases = {0: 0}
    return pl.pallas_call(
        partial(
            by_pair,
            partial(attend_backward_kernel, ranges, biased),
            "LLLSSLLLGTGXXXX" if biased else "LLLSSLLLLTXX",
            len(after),
        ),
        grid=(pairs // GROUP, sequences),
        in_specs=[pl.BlockSpec(memory_space=pl.ANY)] * len(after) + in_specs,
        out_specs=out_specs,
        out_shape=out_shape,
        scratch_shapes=scratch,
        input_output_aliases=aliases,
        compiler_params=pltpu.CompilerParams(vmem_limit_bytes=VMEM_LIMIT),
        cost_estimate=LIGHT,
    )(*after, *args)


def shares(core, value, keep_ref, send_ref, *at):
    rows, cols = value.shape
    parts = value.astype(bf16).reshape(2, 2, rows // 4, cols)
    for y in range(2):
        place = (y,) + at
        keep_ref[place] = jnp.where(core == 0, parts[y, 0], parts[y, 1])
        send_ref[place] = jnp.where(core == 0, parts[y, 1], parts[y, 0])


def place_pieces(where_ref, full, own, core, y, x, yc, xc):
    shard = where_ref[0]
    rows, cols = own.shape
    half = cols // 2

    def at(index):
        return pl.ds(pl.multiple_of(index * rows, rows), rows)

    full[at(shard), :] = own[...]
    full[at(shard ^ 1), :] = core[...]
    for bit in range(2):

        @pl.when(where_ref[1] == bit)
        def _():
            mine = slice(bit * half, (bit + 1) * half)
            other = slice((1 - bit) * half, (2 - bit) * half)
            full[at(shard ^ 2), mine] = y[...]
            full[at(shard ^ 2), other] = x[...]
            full[at(shard ^ 3), mine] = yc[...]
            full[at(shard ^ 3), other] = xc[...]


def whole_spec(array):
    return pl.BlockSpec(
        array.shape, lambda i, c: (0,) * array.ndim, pipeline_mode=pl.Buffered(1)
    )


def normed_rows(x, gain):
    factor = lax.rsqrt(jnp.mean(x * x, -1, keepdims=True) + eps)
    return (x * factor * gain).astype(bf16)


def first_kernel(where_ref, x_ref, onehot_ref, valid_ref, *refs):
    pieces_in = refs[:6]
    full, gains_ref, g_ref, n_ref, qkv_ref = refs[6:]

    @pl.when(pl.program_id(0) == 0)
    def _():
        place_pieces(where_ref, full, *pieces_in)
        small = full[:, 3 * INNER : 3 * INNER + LANES].astype(f32).T
        gains_ref[...] = small[0:8]
        table = small[16:32].astype(bf16)
        bias = jnp.where(valid_ref[...] > 0, dot_nn(table, onehot_ref[...]), masked_score)
        for pair in range(PAIRS):
            g_ref[pair] = bias[2 * pair : 2 * pair + 2]

    normed = normed_rows(x_ref[...].astype(f32), gains_ref[0:1, :])
    n_ref[...] = normed
    for part in range(3):
        columns = slice(part * D, (part + 1) * D)
        qkv_ref[:, columns] = dot_nn(normed, full[:, columns]).astype(bf16)


def first_step(where, x, pieces_in, onehot, valid):
    tokens = x.shape[0]
    width = pieces_in[0].shape[1]
    block = pl.BlockSpec((ROWS, D), lambda i, c: (i, 0))
    return pl.pallas_call(
        first_kernel,
        grid_spec=pltpu.PrefetchScalarGridSpec(
            num_scalar_prefetch=1,
            grid=(tokens // ROWS,),
            in_specs=[block, whole_spec(onehot), whole_spec(valid)]
            + [whole_spec(p) for p in pieces_in],
            out_specs=[
                pl.BlockSpec((D, width), lambda i, c: (0, 0)),
                pl.BlockSpec((8, D), lambda i, c: (0, 0)),
                pl.BlockSpec((PAIRS, 2, SPAN), lambda i, c: (0, 0, 0)),
                block,
                pl.BlockSpec((ROWS, 3 * INNER), lambda i, c: (i, 0)),
            ],
        ),
        out_shape=[
            jax.ShapeDtypeStruct((D, width), bf16),
            jax.ShapeDtypeStruct((8, D), f32),
            jax.ShapeDtypeStruct((PAIRS, 2, SPAN), f32),
            jax.ShapeDtypeStruct((tokens, D), bf16),
            jax.ShapeDtypeStruct((tokens, 3 * INNER), bf16),
        ],
        compiler_params=pltpu.CompilerParams(vmem_limit_bytes=VMEM_LIMIT),
        cost_estimate=LIGHT,
    )(where, x, onehot, valid, *pieces_in)


def encoder_kernel(waits, where_ref, *refs):
    refs = refs[waits:]
    x_ref, pieces_in = refs[0], refs[1:7]
    full, kv_ref = refs[7:]

    @pl.when(pl.program_id(0) == 0)
    def _():
        place_pieces(where_ref, full, *pieces_in)

    for part in range(2):
        columns = slice(part * D, (part + 1) * D)
        kv_ref[:, columns] = dot_nn(x_ref[...], full[:, columns]).astype(bf16)


def encoder_step(where, x, pieces_in, after):
    tokens = x.shape[0]
    width = pieces_in[0].shape[1]
    return pl.pallas_call(
        partial(encoder_kernel, len(after)),
        grid_spec=pltpu.PrefetchScalarGridSpec(
            num_scalar_prefetch=1,
            grid=(tokens // ROWS,),
            in_specs=[pl.BlockSpec(memory_space=pl.ANY)] * len(after)
            + [pl.BlockSpec((ROWS, D), lambda i, c: (i, 0))]
            + [whole_spec(p) for p in pieces_in],
            out_specs=[
                pl.BlockSpec((D, width), lambda i, c: (0, 0)),
                pl.BlockSpec((ROWS, 2 * INNER), lambda i, c: (i, 0)),
            ],
        ),
        out_shape=[
            jax.ShapeDtypeStruct((D, width), bf16),
            jax.ShapeDtypeStruct((tokens, 2 * INNER), bf16),
        ],
        compiler_params=pltpu.CompilerParams(vmem_limit_bytes=VMEM_LIMIT),
        cost_estimate=LIGHT,
    )(where, *after, x, *pieces_in)


def middle_kernel(x_ref, attn_ref, out_w_ref, gain_ref, q_w_ref, first_ref, n_ref, cq_ref):
    first = x_ref[...].astype(f32) + dot_nn(attn_ref[...], out_w_ref[...])
    first_ref[...] = first
    normed = normed_rows(first, gain_ref[...])
    n_ref[...] = normed
    cq_ref[...] = dot_nn(normed, q_w_ref[...]).astype(bf16)


def middle_step(x, attn, gain, w_cross):
    tokens = x.shape[0]
    block = pl.BlockSpec((ROWS, D), lambda i: (i, 0))
    return pl.pallas_call(
        middle_kernel,
        grid=(tokens // ROWS,),
        in_specs=[
            block,
            block,
            pl.BlockSpec((D, D), lambda i: (0, 4)),
            pl.BlockSpec((1, D), lambda i: (0, 0)),
            pl.BlockSpec((D, D), lambda i: (0, 2)),
        ],
        out_specs=[block] * 3,
        out_shape=[
            jax.ShapeDtypeStruct((tokens, D), f32),
            jax.ShapeDtypeStruct((tokens, D), bf16),
            jax.ShapeDtypeStruct((tokens, D), bf16),
        ],
        compiler_params=pltpu.CompilerParams(vmem_limit_bytes=VMEM_LIMIT),
        cost_estimate=LIGHT,
    )(x, attn, w_cross, gain, w_cross)


def shares(core, value, keep_ref, send_ref, *at, start=0):
    rows, cols = value.shape
    parts = value.astype(bf16).reshape(2, 2, rows // 4, cols)
    columns = slice(start, start + cols)
    for y in range(2):
        place = (y,) + at + (slice(None), columns)
        keep_ref[place] = jnp.where(core == 0, parts[y, 0], parts[y, 1])
        send_ref[place] = jnp.where(core == 0, parts[y, 1], parts[y, 0])


def feed_forward_kernel(
    where_ref, x1_ref, attn_ref, w2_ref, gain_ref, dout_ref,
    own_g, own_u, core_g, core_u, y_in, x_in, yc_in, xc_in,
    own_o, core_o, y_o, x_o, yc_o, xc_o,
    layer_ref, gx_ref, gx16_ref, gk_ref, gs_ref, ok_ref, os_ref,
    wg, wu, wo, n3, n3t, acc, dn, hid, dgate, dup,
):
    step = pl.program_id(0)
    shard, across = where_ref[0], where_ref[1]
    tokens = x1_ref.shape[0]
    chunks = tokens // ROWS
    rows_in = own_g.shape[0]

    def at(index):
        return pl.ds(pl.multiple_of(index * rows_in, rows_in), rows_in)

    wg[at(shard), :] = own_g[...]
    wu[at(shard), :] = own_u[...]
    wg[at(shard ^ 1), :] = core_g[...]
    wu[at(shard ^ 1), :] = core_u[...]

    @pl.when(across == 0)
    def _():
        wg[at(shard ^ 2), :] = y_in[...]
        wu[at(shard ^ 2), :] = x_in[...]
        wg[at(shard ^ 3), :] = yc_in[...]
        wu[at(shard ^ 3), :] = xc_in[...]

    @pl.when(across == 1)
    def _():
        wg[at(shard ^ 2), :] = x_in[...]
        wu[at(shard ^ 2), :] = y_in[...]
        wg[at(shard ^ 3), :] = xc_in[...]
        wu[at(shard ^ 3), :] = yc_in[...]

    half = D // 2
    for turn, whole in ((0, own_o), (1, core_o)):

        @pl.when(step == turn)
        def _():
            wo[...] = whole[...]

    for turn, near, far in ((2, y_o, x_o), (3, yc_o, xc_o)):
        for bit in range(2):

            @pl.when((step == turn) & (across == bit))
            def _():
                wo[:, bit * half : (bit + 1) * half] = near[...]
                wo[:, (1 - bit) * half : (2 - bit) * half] = far[...]

    @pl.when(step == 0)
    def _():
        gain = gain_ref[...]
        for chunk in range(chunks):
            rows = slice(chunk * ROWS, (chunk + 1) * ROWS)
            x = x1_ref[rows, :] + dot_nn(attn_ref[rows, :], w2_ref[...])
            gx_ref[rows, :] = x
            normed = normed_rows(x, gain)
            n3[rows, :] = normed
            n3t[:, rows] = normed.T
            acc[rows, :] = jnp.zeros((ROWS, D), f32)
            dn[rows, :] = jnp.zeros((ROWS, D), f32)

    c = math.sqrt(2.0 / math.pi)
    for chunk in range(chunks):
        rows = slice(chunk * ROWS, (chunk + 1) * ROWS)
        normed = n3[rows, :]
        gate = dot_nn(normed, wg[...])
        up = dot_nn(normed, wu[...])
        dhidden = dot_nt(dout_ref[rows, :], wo[...]).astype(bf16).astype(f32)
        square = gate * gate
        t = jnp.tanh(c * gate * (1.0 + 0.044715 * square))
        mid = 0.5 * (1.0 + t)
        act = gate * mid
        slope = mid + (0.5 * c) * gate * (1.0 - t * t) * (1.0 + (3.0 * 0.044715) * square)
        hid[rows, :] = (act * up).astype(bf16)
        dgate[rows, :] = (dhidden * up * slope).astype(bf16)
        dup[rows, :] = (dhidden * act).astype(bf16)
        acc[rows, :] += dot_nn(hid[rows, :], wo[...])
        dn[rows, :] += dot_nt(dgate[rows, :], wg[...]) + dot_nt(dup[rows, :], wu[...])
    core = shard % 2
    for part, grads in enumerate((dgate, dup)):
        for start in range(0, FF_BLOCK, ROWS):
            value = dot_nn(n3t[...], grads[:, start : start + ROWS])
            shares(core, value, gk_ref, gs_ref, part, start=start)
    out_grad = dot_tn(hid[...], dout_ref[...]).astype(bf16)

    @pl.when(step % 2 == 0)
    def _():
        ok_ref[0] = out_grad

    @pl.when(step % 2 == 1)
    def _():
        os_ref[0] = out_grad

    @pl.when(step == pl.num_programs(0) - 1)
    def _():
        gain = gain_ref[...]
        for chunk in range(chunks):
            rows = slice(chunk * ROWS, (chunk + 1) * ROWS)
            x = gx_ref[rows, :]
            layer_ref[rows, :] = (x + acc[rows, :]).astype(bf16)
            factor = lax.rsqrt(jnp.mean(x * x, -1, keepdims=True) + eps)
            d = dn[rows, :]
            weighted = d * gain
            back = factor * weighted - x * (
                factor * factor * factor * jnp.mean(weighted * x, -1, keepdims=True)
            )
            gx = dout_ref[rows, :].astype(f32) + back
            gx_ref[rows, :] = gx
            gx16_ref[rows, :] = gx.astype(bf16)


def feed_forward(where, x1, attn, w_cross, gain, dout, in_pieces, out_pieces):
    tokens = x1.shape[0]
    steps = FF // FF_BLOCK
    one = pl.Buffered(1)
    rows_in = in_pieces[0].shape[0]

    def whole(width=D):
        return pl.BlockSpec((tokens, width), lambda f, c: (0, 0), pipeline_mode=one)

    def streamed(at):
        return pl.BlockSpec((rows_in, FF_BLOCK), lambda f, c: (0, at + (c[0] ^ f)))

    resident = pl.BlockSpec((tokens, D), lambda f, c: (0, 0))
    in_share = pl.BlockSpec((2, 2, D // 4, FF_BLOCK), lambda f, c: (0, 0, 0, c[0] ^ f))
    out_share = pl.BlockSpec((1, FF_BLOCK, D), lambda f, c: ((c[0] ^ f) // 2, 0, 0))
    in_type = jax.ShapeDtypeStruct((2, 2, D // 4, FF), bf16)
    out_type = jax.ShapeDtypeStruct((2, FF_BLOCK, D), bf16)
    own_i, core_i, *halves_i = in_pieces
    return pl.pallas_call(
        feed_forward_kernel,
        grid_spec=pltpu.PrefetchScalarGridSpec(
            num_scalar_prefetch=1,
            grid=(steps,),
            in_specs=[
                whole(),
                whole(),
                pl.BlockSpec((D, D), lambda f, c: (0, 3), pipeline_mode=one),
                pl.BlockSpec((1, D), lambda f, c: (0, 0)),
                whole(),
                streamed(0), streamed(steps), streamed(0), streamed(steps),
                streamed(0), streamed(0), streamed(0), streamed(0),
            ]
            + [whole_spec(p) for p in out_pieces],
            out_specs=[resident, resident, resident, in_share, in_share, out_share, out_share],
            scratch_shapes=[
                pltpu.VMEM((D, FF_BLOCK), bf16),
                pltpu.VMEM((D, FF_BLOCK), bf16),
                pltpu.VMEM((FF_BLOCK, D), bf16),
                pltpu.VMEM((tokens, D), bf16),
                pltpu.VMEM((D, tokens), bf16),
                pltpu.VMEM((tokens, D), f32),
                pltpu.VMEM((tokens, D), f32),
                pltpu.VMEM((tokens, FF_BLOCK), bf16),
                pltpu.VMEM((tokens, FF_BLOCK), bf16),
                pltpu.VMEM((tokens, FF_BLOCK), bf16),
            ],
        ),
        out_shape=[
            jax.ShapeDtypeStruct((tokens, D), bf16),
            jax.ShapeDtypeStruct((tokens, D), f32),
            jax.ShapeDtypeStruct((tokens, D), bf16),
            in_type, in_type, out_type, out_type,
        ],
        compiler_params=pltpu.CompilerParams(vmem_limit_bytes=VMEM_LIMIT),
        cost_estimate=LIGHT,
    )(where, x1, attn, w_cross, gain, dout, own_i, own_i, core_i, core_i, *halves_i, *out_pieces)


def weight_grad_kernel(counts, firsts, waits, core_ref, *refs):
    refs = refs[waits:]
    terms = len(counts)
    lefts, rights = refs[0:terms], refs[terms : 2 * terms]
    refs = refs[2 * terms :]
    second = firsts is not None
    if second:
        tiny_ref, keep_ref, send_ref, keep2_ref, send2_ref = refs
    else:
        keep_ref, send_ref = refs
    step = pl.program_id(0)
    core = core_ref[0] % 2
    at = 0
    for left, right, count in zip(lefts, rights, counts):

        def product(keep, send):
            for start in range(0, D, ROWS):
                columns = slice(start, start + ROWS)
                block = right[:, columns] if len(right.shape) == 2 else right[0, :, columns]
                shares(core, dot_tn(left[...], block), keep, send, start=start)

        @pl.when((step >= at) & (step < (firsts if second else at + count)))
        def _():
            product(keep_ref, send_ref)

        if second:

            @pl.when(step >= firsts)
            def _():
                product(keep2_ref, send2_ref)
                tiny = tiny_ref[...]
                for y in range(2):
                    keep2_ref[y, :, D:] = jnp.where(core == 0, tiny[y, 0], tiny[y, 1])
                    send2_ref[y, :, D:] = jnp.where(core == 0, tiny[y, 1], tiny[y, 0])

        at += count


def weight_grad(where, terms, tiny=None, after=()):
    tokens = terms[0][0].shape[0]
    counts = []
    rights = []
    at = 0
    for _, right in terms:
        deep = right.ndim == 3
        count = right.shape[0] if deep else 1

        def place(j, c, at=at, count=count, deep=deep):
            return (jnp.clip(j - at, 0, count - 1), 0, 0) if deep else (0, 0)

        rights.append(pl.BlockSpec((1, tokens, D) if deep else (tokens, D), place))
        counts.append(count)
        at += count
    firsts = None if tiny is None else at - 1
    blocks = at if tiny is None else at - 1
    share = pl.BlockSpec((2, D // 4, D), lambda j, c: (0, 0, jnp.minimum(j, blocks - 1)))
    out_specs = [share, share]
    out_shape = [jax.ShapeDtypeStruct((2, D // 4, blocks * D), bf16)] * 2
    extra_specs, extra = [], []
    if tiny is not None:
        extra_specs, extra = [pl.BlockSpec(tiny.shape, lambda j, c: (0, 0, 0, 0))], [tiny]
        wide = D + tiny.shape[-1]
        out_specs += [pl.BlockSpec((2, D // 4, wide), lambda j, c: (0, 0, 0))] * 2
        out_shape += [jax.ShapeDtypeStruct((2, D // 4, wide), bf16)] * 2
    return pl.pallas_call(
        partial(weight_grad_kernel, counts, firsts, len(after)),
        grid_spec=pltpu.PrefetchScalarGridSpec(
            num_scalar_prefetch=1,
            grid=(at,),
            in_specs=[pl.BlockSpec(memory_space=pl.ANY)] * len(after)
            + [pl.BlockSpec((tokens, D), lambda j, c: (0, 0))] * len(terms)
            + rights
            + extra_specs,
            out_specs=out_specs,
        ),
        out_shape=out_shape,
        compiler_params=pltpu.CompilerParams(vmem_limit_bytes=VMEM_LIMIT),
        cost_estimate=LIGHT,
    )(where, *after, *[left for left, _ in terms], *[right for _, right in terms], *extra)


def norm_back_kernel(normed, onward, waits, *refs):
    refs = refs[waits:]
    grad_ref, w_ref = refs[:2]
    total = None
    for part in range(grad_ref.shape[0]):
        term = dot_nt(grad_ref[part], w_ref[:, part * D : (part + 1) * D])
        total = term if total is None else total + term
    if not normed:
        refs[2][...] = total.astype(refs[2].dtype)
        return
    x_ref, gain_ref, up_ref = refs[2:5]
    refs = refs[5:]
    if onward:
        next_ref, out_ref, gain_grad_ref, out16_ref, onward_ref = refs
    else:
        out_ref, gain_grad_ref = refs
    x = x_ref[...].astype(f32)
    factor = lax.rsqrt(jnp.mean(x * x, -1, keepdims=True) + eps)
    weighted = total * gain_ref[...]
    grad_gain = jnp.sum(total * x * factor, axis=0, keepdims=True)

    @pl.when(pl.program_id(0) == 0)
    def _():
        gain_grad_ref[...] = jnp.zeros_like(gain_grad_ref)

    gain_grad_ref[...] += grad_gain
    scale = factor * factor * factor * jnp.mean(weighted * x, -1, keepdims=True)
    out = up_ref[...] + factor * weighted - x * scale
    out_ref[...] = out
    if onward:
        out16 = out.astype(bf16)
        out16_ref[...] = out16
        onward_ref[...] = dot_nt(out16, next_ref[...]).astype(bf16)


def norm_back(
    grads, w, w_at, x=None, gain=None, upstream=None, w_next=None, next_at=0, after=(), kind=f32
):
    if grads.ndim == 2:
        grads = grads[None]
    parts, tokens, _ = grads.shape
    block = pl.BlockSpec((ROWS, D), lambda i: (i, 0))
    row = pl.BlockSpec((1, D), lambda i: (0, 0))
    in_specs = [pl.BlockSpec(memory_space=pl.ANY)] * len(after)
    in_specs += [
        pl.BlockSpec((parts, ROWS, D), lambda i: (0, i, 0)),
        pl.BlockSpec((D, parts * D), lambda i: (0, w_at)),
    ]
    args = [*after, grads, w]
    wide = jax.ShapeDtypeStruct((tokens, D), kind)
    half = jax.ShapeDtypeStruct((tokens, D), bf16)
    out_specs, out_shape = [block], [wide]
    if x is not None:
        in_specs += [block, row, block]
        args += [x, gain, upstream]
        out_specs.append(row)
        out_shape.append(jax.ShapeDtypeStruct((1, D), f32))
        if w_next is not None:
            in_specs.append(pl.BlockSpec((D, D), lambda i: (0, next_at)))
            args.append(w_next)
            out_specs += [block, block]
            out_shape += [half, half]
    return pl.pallas_call(
        partial(norm_back_kernel, x is not None, w_next is not None, len(after)),
        grid=(tokens // ROWS,),
        in_specs=in_specs,
        out_specs=out_specs,
        out_shape=out_shape,
        compiler_params=pltpu.CompilerParams(vmem_limit_bytes=VMEM_LIMIT),
        cost_estimate=LIGHT,
    )(*args)


def exchange(array, axis, size, bit):
    return lax.ppermute(array, axis, [(i, i ^ bit) for i in range(size)])


def part_of(array, dim, index):
    half = array.shape[dim] // 2
    return lax.dynamic_slice_in_dim(array, index * half, half, dim)


def tie(value, *others):
    return lax.optimization_barrier((value, *others))[0]


def meet(done, *moves):
    *gots, done = lax.optimization_barrier((*[m.got for m in moves], done))
    for move, got in zip(moves, gots):
        move.got = got
    return done


class Gather:
    def __init__(self, own, sizes, *after):
        self.sizes = sizes
        self.own = own
        half = part_of(own, 1, lax.axis_index("rep") % 2)
        if after:
            half = tie(half, *after)
        self.half = half
        self.got = exchange(half, "shard", sizes[0], 2)

    def cross(self):
        self.y = self.got
        self.got = exchange(self.y, "rep", self.sizes[1], 1)
        self.core = exchange(tie(self.own, self.y), "shard", self.sizes[0], 1)
        self.yc = exchange(self.y, "shard", self.sizes[0], 1)

    def pieces(self):
        self.x = self.got
        xc = exchange(self.x, "shard", self.sizes[0], 1)
        return self.own, self.core, self.y, self.x, self.yc, xc


class Chain:
    def __init__(self, keep, send, sizes, dims, order, turned=False):
        self.shards, self.reps = sizes
        self.bits = [1 << b for b in range(self.reps.bit_length() - 1)]
        self.dims = [dims[min(i, len(dims) - 1)] for i in range(len(self.bits))]
        if turned:
            self.bits[:2] = self.bits[1::-1]
            self.dims[:2] = self.dims[1::-1]
        steps = []
        for name in order:
            if name == "y":
                steps.append(("shard", 2, 0))
            else:
                steps += [("rep", bit, dim) for bit, dim in zip(self.bits, self.dims)]
        self.steps = steps
        self.kept = keep
        self.got = exchange(send, "shard", self.shards, 1)
        self.sent = send
        self.at = 0

    def own(self):
        while self.at < len(self.steps):
            self.advance()
        return (self.kept.astype(f32) + self.got.astype(f32)).astype(bf16)

    def advance(self):
        axis, bit, dim = self.steps[self.at]
        self.at += 1
        mine = (lax.axis_index(axis) // bit) % 2
        size = self.shards if axis == "shard" else self.reps
        def half(index):
            kept, got = (part_of(part, dim, index).astype(f32) for part in (self.kept, self.got))
            return lax.optimization_barrier((kept + got).astype(bf16))

        self.sent = half(1 - mine)
        self.kept = half(mine)
        self.got = exchange(self.sent, axis, size, bit)
        return self.got


class Spread:
    def __init__(self, own, sizes, bits, dims):
        self.own = own
        self.reps = sizes[1]
        self.left = list(zip(bits, dims))
        self.got = None
        self.advance()

    def pair(self):
        bit, _ = self.now
        mine = (lax.axis_index("rep") // bit) % 2
        low = jnp.where(mine == 0, self.own, self.got)
        high = jnp.where(mine == 0, self.got, self.own)
        return low, high

    def advance(self):
        if self.got is not None:
            self.own = jnp.concatenate(self.pair(), axis=self.now[1])
        self.now = self.left.pop()
        self.got = exchange(self.own, "rep", self.reps, self.now[0])


def together(*moves):
    gots = lax.optimization_barrier(tuple(m.got for m in moves))
    for move, got in zip(moves, gots):
        move.got = got


def unpack_kernel(where_ref, own_ref, got_ref, w_ref, in_ref, out_ref, sum_ref):
    mine = where_ref[2]
    half, _, rows, cols = own_ref.shape
    out_rows = out_ref.shape[0] // (2 * half)
    total = jnp.zeros((rows, LANES), f32)
    for blocks_ref, bit in ((own_ref, mine), (got_ref, 1 - mine)):
        for block in range(half):
            at = block // 2 * 4 + bit * 2 + block % 2
            for part in range(2):
                place = pl.ds(pl.multiple_of(part * FF + at * cols, cols), cols)
                value = blocks_ref[block, part].astype(f32)
                in_ref[:, place] = value
                product = value * w_ref[:, place].astype(f32)
                for lane in range(0, cols, LANES):
                    total = total + product[:, lane : lane + LANES]
            place = pl.ds(pl.multiple_of(at * out_rows, out_rows), out_rows)
            for group in range(D // cols):
                out_ref[place, group * cols : (group + 1) * cols] = blocks_ref[
                    block, 2, group * out_rows : (group + 1) * out_rows, :
                ].astype(f32)
    row = jnp.broadcast_to(jnp.sum(total, axis=1, keepdims=True), (rows, LANES)).T
    sum_ref[...] = row[0:8]


def unpack(where, own, got, w):
    rows = own.shape[2]

    def whole(shape):
        return pl.BlockSpec(shape, lambda i, c: (0,) * len(shape))

    outs = [
        jax.ShapeDtypeStruct((rows, 2 * FF), f32),
        jax.ShapeDtypeStruct((FF * rows // D, D), f32),
        jax.ShapeDtypeStruct((8, rows), f32),
    ]
    return pl.pallas_call(
        unpack_kernel,
        grid_spec=pltpu.PrefetchScalarGridSpec(
            num_scalar_prefetch=1,
            grid=(1,),
            in_specs=[whole(own.shape), whole(got.shape), whole(w.shape)],
            out_specs=[whole(o.shape) for o in outs],
        ),
        out_shape=outs,
        compiler_params=pltpu.CompilerParams(vmem_limit_bytes=VMEM_LIMIT),
        cost_estimate=LIGHT,
    )(where, own, got, w)


def bias_rows(shards):
    lane = np.arange(SPAN)
    distance = np.where(lane < SEQ, SEQ - LANES - lane, 2 * SEQ - lane)
    bucket = np.zeros(SPAN, np.int64)
    for edge in bucket_edges:
        bucket += distance >= edge
    valid = (distance >= 0) & (distance < SEQ)
    onehot = np.zeros((SPAN, NUM_BUCKETS), np.float32)
    onehot[np.arange(SPAN)[valid], bucket[valid]] = 1.0
    own = NUM_BUCKETS // shards
    rows = np.arange(NUM_BUCKETS) // own * (D // shards) + np.arange(NUM_BUCKETS) % own
    placed = np.zeros((D, SPAN), np.float32)
    placed[rows] = onehot.T
    return onehot, placed, valid[None].astype(np.float32)


def local(
    sizes,
    hidden_in,
    enc_states,
    dec_segments,
    enc_segments,
    out_grad,
    gains,
    rel_table,
    self_qkv,
    self_out,
    cross_q,
    cross_kv,
    cross_out,
    ff_in,
    ff_out,
):
    shards, reps = sizes
    own_rows = D // shards
    own_buckets = NUM_BUCKETS // shards
    width = reps.bit_length() - 1
    shard = lax.axis_index("shard")
    rep = lax.axis_index("rep")
    where = jnp.stack([shard, rep % 2, rep // 2 % 2]).astype(jnp.int32)
    small = jnp.concatenate(
        [
            gains.T,
            jnp.zeros((own_rows, 13), bf16),
            jnp.pad(rel_table, ((0, own_rows - own_buckets), (0, 2 * LANES - 16 - HEADS))),
        ],
        axis=1,
    )
    self_set = Gather(jnp.concatenate([self_qkv, small], axis=1), sizes)
    self_set.cross()
    cross_set = Gather(
        jnp.concatenate([cross_kv, cross_q, cross_out, self_out], axis=1), sizes, self_set.y
    )
    self_pieces = self_set.pieces()

    lane = jnp.arange(LANES, dtype=jnp.int32)[None, :]
    dec_ids = dec_segments[:, None]
    enc_ids = enc_segments[:, None]
    ones = ((lane % HEAD_DIM >= 2) & (lane % HEAD_DIM <= 4)).astype(f32)

    def key_extra(ids):
        return jnp.where(lane < 2, jnp.where(lane != ids, masked_score, 0.0), ones).astype(bf16)

    q_extra = ((lane < 2) & (lane == dec_ids)).astype(bf16)
    self_extra = key_extra(dec_ids)
    cross_extra = key_extra(enc_ids)
    onehot, placed, valid = bias_rows(shards)
    w_self, gains_all, g, normed_one, qkv = first_step(
        where, hidden_in, self_pieces, placed.astype(bf16), valid
    )
    meet(normed_one, cross_set)
    cross_set.cross()
    out_set = Gather(ff_out, sizes, cross_set.y)
    in_set = Gather(ff_in, sizes, cross_set.y)
    attn_one, lows_one = attend_forward(
        qkv, 0, qkv, PAIRS, qkv, 2 * PAIRS, q_extra, self_extra, g, SELF_RANGES,
        after=[out_set.half, in_set.half],
    )
    meet(attn_one, cross_set)
    cross_pieces = cross_set.pieces()
    w_cross, ckv = encoder_step(where, enc_states, cross_pieces, [attn_one])
    ckv = meet(ckv, out_set, in_set)
    out_set.cross()
    in_set.cross()
    first, normed_two, cq = middle_step(hidden_in, attn_one, gains_all[1:2], w_cross)
    attn_two, lows_two = attend_forward(
        cq, 0, ckv, 0, ckv, PAIRS, q_extra, cross_extra, None, CROSS_RANGES
    )
    meet(attn_two, out_set, in_set)
    ff_out_pieces = out_set.pieces()
    ff_in_pieces = in_set.pieces()
    layer_out, grad_second, out_two, in_keep, in_send, out_keep, out_send = feed_forward(
        where, first, attn_two, w_cross, gains_all[2:3], out_grad, ff_in_pieces, ff_out_pieces
    )
    ff_in_chain = Chain(in_keep, in_send, sizes, [3], "yr")
    ff_out_chain = Chain(out_keep, out_send, sizes, [1], "ry")
    (grad_attn_two,) = norm_back(out_two, w_cross, 3, kind=bf16, after=[layer_out])
    meet(grad_attn_two, ff_in_chain, ff_out_chain)
    ff_out_chain.advance()
    ff_in_chain.advance()
    grad_cq, grad_ckv = attend_backward(
        cq, 0, ckv, 0, ckv, PAIRS, q_extra, cross_extra, lows_two, attn_two, grad_attn_two,
        None, CROSS_RANGES, after=[ff_in_chain.sent, ff_out_chain.sent],
    )
    meet(grad_cq, ff_out_chain)
    ff_out_chain.advance()
    grad_first, _, out_one, grad_attn_one = norm_back(
        grad_cq, w_cross, 2, first, gains_all[1:2], grad_second, w_cross, 4,
        after=[ff_out_chain.sent],
    )
    meet(grad_attn_one, ff_in_chain, ff_out_chain)
    ff_in_chain.advance()
    ff_out_chain.advance()
    cross_keep, cross_send = weight_grad(
        where,
        [(enc_states, grad_ckv), (normed_two, grad_cq), (attn_two, out_two), (attn_one, out_one)],
        after=[ff_in_chain.sent, ff_out_chain.sent],
    )
    cross_send = meet(cross_send, ff_in_chain, ff_out_chain)
    ff_in_chain.advance()
    ff_out_chain.advance()
    cross_chain = Chain(cross_keep, cross_send, sizes, [2, 1], "yr", turned=True)
    (enc_grad,) = norm_back(
        grad_ckv, w_cross, 0, after=[cross_keep, ff_in_chain.sent, ff_out_chain.sent]
    )
    meet(enc_grad, cross_chain, ff_in_chain, ff_out_chain)
    cross_chain.advance()
    ff_in_chain.advance()
    out_own = ff_out_chain.own()[0]
    backward = partial(
        attend_backward, qkv, 0, qkv, PAIRS, qkv, 2 * PAIRS, q_extra, self_extra, lows_one,
        attn_one, grad_attn_one, g, SELF_RANGES, pairs=PAIRS // 2,
    )
    some_qkv, some_rel = backward(after=[cross_chain.sent, ff_in_chain.sent, out_own])
    some_qkv = meet(some_qkv, ff_in_chain)
    in_own = ff_in_chain.own()[0]
    rows, columns = in_own.shape[1:]
    out_rows = out_own.shape[0]
    out_own = out_own.reshape(out_rows, -1, columns).transpose(1, 0, 2).reshape(1, rows, columns)
    bits = [2, 1, 4] if reps == 8 else ff_in_chain.bits
    blocks = Spread(
        jnp.concatenate([in_own, out_own], axis=0)[None], sizes, bits, [0] * len(bits)
    )
    grad_qkv, more_rel = backward(after=[blocks.own], first=PAIRS // 2, into=some_qkv)
    rel_part = jnp.concatenate([some_rel, more_rel], axis=0)
    grad_qkv = meet(grad_qkv, cross_chain, blocks)
    cross_chain.advance()
    blocks.advance()
    table_part = jnp.einsum(
        "hu,ub->bh",
        rel_part.reshape(HEADS, SPAN),
        onehot,
        precision=lax.Precision.HIGHEST,
        preferred_element_type=f32,
    )
    tiny = table_part.reshape(2, 2, own_buckets, HEADS).astype(bf16)
    tiny = jnp.pad(tiny, ((0, 0), (0, 0), (0, own_rows - own_buckets), (0, 2 * LANES - HEADS)))
    self_keep, self_send, last_keep, last_send = weight_grad(
        where, [(normed_one, grad_qkv)], tiny=tiny, after=[blocks.own, cross_chain.sent]
    )
    self_send = meet(self_send, blocks, cross_chain)
    blocks.advance()
    cross_chain.advance()
    self_chain = Chain(self_keep, self_send, sizes, [2, 1], "yr")
    last_chain = Chain(last_keep, last_send, sizes, [2, 1], "ry")
    self_chain.advance()
    last_chain.advance()
    in_grad, _ = norm_back(
        grad_qkv, w_self, 0, hidden_in, gains_all[0:1], grad_first,
        after=[self_chain.sent, last_chain.sent, cross_chain.sent, blocks.own],
    )
    meet(in_grad, self_chain, last_chain, cross_chain)
    self_chain.advance()
    last_chain.advance()
    cross_chain.advance()
    cross_spread = None
    while last_chain.at < len(last_chain.steps):
        if last_chain.at == 3:
            together(self_chain, last_chain, cross_chain, blocks)
            cross_spread = Spread(cross_chain.own(), sizes, cross_chain.bits, cross_chain.dims)
        else:
            together(self_chain, last_chain)
        self_chain.advance()
        last_chain.advance()
    together(self_chain, last_chain, cross_spread)
    if cross_spread.left:
        cross_spread.advance()
    self_width = self_chain.got.shape[2]
    self_spread = Spread(
        jnp.concatenate([self_chain.own(), last_chain.own()], axis=2),
        sizes, self_chain.bits, self_chain.dims,
    )
    while self_spread.left:
        if cross_spread.left:
            together(self_spread, cross_spread)
            cross_spread.advance()
        self_spread.advance()
    low, high = self_spread.pair()
    low, high = low[0], high[0]
    self_grad = jnp.concatenate(
        [low[:, :self_width], high[:, :self_width], low[:, self_width:], high[:, self_width:]],
        axis=1,
    ).astype(f32)
    cross_grad = jnp.concatenate(cross_spread.pair(), axis=cross_spread.now[1])[0].astype(f32)

    if reps == 8:
        got = tie(blocks.got, cross_spread.own, self_spread.own)
        ff_in_grad, ff_out_grad, in_sums = unpack(where, blocks.own, got, ff_in)
        in_sums = in_sums[0]
    else:
        while blocks.left:
            blocks.advance()
        spread = jnp.concatenate(blocks.pair(), axis=0)
        in_grads = spread[:, :2].transpose(2, 1, 0, 3)
        ff_in_grad = in_grads.reshape(own_rows, 2 * FF).astype(f32)
        out_grads = spread[:, 2].reshape(reps, -1, out_rows, columns).transpose(0, 2, 1, 3)
        ff_out_grad = out_grads.reshape(ff_out.shape).astype(f32)
        in_sums = jnp.sum(ff_in.astype(f32) * ff_in_grad, axis=1)

    self_qkv_grad = self_grad[:, : 3 * INNER]
    cross_query_gradient = cross_grad[:, 2 * INNER : 3 * INNER]

    sums = jnp.stack(
        [
            jnp.sum(self_qkv.astype(f32) * self_qkv_grad, axis=1),
            jnp.sum(cross_q.astype(f32) * cross_query_gradient, axis=1),
            in_sums,
        ]
    )
    gains_grad = sums / gains.astype(f32)
    rel_table_grad = self_grad[:own_buckets, 3 * INNER : 3 * INNER + HEADS]
    return (
        layer_out,
        in_grad,
        enc_grad,
        gains_grad,
        rel_table_grad,
        self_qkv_grad,
        cross_grad[:, 3 * INNER + D :],
        cross_query_gradient,
        cross_grad[:, : 2 * INNER],
        cross_grad[:, 3 * INNER : 3 * INNER + D],
        ff_in_grad,
        ff_out_grad,
    )


def solution(mesh):
    tokens = P(("rep", "shard"), None)
    ids = P(("rep", "shard"))
    rows = P("shard", None)
    columns = P(None, "shard")
    in_specs = (tokens, tokens, ids, ids, tokens, columns) + (rows,) * 8
    out_specs = (tokens, tokens, tokens, columns) + (rows,) * 8
    sizes = (mesh.shape["shard"], mesh.shape["rep"])
    return jax.shard_map(
        partial(local, sizes), mesh=mesh, in_specs=in_specs, out_specs=out_specs, check_vma=False
    )
```
